128 devices in a mesh: weights: 8 (over z, core), context: 4 (over x), tensor: 4 (over y).
Axes of the slice: x: 4, y: 4, z: 4, core: 2. Of those that a mesh axis runs over, the one named last changes fastest.
Arguments:
- tokens: bfloat16 [16384, 2048], P(('weights', 'context')), may hold values from -6 to 6
- cotangent: bfloat16 [16384, 2048], P(('weights', 'context')), may hold values from -6 to 6
- token_document_ids: int32 [8, 2048], P('weights'), may hold values from 0 to 2, as said below
- sequence_adapter_index: int32 [8], P('weights'), may hold values from 0 to 7
- mixer_norm_gain: float32 [2048], replicated, may hold values from 0.1 to 1.9
- head_norm_gain: float32 [128], replicated, may hold values from 0.1 to 1.9
- feedforward_norm_gain: float32 [2048], replicated, may hold values from 0.1 to 1.9
- short_filter_kernels: float32 [3, 4, 2048], P(None, None, 'tensor'), may hold values from -3 to 3
- query_weight: bfloat16 [2048, 2048], P(('weights', 'context'), 'tensor'), may hold values from -0.125 to 0.125
- key_weight: bfloat16 [2048, 2048], P(('weights', 'context'), 'tensor'), may hold values from -0.125 to 0.125
- value_weight: bfloat16 [2048, 2048], P(('weights', 'context'), 'tensor'), may hold values from -0.125 to 0.125
- strength_weight: bfloat16 [2048, 16], P(('weights', 'context'), 'tensor'), may hold values from -0.125 to 0.125
- mixer_output_weight: bfloat16 [2048, 2048], P('tensor', ('weights', 'context')), may hold values from -0.125 to 0.125
- gate_weight: bfloat16 [2048, 5632], P(('weights', 'context'), 'tensor'), may hold values from -0.125 to 0.125
- up_weight: bfloat16 [2048, 5632], P(('weights', 'context'), 'tensor'), may hold values from -0.125 to 0.125
- down_weight: bfloat16 [5632, 2048], P('tensor', ('weights', 'context')), may hold values from -0.078125 to 0.078125
- adapter_attention_input: bfloat16 [4, 8, 2048, 16], replicated, may hold values from -0.125 to 0.125
- adapter_triple_output: bfloat16 [3, 8, 16, 2048], P(None, None, None, 'tensor'), may hold values from -1.5 to 1.5
- adapter_strength_output: bfloat16 [8, 16, 16], P(None, None, 'tensor'), may hold values from -1.5 to 1.5
- adapter_projection_input: bfloat16 [8, 2048, 16], P(None, 'tensor'), may hold values from -0.125 to 0.125
- adapter_projection_output: bfloat16 [8, 16, 2048], replicated, may hold values from -1.5 to 1.5
- adapter_feedforward_input: bfloat16 [2, 8, 2048, 16], replicated, may hold values from -0.125 to 0.125
- adapter_feedforward_output: bfloat16 [2, 8, 16, 5632], P(None, None, None, 'tensor'), may hold values from -1.5 to 1.5
- adapter_down_input: bfloat16 [8, 5632, 16], P(None, 'tensor'), may hold values from -0.078125 to 0.078125
- adapter_down_output: bfloat16 [8, 16, 2048], replicated, may hold values from -1.5 to 1.5
Outputs:
- block_out: bfloat16 [16384, 2048], P(('weights', 'context'))
- tokens_grad: float32 [16384, 2048], P(('weights', 'context'))
- grad_attn_in: float32 [4, 8, 2048, 16], replicated
- grad_qkv_out: float32 [3, 8, 16, 2048], P(None, None, None, 'tensor')
- grad_beta_out: float32 [8, 16, 16], P(None, None, 'tensor')
- grad_o_in: float32 [8, 2048, 16], P(None, 'tensor')
- grad_o_out: float32 [8, 16, 2048], replicated
- grad_ffn_in: float32 [2, 8, 2048, 16], replicated
- grad_ffn_out: float32 [2, 8, 16, 5632], P(None, None, None, 'tensor')
- grad_down_in: float32 [8, 5632, 16], P(None, 'tensor')
- grad_down_out: float32 [8, 16, 2048], replicated
The draws below stay inside these ranges and needn't reach their ends.
Inputs may be any that keep to these rules, and one draw needn't show every extreme that they name: `token_document_ids`: segment ids never fall along a sequence.
All inputs are finite; a program needn't handle non-finite values.
Results may differ from the reference program's by a relative error of at most 0.023.
Values may be sent and summed in bfloat16 or wider, within the bound.
No kernel may reach another device: no remote copies, remote signals or barrier semaphores. Data moves between devices by JAX's collectives and lax.ppermute only.
A program may use at most 192 MiB of HBM per device.

```python
import jax
import jax.numpy as jnp
from jax import lax

MODEL_WIDTH = 2048
HEAD_COUNT = 16
HEAD_DIM = 128
HIDDEN_UNITS = 5632
CONV = 4
BLOCK = 64
ADAPTER_RANK = 16
ADAPTER_COUNT = 8
SPAN = 512
HEAD_FEATURES = 2048
LEN = 2048
SEQS = 8
TOKENS = 16384


def draw_token_document_ids(key, part):
    key = jax.random.fold_in(key, 11)
    first_key, second_key = jax.random.split(key)
    first_end = jax.random.randint(first_key, (SEQS, 1), 1, SPAN)
    last_start = jax.random.randint(second_key, (SEQS, 1), LEN - SPAN + 1, LEN)
    positions = jnp.arange(LEN, dtype=jnp.int32)[None, :]
    return (positions >= first_end).astype(jnp.int32) + (positions >= last_start).astype(jnp.int32)


def touch_ends(values, stream_key, smallest, high):
    longest = values.shape.index(max(values.shape))
    spots = []
    for shift in (0, 1):
        where = [jax.random.randint(jax.random.fold_in(stream_key, axis), (), 0, length) for axis, length in enumerate(values.shape)]
        where[longest] = (where[longest] + shift) % values.shape[longest]
        spots.append(tuple(where))
    return values.at[spots[0]].set(smallest).at[spots[1]].set(high)


def levels(own_key, dims, shards, low, top_value):
    def one(dim, blocks):
        steps = jax.random.uniform(jax.random.fold_in(jax.random.fold_in(own_key, 6), dim), (blocks,), jnp.float32, low / len(shards), top_value / len(shards))
        return jnp.repeat(jnp.exp(steps), dims[dim] // blocks).reshape((-1,) + (1,) * (len(dims) - dim - 1))

    level = one(*shards[0])
    for cut in shards[1:]:
        level = level * one(*cut)
    return level


def normal_values(rng, extent, scale, limit, shards=(), kind=jnp.bfloat16):
    level = levels(rng, extent, shards, -0.22, 0.18) if shards else 1.0
    array = jax.random.normal(rng, extent, jnp.float32) * scale * level
    return jnp.minimum(jnp.maximum(array, -limit), limit).astype(kind)


def setup_inputs(seed: int = 0) -> dict:
    key_of = jax.random.split(jax.random.key(seed), 26)
    return {
        "tokens": normal_values(key_of[0], (TOKENS, MODEL_WIDTH), 1.0, 6.0, ((0, 32),)),
        "cotangent": normal_values(key_of[1], (TOKENS, MODEL_WIDTH), 1.0, 6.0, ((0, 32),)),
        "token_document_ids": draw_token_document_ids(jax.random.fold_in(key_of[25], 71), 0),
        "sequence_adapter_index": touch_ends(jax.random.randint(key_of[3], (SEQS,), 0, ADAPTER_COUNT), jax.random.fold_in(key_of[3], 1), 0, ADAPTER_COUNT - 1).astype(jnp.int32),
        "mixer_norm_gain": jnp.clip(1.0 + 0.18 * jax.random.normal(key_of[4], (MODEL_WIDTH,), jnp.float32), 0.1, 1.9),
        "head_norm_gain": jnp.clip(1.0 + 0.18 * jax.random.normal(key_of[5], (HEAD_DIM,), jnp.float32), 0.1, 1.9),
        "feedforward_norm_gain": jnp.clip(1.0 + 0.18 * jax.random.normal(key_of[6], (MODEL_WIDTH,), jnp.float32), 0.1, 1.9),
        "short_filter_kernels": normal_values(key_of[7], (3, CONV, HEAD_FEATURES), CONV ** -0.5, 3.0, ((2, 4),), jnp.float32),
        "query_weight": normal_values(key_of[8], (MODEL_WIDTH, HEAD_FEATURES), MODEL_WIDTH ** -0.5, 0.125, ((0, 32), (1, 4))),
        "key_weight": normal_values(key_of[9], (MODEL_WIDTH, HEAD_FEATURES), MODEL_WIDTH ** -0.5, 0.125, ((0, 32), (1, 4))),
        "value_weight": normal_values(key_of[10], (MODEL_WIDTH, HEAD_FEATURES), MODEL_WIDTH ** -0.5, 0.125, ((0, 32), (1, 4))),
        "strength_weight": normal_values(key_of[11], (MODEL_WIDTH, HEAD_COUNT), MODEL_WIDTH ** -0.5, 0.125, ((0, 32), (1, 4))),
        "mixer_output_weight": normal_values(key_of[12], (HEAD_FEATURES, MODEL_WIDTH), HEAD_FEATURES ** -0.5, 0.125, ((0, 4), (1, 32))),
        "gate_weight": normal_values(key_of[13], (MODEL_WIDTH, HIDDEN_UNITS), MODEL_WIDTH ** -0.5, 0.125, ((0, 32), (1, 4))),
        "up_weight": normal_values(key_of[14], (MODEL_WIDTH, HIDDEN_UNITS), MODEL_WIDTH ** -0.5, 0.125, ((0, 32), (1, 4))),
        "down_weight": normal_values(key_of[15], (HIDDEN_UNITS, MODEL_WIDTH), HIDDEN_UNITS ** -0.5, 0.078125, ((0, 4), (1, 32))),
        "adapter_attention_input": normal_values(key_of[16], (4, ADAPTER_COUNT, MODEL_WIDTH, ADAPTER_RANK), MODEL_WIDTH ** -0.5, 0.125),
        "adapter_triple_output": normal_values(key_of[17], (3, ADAPTER_COUNT, ADAPTER_RANK, HEAD_FEATURES), ADAPTER_RANK ** -0.5, 1.5, ((3, 4),)),
        "adapter_strength_output": normal_values(key_of[18], (ADAPTER_COUNT, ADAPTER_RANK, HEAD_COUNT), ADAPTER_RANK ** -0.5, 1.5, ((2, 4),)),
        "adapter_projection_input": normal_values(key_of[19], (ADAPTER_COUNT, HEAD_FEATURES, ADAPTER_RANK), HEAD_FEATURES ** -0.5, 0.125, ((1, 4),)),
        "adapter_projection_output": normal_values(key_of[20], (ADAPTER_COUNT, ADAPTER_RANK, MODEL_WIDTH), ADAPTER_RANK ** -0.5, 1.5),
        "adapter_feedforward_input": normal_values(key_of[21], (2, ADAPTER_COUNT, MODEL_WIDTH, ADAPTER_RANK), MODEL_WIDTH ** -0.5, 0.125),
        "adapter_feedforward_output": normal_values(key_of[22], (2, ADAPTER_COUNT, ADAPTER_RANK, HIDDEN_UNITS), ADAPTER_RANK ** -0.5, 1.5, ((3, 4),)),
        "adapter_down_input": normal_values(key_of[23], (ADAPTER_COUNT, HIDDEN_UNITS, ADAPTER_RANK), HIDDEN_UNITS ** -0.5, 0.078125, ((1, 4),)),
        "adapter_down_output": normal_values(key_of[24], (ADAPTER_COUNT, ADAPTER_RANK, MODEL_WIDTH), ADAPTER_RANK ** -0.5, 1.5),
    }


EXACT_ARITHMETIC = lax.Precision.HIGHEST
EPSILON = 1e-06

@jax.custom_vjp
def low(v):
    return lax.optimization_barrier(v.astype(jnp.bfloat16)).astype(jnp.float32)

@jax.custom_vjp
def low_back(v):
    return v

def low_keep(v):
    return (low(v), None)

def low_pass(kept, grad):
    return (grad,)

def back_keep(v):
    return (v, None)

def back_low(kept, grad):
    return (low(grad),)
low.defvjp(low_keep, low_pass)
low_back.defvjp(back_keep, back_low)

def both_ways(values):
    return low_back(low(values))

def product(left, right):
    return jnp.dot(left, right, precision=EXACT_ARITHMETIC)

def rms_scale(values, gain):
    return values * lax.rsqrt(lax.optimization_barrier(jnp.mean(values * values, axis=-1, keepdims=True)) + EPSILON) * gain

def unit_rows(values):
    return values * lax.rsqrt(lax.optimization_barrier(jnp.sum(values * values, axis=-1, keepdims=True)) + EPSILON)

def block_solve(key_unit, value_rows, beta_rate, segments):
    tile_line_batch = segments.shape[0]
    same_doc = (segments[:, None] == segments[None, :]).astype(jnp.float32)
    row_ids = jnp.arange(tile_line_batch, dtype=jnp.int32)[:, None]
    col_ids = jnp.arange(tile_line_batch, dtype=jnp.int32)[None, :]
    strict = (row_ids > col_ids).astype(jnp.float32) * same_doc
    key_rows = jnp.transpose(key_unit, (1, 0, 2))
    values_head = jnp.transpose(value_rows, (1, 0, 2))
    rates = jnp.transpose(beta_rate, (1, 0))[:, :, None]
    key_gram = jnp.einsum('hik,hjk->hij', key_rows, key_rows, precision=EXACT_ARITHMETIC)
    unit_lower = jnp.eye(tile_line_batch, dtype=jnp.float32)[None] + rates * key_gram * strict[None]
    weighted_value = jax.scipy.linalg.solve_triangular(unit_lower, rates * key_rows, lower=True, unit_diagonal=True)
    state_updates = jax.scipy.linalg.solve_triangular(unit_lower, rates * values_head, lower=True, unit_diagonal=True)
    return (weighted_value, state_updates)

def block_step(recurrent_associative_matrix, pieces):
    query_unit, key_unit, weighted_value, state_updates, segments, previous = pieces
    tile_line_batch = segments.shape[0]
    same_doc = (segments[:, None] == segments[None, :]).astype(jnp.float32)
    row_ids = jnp.arange(tile_line_batch, dtype=jnp.int32)[:, None]
    col_ids = jnp.arange(tile_line_batch, dtype=jnp.int32)[None, :]
    causal = (row_ids >= col_ids).astype(jnp.float32) * same_doc
    running_recurrent_matrix = (segments == previous).astype(jnp.float32)
    closing_segment_number = (segments == segments[tile_line_batch - 1]).astype(jnp.float32)
    query_rows = jnp.transpose(query_unit, (1, 0, 2))
    key_rows = jnp.transpose(key_unit, (1, 0, 2))
    adjusted_target_vector = state_updates - running_recurrent_matrix[None, :, None] * jnp.einsum('iul,ilt->iut', weighted_value, recurrent_associative_matrix, precision=EXACT_ARITHMETIC)
    scores = jnp.einsum('hik,hjk->hij', query_rows, key_rows, precision=EXACT_ARITHMETIC) * causal[None]
    layer_outputs = running_recurrent_matrix[None, :, None] * jnp.einsum('iul,ilt->iut', query_rows, recurrent_associative_matrix, precision=EXACT_ARITHMETIC)
    layer_outputs = layer_outputs + jnp.einsum('hij,hjv->hiv', scores, adjusted_target_vector, precision=EXACT_ARITHMETIC)
    recurrent_associative_matrix = running_recurrent_matrix[tile_line_batch - 1] * recurrent_associative_matrix + jnp.einsum('ohk,ohz->okz', key_rows * closing_segment_number[None, :, None], adjusted_target_vector, precision=EXACT_ARITHMETIC)
    return (recurrent_associative_matrix, jnp.transpose(layer_outputs, (1, 0, 2)))

def span_run(recurrent_associative_matrix, query_unit, key_unit, value_rows, beta_rate, segments, previous, tile_line_batch):
    length, heads, head_dim = query_unit.shape
    blocks = length // tile_line_batch
    key_blocks = key_unit.reshape(blocks, tile_line_batch, heads, head_dim)
    segment_blocks = segments.reshape(blocks, tile_line_batch)
    weighted_value, state_updates = jax.vmap(block_solve)(key_blocks, value_rows.reshape(blocks, tile_line_batch, heads, value_rows.shape[2]), beta_rate.reshape(blocks, tile_line_batch, heads), segment_blocks)
    pieces = (query_unit.reshape(blocks, tile_line_batch, heads, head_dim), key_blocks, weighted_value, state_updates, segment_blocks, previous.reshape(blocks, tile_line_batch)[:, 0])
    recurrent_associative_matrix, layer_outputs = lax.scan(jax.checkpoint(block_step), recurrent_associative_matrix, pieces)
    return (layer_outputs.reshape(length, heads, value_rows.shape[2]), recurrent_associative_matrix)

def conv_mix(extended, kernels, seg_window):
    taps = kernels.shape[0]
    length = extended.shape[0] - taps + 1
    current = seg_window[taps - 1:]
    accumulated = jnp.zeros((length, extended.shape[1]), jnp.float32)
    for offset in range(taps):
        shifted = lax.slice_in_dim(extended, taps - 1 - offset, taps - 1 - offset + length, axis=0)
        same_doc = (lax.slice_in_dim(seg_window, taps - 1 - offset, taps - 1 - offset + length) == current).astype(jnp.float32)
        accumulated = accumulated + kernels[offset][None, :] * shifted * same_doc[:, None]
    return accumulated

def choose(lookup_table, pick, axis):
    return jnp.tensordot(pick, jnp.moveaxis(lookup_table, axis, 0), axes=1, precision=EXACT_ARITHMETIC)

def layer(inputs, segments, pick, frozen, adapter_choices_list):
    mixer_norm_gain, head_norm_gain, feedforward_norm_gain, short_filter_kernels, query_weight, key_weight, value_weight, strength_weight, mixer_output_weight, gate_weight, up_weight, down_weight = frozen
    attention_input_maps = choose(adapter_choices_list[0], pick, 1)
    triple_output_maps = choose(adapter_choices_list[1], pick, 1)
    strength_output_maps = choose(adapter_choices_list[2], pick, 0)
    projection_input_maps = choose(adapter_choices_list[3], pick, 0)
    projection_output_maps = choose(adapter_choices_list[4], pick, 0)
    feedforward_input_maps = choose(adapter_choices_list[5], pick, 1)
    feedforward_output_maps = choose(adapter_choices_list[6], pick, 1)
    down_input_maps = choose(adapter_choices_list[7], pick, 0)
    down_output_maps = choose(adapter_choices_list[8], pick, 0)
    length = inputs.shape[0]
    heads = strength_weight.shape[1]
    head_dim = head_norm_gain.shape[0]
    taps = short_filter_kernels.shape[1]
    normed = low(rms_scale(inputs, mixer_norm_gain))
    low_attn = both_ways(jnp.einsum('td,pdr->ptr', normed, attention_input_maps, precision=EXACT_ARITHMETIC))
    projected = jnp.concatenate([product(normed, query_weight) + product(low_attn[0], triple_output_maps[0]), product(normed, key_weight) + product(low_attn[1], triple_output_maps[1]), product(normed, value_weight) + product(low_attn[2], triple_output_maps[2])], axis=1)
    projected = low_back(projected)
    beta_logit = low_back(product(normed, strength_weight) + product(low_attn[3], strength_output_maps))
    pad_rows = jnp.zeros((taps - 1, projected.shape[1]), jnp.float32)
    pad_ids = jnp.full((taps - 1,), -1, jnp.int32)
    seg_window = jnp.concatenate([pad_ids, segments.astype(jnp.int32)])
    kernels = jnp.transpose(short_filter_kernels, (1, 0, 2)).reshape(taps, -1)
    mixed = jax.nn.silu(conv_mix(jnp.concatenate([pad_rows, projected], axis=0), kernels, seg_window))
    parts = mixed.reshape(length, 3, heads, head_dim)
    query_unit = unit_rows(parts[:, 0]) * head_dim ** (-0.5)
    key_unit = unit_rows(parts[:, 1])
    value_rows = parts[:, 2]
    beta_rate = jax.nn.sigmoid(beta_logit)
    previous = seg_window[taps - 2:taps - 2 + length]
    recurrent_associative_matrix = jnp.zeros((heads, head_dim, head_dim), jnp.float32)
    attended, unused_end = span_run(recurrent_associative_matrix, query_unit, key_unit, value_rows, beta_rate, seg_window[taps - 1:], previous, BLOCK)
    head_out = low(rms_scale(attended, head_norm_gain).reshape(length, heads * head_dim))
    low_o = both_ways(product(head_out, projection_input_maps))
    branch = low_back(product(head_out, mixer_output_weight) + product(low_o, projection_output_maps))
    middle = inputs + branch
    normed_ffn = low(rms_scale(middle, feedforward_norm_gain))
    low_ffn = both_ways(jnp.einsum('td,pdr->ptr', normed_ffn, feedforward_input_maps, precision=EXACT_ARITHMETIC))
    gate_act = low_back(product(normed_ffn, gate_weight) + product(low_ffn[0], feedforward_output_maps[0]))
    up_act = low_back(product(normed_ffn, up_weight) + product(low_ffn[1], feedforward_output_maps[1]))
    hidden = low(jax.nn.silu(gate_act) * up_act)
    low_down = both_ways(product(hidden, down_input_maps))
    return middle + low_back(product(hidden, down_weight) + product(low_down, down_output_maps))

def reference(tokens, cotangent, token_document_ids, sequence_adapter_index, mixer_norm_gain, head_norm_gain, feedforward_norm_gain, short_filter_kernels, query_weight, key_weight, value_weight, strength_weight, mixer_output_weight, gate_weight, up_weight, down_weight, adapter_attention_input, adapter_triple_output, adapter_strength_output, adapter_projection_input, adapter_projection_output, adapter_feedforward_input, adapter_feedforward_output, adapter_down_input, adapter_down_output):
    frozen = tuple((lookup_table.astype(jnp.float32) for lookup_table in (mixer_norm_gain, head_norm_gain, feedforward_norm_gain, short_filter_kernels, query_weight, key_weight, value_weight, strength_weight, mixer_output_weight, gate_weight, up_weight, down_weight)))
    adapter_choices_list = tuple((lookup_table.astype(jnp.float32) for lookup_table in (adapter_attention_input, adapter_triple_output, adapter_strength_output, adapter_projection_input, adapter_projection_output, adapter_feedforward_input, adapter_feedforward_output, adapter_down_input, adapter_down_output)))
    inputs_all = tokens.astype(jnp.float32).reshape(SEQS, LEN, MODEL_WIDTH)
    cotangent_all = cotangent.astype(jnp.float32).reshape(SEQS, LEN, MODEL_WIDTH)

    def one_sequence(totals, items):
        inputs, grad_out, segments, chosen_adapter = items
        pick = (jnp.arange(ADAPTER_COUNT, dtype=jnp.int32) == chosen_adapter).astype(jnp.float32)

        def forward(values, tables):
            return layer(values, segments, pick, frozen, tables)
        layer_outputs, backward = jax.vjp(forward, inputs, adapter_choices_list)
        grad_inputs, grad_tables = backward(grad_out)
        totals = jax.tree.map(lambda first, second: first + second, totals, grad_tables)
        return (totals, (layer_outputs.astype(jnp.bfloat16), grad_inputs))
    start_totals = tuple((jnp.zeros_like(lookup_table) for lookup_table in adapter_choices_list))
    totals, (outputs_all, grads_all) = lax.scan(one_sequence, start_totals, (inputs_all, cotangent_all, token_document_ids.astype(jnp.int32), sequence_adapter_index.astype(jnp.int32)))
    return (outputs_all.reshape(TOKENS, MODEL_WIDTH), grads_all.reshape(TOKENS, MODEL_WIDTH), totals[0], totals[1], totals[2], totals[3], totals[4], totals[5], totals[6], totals[7], totals[8])
```

```python
import functools

import jax
import jax.numpy as jnp
from jax import lax
from jax.experimental import pallas as pl
from jax.experimental.pallas import tpu as pltpu
from jax.sharding import PartitionSpec as P

EPSILON = 1e-06
HALO = 8
CHUNK = 128
LANES = 128
F32 = jnp.float32
BF16 = jnp.bfloat16
VMEM_LIMIT = 48 * 1024 * 1024


def dot_low(left, right, left_dim=1, right_dim=0):
    return lax.dot_general(
        left.astype(BF16),
        right.astype(BF16),
        (((left_dim,), (right_dim,)), ((), ())),
        preferred_element_type=F32,
    )


def split(values):
    high = values.astype(BF16)
    return high, (values - high.astype(F32)).astype(BF16)


def dot_fine(left, right, left_dim=1, right_dim=0):
    left_high, left_low = split(left)
    right_high, right_low = split(right)
    dims = (((left_dim,), (right_dim,)), ((), ()))
    product = functools.partial(lax.dot_general, dimension_numbers=dims, preferred_element_type=F32)
    return product(left_high, right_high) + (
        product(left_high, right_low) + product(left_low, right_high)
    )


def conv_rows(x_ref, columns, taps_ref, seg_ref, span):
    here = seg_ref[HALO : HALO + span, :]
    total = taps_ref[0:1, columns] * x_ref[HALO : HALO + span, columns]
    for tap in range(1, taps_ref.shape[0]):
        same = (seg_ref[HALO - tap : HALO - tap + span, :] == here).astype(F32)
        total = total + taps_ref[tap : tap + 1, columns] * (
            x_ref[HALO - tap : HALO - tap + span, columns] * same
        )
    return total


def inverse_norm(values):
    return lax.rsqrt(jnp.sum(values * values, axis=-1, keepdims=True) + EPSILON)


def head_column(array, head):
    lane = lax.broadcasted_iota(jnp.int32, array.shape, 1)
    return jnp.sum(jnp.where(lane == head, array, 0.0), axis=1, keepdims=True)


def chunk_masks(seg_ref, row_ref, chunk):
    start = HALO + chunk * CHUNK
    column = seg_ref[start : start + CHUNK, :]
    row = row_ref[chunk : chunk + 1, :]
    before = seg_ref[start - 1 : start, :]
    last = seg_ref[start + CHUNK - 1 : start + CHUNK, :]
    same = column == row
    row_ids = lax.broadcasted_iota(jnp.int32, (CHUNK, CHUNK), 0)
    col_ids = lax.broadcasted_iota(jnp.int32, (CHUNK, CHUNK), 1)
    strict = (same & (row_ids > col_ids)).astype(F32)
    causal = (same & (row_ids >= col_ids)).astype(F32)
    running = (column == before).astype(F32)
    closing = (column == last).astype(F32)
    carried = (before == last).astype(F32)
    return strict, causal, running, closing, carried


def unit_lower_inverses(lowers):
    size = lowers[0].shape[0]
    row_ids = lax.broadcasted_iota(jnp.int32, (size, size), 0)
    col_ids = lax.broadcasted_iota(jnp.int32, (size, size), 1)
    identity = (row_ids == col_ids).astype(F32)
    pair = (row_ids >> 1) == (col_ids >> 1)
    inverses = [identity - jnp.where(pair, lower, 0.0) for lower in lowers]
    bits = 2
    while (1 << bits) <= size:
        joined = ((row_ids >> bits) == (col_ids >> bits)) & (
            (row_ids >> (bits - 1)) != (col_ids >> (bits - 1))
        )
        inner = [
            dot_fine(jnp.where(joined, lower, 0.0), inverse)
            for lower, inverse in zip(lowers, inverses)
        ]
        inverses = [
            inverse - dot_fine(inverse, part) for inverse, part in zip(inverses, inner)
        ]
        bits += 1
    return inverses


def delta_local_kernel(
    q_ref, k_ref, v_ref, logit_ref, taps_q, taps_k, taps_v, seg_ref, row_ref,
    qp_ref, op_ref, map_ref, inverse_ref, prefix_ref, *, span, head_dim, group,
):
    chunks = span // CHUNK
    step = pl.program_id(0)
    masks = [chunk_masks(seg_ref, row_ref, chunk) for chunk in range(chunks)]
    rates_all = jax.nn.sigmoid(logit_ref[HALO : HALO + span, :])
    work = []
    for local in range(group):
        columns = slice(local * head_dim, (local + 1) * head_dim)
        queries = jax.nn.silu(conv_rows(q_ref, columns, taps_q, seg_ref, span))
        queries = queries * (inverse_norm(queries) * head_dim**-0.5)
        keys = jax.nn.silu(conv_rows(k_ref, columns, taps_k, seg_ref, span))
        keys = keys * inverse_norm(keys)
        values = jax.nn.silu(conv_rows(v_ref, columns, taps_v, seg_ref, span))
        rates = head_column(rates_all, step * group + local)
        for chunk in range(chunks):
            rows = slice(chunk * CHUNK, (chunk + 1) * CHUNK)
            work.append((local, chunk, queries[rows], keys[rows], values[rows], rates[rows]))
    lowers = [
        dot_fine(keys, keys, 1, 1) * (rates * masks[chunk][0])
        for _, chunk, _, keys, _, rates in work
    ]
    inverses = unit_lower_inverses(lowers)
    prefix = None
    for (local, chunk, queries, keys, values, rates), inverse in zip(work, inverses):
        columns = slice(local * head_dim, (local + 1) * head_dim)
        rows = slice(chunk * CHUNK, (chunk + 1) * CHUNK)
        strict, causal, running, closing, carried = masks[chunk]
        inverse_ref[local, rows, :] = inverse
        solved = dot_fine(inverse, jnp.concatenate([rates * values, rates * keys], axis=1))
        updates = solved[:, :head_dim]
        weighted = running * solved[:, head_dim:]
        both = jnp.concatenate([updates, weighted], axis=1)
        scores = dot_low(queries, keys, 1, 1) * causal
        near = dot_low(scores, both)
        ends = dot_low(closing * keys, both, 0, 0)
        reach = running * queries - near[:, head_dim:]
        if chunk == 0:
            row_ids = lax.broadcasted_iota(jnp.int32, (head_dim, head_dim), 0)
            col_ids = lax.broadcasted_iota(jnp.int32, (head_dim, head_dim), 1)
            identity = (row_ids == col_ids).astype(F32)
            prefix = jnp.concatenate([jnp.zeros((head_dim, head_dim), F32), identity], axis=1)
        prefix_ref[local, chunk * head_dim : (chunk + 1) * head_dim, :] = prefix
        seen = dot_low(reach, prefix)
        op_ref[rows, columns] = near[:, :head_dim] + seen[:, :head_dim]
        qp_ref[rows, columns] = seen[:, head_dim:].astype(BF16)
        moved = carried * prefix - dot_low(ends[:, head_dim:], prefix)
        prefix = jnp.concatenate(
            [moved[:, :head_dim] + ends[:, :head_dim], moved[:, head_dim:]], axis=1
        )
        if chunk == chunks - 1:
            map_ref[local] = prefix.astype(BF16)


def delta_local(projected, taps, seg_column, seg_rows, heads, head_dim, span, group):
    rows = projected.shape[0]
    width = group * head_dim
    steps = heads // group
    third = lambda part: pl.BlockSpec((rows, width), lambda i: (0, part * steps + i))
    tap_third = lambda part: pl.BlockSpec((taps.shape[0], width), lambda i: (0, part * steps + i))
    whole = lambda array: pl.BlockSpec(array.shape, lambda i: (0,) * array.ndim)
    chunks = span // CHUNK
    return pl.pallas_call(
        functools.partial(delta_local_kernel, span=span, head_dim=head_dim, group=group),
        grid=(steps,),
        in_specs=[
            third(0), third(1), third(2),
            pl.BlockSpec((rows, LANES), lambda i: (0, 3 * heads * head_dim // LANES)),
            tap_third(0), tap_third(1), tap_third(2), whole(seg_column), whole(seg_rows),
        ],
        out_specs=[
            pl.BlockSpec((span, width), lambda i: (0, i)),
            pl.BlockSpec((span, width), lambda i: (0, i)),
            pl.BlockSpec((group, head_dim, 2 * head_dim), lambda i: (i, 0, 0)),
            pl.BlockSpec((group, span, CHUNK), lambda i: (i, 0, 0)),
            pl.BlockSpec((group, chunks * head_dim, 2 * head_dim), lambda i: (i, 0, 0)),
        ],
        out_shape=[
            jax.ShapeDtypeStruct((span, heads * head_dim), BF16),
            jax.ShapeDtypeStruct((span, heads * head_dim), F32),
            jax.ShapeDtypeStruct((heads, head_dim, 2 * head_dim), BF16),
            jax.ShapeDtypeStruct((heads, span, CHUNK), F32),
            jax.ShapeDtypeStruct((heads, chunks * head_dim, 2 * head_dim), F32),
        ],
        compiler_params=pltpu.CompilerParams(vmem_limit_bytes=VMEM_LIMIT),
        name="delta_local",
    )(projected, projected, projected, projected, taps, taps, taps, seg_column, seg_rows)


def attend_kernel(op_ref, qp_ref, one_ref, two_ref, three_ref, gain_ref, out_ref, att_ref, state_ref):
    heads, head_dim = one_ref.shape[0], one_ref.shape[1]
    for head in range(heads):
        columns = slice(head * head_dim, (head + 1) * head_dim)
        state = two_ref[head, :, :head_dim].astype(F32) + dot_low(
            two_ref[head, :, head_dim:], three_ref[head]
        )
        state = one_ref[head, :, :head_dim].astype(F32) + dot_low(
            one_ref[head, :, head_dim:], state
        )
        state_ref[head] = state
        attended = op_ref[:, columns] + dot_low(qp_ref[:, columns], state)
        att_ref[:, columns] = attended
        scale = lax.rsqrt(jnp.mean(attended * attended, axis=-1, keepdims=True) + EPSILON)
        out_ref[:, columns] = (attended * scale * gain_ref[...]).astype(BF16)


def attend(op, qp, one, two, three, gain):
    heads, head_dim = one.shape[0], one.shape[1]
    return pl.pallas_call(
        attend_kernel,
        out_shape=[
            jax.ShapeDtypeStruct(op.shape, BF16),
            jax.ShapeDtypeStruct(op.shape, F32),
            jax.ShapeDtypeStruct((heads, head_dim, head_dim), F32),
        ],
        compiler_params=pltpu.CompilerParams(vmem_limit_bytes=VMEM_LIMIT),
        name="attend",
    )(op, qp, one, two, three, gain)


def attend_back_kernel(grad_ref, att_ref, qp_ref, gain_ref, out_ref, own_ref):
    heads, head_dim = own_ref.shape[0], own_ref.shape[1]
    for head in range(heads):
        columns = slice(head * head_dim, (head + 1) * head_dim)
        attended = att_ref[:, columns]
        scale = lax.rsqrt(jnp.mean(attended * attended, axis=-1, keepdims=True) + EPSILON)
        gained = grad_ref[:, columns] * gain_ref[...]
        along = jnp.mean(attended * gained, axis=-1, keepdims=True)
        grad = scale * gained - attended * (scale * scale * scale * along)
        out_ref[:, columns] = grad
        own_ref[head] = dot_low(qp_ref[:, columns], grad, 0, 0).astype(BF16)


def attend_back(grad, attended, qp, gain, heads, head_dim):
    return pl.pallas_call(
        attend_back_kernel,
        out_shape=[
            jax.ShapeDtypeStruct(grad.shape, F32),
            jax.ShapeDtypeStruct((heads, head_dim, head_dim), BF16),
        ],
        compiler_params=pltpu.CompilerParams(vmem_limit_bytes=VMEM_LIMIT),
        name="attend_back",
    )(grad, attended, qp, gain)


def delta_back_kernel(
    q_ref, k_ref, v_ref, logit_ref, taps_q, taps_k, taps_v, seg_ref, row_ref,
    inverse_ref, prefix_ref, state_ref, grad_ref,
    own_one, own_two, own_three, map_one, map_two,
    out_ref, halo_ref, tail_ref, dz_ref, *, span, heads, head_dim, group,
):
    chunks = span // CHUNK
    step = pl.program_id(0)
    features = heads * head_dim
    masks = [chunk_masks(seg_ref, row_ref, chunk) for chunk in range(chunks)]
    rates_all = jax.nn.sigmoid(logit_ref[HALO : HALO + span, :])
    lane = lax.broadcasted_iota(jnp.int32, (CHUNK, LANES), 1)
    dz_ref[0:HALO, :] = jnp.zeros((HALO, head_dim), F32)
    dz_ref[HALO + span :, :] = jnp.zeros((HALO, head_dim), F32)

    @pl.when(step == 0)
    def _():
        out_ref[:, 3 * features :] = jnp.zeros((span, LANES), BF16)

    for local in range(group):
        columns = slice(local * head_dim, (local + 1) * head_dim)
        conv_q = conv_rows(q_ref, columns, taps_q, seg_ref, span)
        conv_k = conv_rows(k_ref, columns, taps_k, seg_ref, span)
        conv_v = conv_rows(v_ref, columns, taps_v, seg_ref, span)
        raw_q = jax.nn.silu(conv_q)
        raw_k = jax.nn.silu(conv_k)
        values_all = jax.nn.silu(conv_v)
        scale_q = inverse_norm(raw_q)
        scale_k = inverse_norm(raw_k)
        queries_all = raw_q * (scale_q * head_dim**-0.5)
        keys_all = raw_k * scale_k
        head = step * group + local
        rates_head = head_column(rates_all, head)
        entry = state_ref[local]
        kept = []
        for chunk in range(chunks):
            rows = slice(chunk * CHUNK, (chunk + 1) * CHUNK)
            strict, causal, running, closing, carried = masks[chunk]
            queries, keys, values = queries_all[rows], keys_all[rows], values_all[rows]
            rates = rates_head[rows]
            inverse = inverse_ref[local, rows, :]
            gram = dot_low(keys, keys, 1, 1)
            solved = dot_fine(inverse, jnp.concatenate([rates * values, rates * keys], axis=1))
            weighted = running * solved[:, head_dim:]
            prefix = prefix_ref[local, chunk * head_dim : (chunk + 1) * head_dim, :]
            state = prefix[:, :head_dim] + dot_low(prefix[:, head_dim:], entry)
            errors = solved[:, :head_dim] - dot_low(weighted, state)
            scores = dot_low(queries, keys, 1, 1) * causal
            grad = grad_ref[rows, columns]
            near = dot_low(scores, grad, 0, 0)
            far = dot_low(running * queries, grad, 0, 0)
            grad_scores = dot_low(grad, errors, 1, 1) * causal
            kept.append((queries, keys, values, rates, inverse, gram, solved, weighted, state,
                         errors, grad, near, far, grad_scores))
        leaving = own_two[local].astype(F32) + dot_low(
            map_two[local, :, head_dim:], own_three[local], 0, 0
        )
        leaving = own_one[local].astype(F32) + dot_low(
            map_one[local, :, head_dim:], leaving, 0, 0
        )
        leavings = [None] * chunks
        grad_errors_all = [None] * chunks
        for chunk in reversed(range(chunks)):
            strict, causal, running, closing, carried = masks[chunk]
            keys, weighted, near, far = (kept[chunk][i] for i in (1, 7, 11, 12))
            leavings[chunk] = leaving
            grad_errors = near + closing * dot_low(keys, leaving)
            grad_errors_all[chunk] = grad_errors
            leaving = carried * leaving + far - dot_low(weighted, grad_errors, 0, 0)
        grads = [[], [], []]
        for chunk in range(chunks):
            rows = slice(chunk * CHUNK, (chunk + 1) * CHUNK)
            strict, causal, running, closing, carried = masks[chunk]
            (queries, keys, values, rates, inverse, gram, solved, weighted, state,
             errors, grad, near, far, grad_scores) = kept[chunk]
            grad_errors, leaving = grad_errors_all[chunk], leavings[chunk]
            grad_queries = running * dot_low(grad, state, 1, 1) + dot_low(grad_scores, keys)
            grad_keys = dot_low(grad_scores, queries, 0, 0) + closing * dot_low(
                errors, leaving, 1, 1
            )
            grad_weighted = -running * dot_low(grad_errors, state, 1, 1)
            grad_right = dot_fine(
                inverse, jnp.concatenate([grad_errors, grad_weighted], axis=1), 0, 0
            )
            right_v, right_k = grad_right[:, :head_dim], grad_right[:, head_dim:]
            grad_lower = -dot_low(grad_right, solved, 1, 1) * strict
            grad_rates = (
                jnp.sum(right_v * values, axis=1, keepdims=True)
                + jnp.sum(right_k * keys, axis=1, keepdims=True)
                + jnp.sum(grad_lower * gram, axis=1, keepdims=True)
            )
            grad_gram = rates * grad_lower
            grad_keys = (
                grad_keys
                + rates * right_k
                + dot_low(grad_gram, keys)
                + dot_low(grad_gram, keys, 0, 0)
            )
            grad_logit = grad_rates * rates * (1.0 - rates)
            previous = out_ref[rows, 3 * features :].astype(F32)
            out_ref[rows, 3 * features :] = jnp.where(lane == head, grad_logit, previous).astype(BF16)
            grads[0].append(grad_queries)
            grads[1].append(grad_keys)
            grads[2].append(rates * right_v)
        here = seg_ref[0 : HALO + span, :]
        for part, (conv, raw, scale, taps) in enumerate(
            ((conv_q, raw_q, scale_q, taps_q), (conv_k, raw_k, scale_k, taps_k), (conv_v, None, None, taps_v))
        ):
            grad = jnp.concatenate(grads[part], axis=0)
            if part < 2:
                if part == 0:
                    grad = grad * head_dim**-0.5
                unit = raw * scale
                grad = scale * (grad - unit * jnp.sum(unit * grad, axis=-1, keepdims=True))
            sig = jax.nn.sigmoid(conv)
            dz_ref[HALO : HALO + span, :] = grad * (sig * (1.0 + conv * (1.0 - sig)))
            total = taps[0:1, columns] * dz_ref[0 : HALO + span, :]
            for tap in range(1, taps.shape[0]):
                same = (seg_ref[tap : tap + HALO + span, :] == here).astype(F32)
                total = total + taps[tap : tap + 1, columns] * (
                    dz_ref[tap : tap + HALO + span, :] * same
                )
            place = pl.ds(pl.multiple_of(part * features + head * head_dim, LANES), head_dim)
            halo_ref[:, place] = total[:HALO]
            tail_ref[:, place] = total[span:]
            out_ref[:, place] = total[HALO:].astype(BF16)


def delta_back(
    projected, taps, seg_column, seg_rows, inverse, prefix, state, grad,
    owns, maps, heads, head_dim, span, group,
):
    rows = projected.shape[0]
    width = group * head_dim
    steps = heads // group
    chunks = span // CHUNK
    third = lambda part: pl.BlockSpec((rows, width), lambda i: (0, part * steps + i))
    tap_third = lambda part: pl.BlockSpec((taps.shape[0], width), lambda i: (0, part * steps + i))
    whole = lambda array: pl.BlockSpec(array.shape, lambda i: (0,) * array.ndim)
    by_head = lambda array: pl.BlockSpec((group,) + array.shape[1:], lambda i: (i, 0, 0))
    total = 3 * heads * head_dim
    return pl.pallas_call(
        functools.partial(
            delta_back_kernel, span=span, heads=heads, head_dim=head_dim, group=group
        ),
        grid=(steps,),
        in_specs=[
            third(0), third(1), third(2),
            pl.BlockSpec((rows, LANES), lambda i: (0, total // LANES)),
            tap_third(0), tap_third(1), tap_third(2), whole(seg_column), whole(seg_rows),
            by_head(inverse), by_head(prefix), by_head(state),
            pl.BlockSpec((span, width), lambda i: (0, i)),
            by_head(owns[0]), by_head(owns[1]), by_head(owns[2]),
            by_head(maps[0]), by_head(maps[1]),
        ],
        out_specs=[
            pl.BlockSpec((span, total + LANES), lambda i: (0, 0)),
            pl.BlockSpec((HALO, total), lambda i: (0, 0)),
            pl.BlockSpec((HALO, total), lambda i: (0, 0)),
        ],
        out_shape=[
            jax.ShapeDtypeStruct((span, total + LANES), BF16),
            jax.ShapeDtypeStruct((HALO, total), F32),
            jax.ShapeDtypeStruct((HALO, total), F32),
        ],
        scratch_shapes=[pltpu.VMEM((span + 2 * HALO, head_dim), F32)],
        compiler_params=pltpu.CompilerParams(vmem_limit_bytes=VMEM_LIMIT),
        name="delta_back",
    )(
        projected, projected, projected, projected, taps, taps, taps, seg_column, seg_rows,
        inverse, prefix, state, grad, *owns, *maps,
    )


def shifted(block, axis, distance, wrap=True):
    size = lax.axis_size(axis)
    if wrap:
        route = [(i, (i + distance) % size) for i in range(size)]
    else:
        route = [(i, i + distance) for i in range(size) if 0 <= i + distance < size]
    return lax.ppermute(block, axis, route)


def order_of(size):
    return sorted(range(1, size), key=lambda k: -min(k, size - k))


def sum_to_owners(parts, axis):
    size = len(parts)
    received = {k: shifted(parts[k].astype(BF16), axis, k) for k in order_of(size)}
    total = parts[0].astype(F32)
    for k in range(1, size):
        total = total + received[k].astype(F32)
    return total


def blocks_of_others(block, axis):
    size = lax.axis_size(axis)
    received = {k: shifted(block, axis, -k) for k in order_of(size)}
    return [block] + [received[k] for k in range(1, size)]


def paired_sum(block, axis):
    blocks = [part.astype(F32) for part in blocks_of_others(block, axis)]
    half = len(blocks) // 2
    while half:
        blocks = [blocks[i] + blocks[i + half] for i in range(half)]
        half //= 2
    return blocks[0]


def dot(left, right):
    return jnp.dot(left, right, preferred_element_type=F32)


def dot_nt(left, right):
    return lax.dot_general(left, right, (((1,), (1,)), ((), ())), preferred_element_type=F32)


def dot_tn(left, right):
    return lax.dot_general(left, right, (((0,), (0,)), ((), ())), preferred_element_type=F32)


def rms_scale(values, gain):
    return values * lax.rsqrt(jnp.mean(values * values, axis=-1, keepdims=True) + EPSILON) * gain


def rms_back(values, gain, grad):
    scale = lax.rsqrt(jnp.mean(values * values, axis=-1, keepdims=True) + EPSILON)
    gained = gain * grad
    return scale * gained - values * (scale**3) * jnp.mean(values * gained, axis=-1, keepdims=True)


def pad_columns(array, width):
    return jnp.pad(array, ((0, 0), (0, width - array.shape[1])))


def pad_rows(array, height):
    return jnp.pad(array, ((0, height - array.shape[0]), (0, 0)))


def on_device(
    tokens,
    cotangent,
    token_document_ids,
    sequence_adapter_index,
    mixer_norm_gain,
    head_norm_gain,
    feedforward_norm_gain,
    short_filter_kernels,
    query_weight,
    key_weight,
    value_weight,
    strength_weight,
    mixer_output_weight,
    gate_weight,
    up_weight,
    down_weight,
    adapter_attention_input,
    adapter_triple_output,
    adapter_strength_output,
    adapter_projection_input,
    adapter_projection_output,
    adapter_feedforward_input,
    adapter_feedforward_output,
    adapter_down_input,
    adapter_down_output,
):
    span, model = tokens.shape
    head_dim = head_norm_gain.shape[0]
    taps = short_filter_kernels.shape[1]
    heads = strength_weight.shape[1]
    features = heads * head_dim
    hidden_units = gate_weight.shape[1]
    adapters = adapter_attention_input.shape[1]
    rank = adapter_attention_input.shape[3]
    owners = lax.axis_size("tensor")
    place = lax.axis_index("tensor")
    position = lax.axis_index("context")
    share = span // owners
    everyone = ("weights", "context")

    def chunk_at(array, k):
        start = lax.rem(place + k, owners) * share
        return lax.dynamic_slice_in_dim(array, start, share, axis=0)

    mixer_pack = jnp.concatenate(
        [query_weight, key_weight, value_weight, pad_columns(strength_weight, LANES),
         mixer_output_weight.T], axis=1
    )
    ffn_pack = jnp.concatenate([gate_weight, up_weight, down_weight.T], axis=1)
    mixer_all = lax.all_gather(mixer_pack, everyone, axis=0, tiled=True)
    ffn_all = lax.all_gather(ffn_pack, everyone, axis=0, tiled=True)
    triple = 3 * features + LANES
    weight_in = mixer_all[:, :triple]
    weight_out = mixer_all[:, triple:]

    chosen = sequence_adapter_index[0]
    take = lambda table, axis: lax.dynamic_index_in_dim(table, chosen, axis, keepdims=False)
    attention_in = jnp.swapaxes(take(adapter_attention_input, 1), 1, 2).reshape(4 * rank, model)
    triple_out = take(adapter_triple_output, 1)
    strength_out = take(adapter_strength_output, 0)
    projection_in = jnp.swapaxes(take(adapter_projection_input, 0), 0, 1)
    projection_out = take(adapter_projection_output, 0)
    feedforward_in = jnp.swapaxes(take(adapter_feedforward_input, 1), 1, 2).reshape(2 * rank, model)
    feedforward_out = take(adapter_feedforward_output, 1)
    down_in = jnp.swapaxes(take(adapter_down_input, 0), 0, 1)
    down_out = take(adapter_down_output, 0)
    low_in = jnp.concatenate(
        [
            jnp.pad(triple_out[part], ((0, 0), (part * features, (2 - part) * features + LANES)))
            for part in range(3)
        ]
        + [jnp.pad(strength_out, ((0, 0), (3 * features, LANES - heads)))],
        axis=0,
    )

    padded_ids = jnp.concatenate(
        [jnp.full((HALO,), -1, jnp.int32), token_document_ids[0], jnp.full((HALO,), -2, jnp.int32)]
    )
    window = lax.dynamic_slice_in_dim(padded_ids, position * span, span + 2 * HALO)
    window = jnp.where(
        jnp.arange(span + 2 * HALO) < span + HALO, window, jnp.full_like(window, -2)
    )
    seg_column = window[:, None]
    seg_rows = window[HALO : HALO + span].reshape(span // CHUNK, CHUNK)
    kernels = jnp.transpose(short_filter_kernels, (1, 0, 2)).reshape(taps, -1)

    edge = shifted(tokens[span - HALO :], "context", 1, wrap=False)
    inputs_ext = jnp.concatenate([edge, tokens], axis=0).astype(F32)
    normed_ext = rms_scale(inputs_ext, mixer_norm_gain).astype(BF16)
    low_ext = dot_nt(normed_ext, attention_in).astype(BF16)
    projected = dot(normed_ext, weight_in) + dot(low_ext, low_in)
    normed = normed_ext[HALO:]
    low_attn = low_ext[HALO:]

    group = 1
    qp, op, maps, inverse, prefix = delta_local(
        projected, kernels, seg_column, seg_rows, heads, head_dim, span, group
    )
    three = shifted(maps[:, :, :head_dim], "context", 3, wrap=False)
    two = shifted(maps, "context", 2, wrap=False)
    one = shifted(maps, "context", 1, wrap=False)
    map_two = shifted(maps, "context", -2, wrap=False)
    map_one = shifted(maps, "context", -1, wrap=False)
    gain_row = head_norm_gain[None, :]
    head_low, attended, state = attend(op, qp, one, two, three, gain_row)

    out_ext = jnp.concatenate([weight_out, pad_rows(projection_in, LANES)], axis=0)
    branch = sum_to_owners(
        [dot_nt(chunk_at(head_low, k), out_ext) for k in range(owners)], "tensor"
    )
    low_o = branch[:, model : model + rank].astype(BF16)
    inputs_own = chunk_at(tokens, 0).astype(F32)
    middle = inputs_own + branch[:, :model] + dot(low_o, projection_out)
    normed_ffn = rms_scale(middle, feedforward_norm_gain).astype(BF16)
    low_ffn = dot_nt(normed_ffn, feedforward_in).astype(BF16)
    ffn_in = blocks_of_others(
        jnp.concatenate([normed_ffn, pad_columns(low_ffn, LANES)], axis=1), "tensor"
    )

    ffn_low = jnp.concatenate(
        [
            jnp.pad(feedforward_out[0], ((0, 0), (0, hidden_units))),
            jnp.pad(feedforward_out[1], ((0, 0), (hidden_units, 0))),
        ],
        axis=0,
    )
    gate_up_ext = jnp.concatenate([ffn_all[:, : 2 * hidden_units], pad_rows(ffn_low, LANES)], axis=0)
    down_ext = jnp.concatenate([ffn_all[:, 2 * hidden_units :], pad_rows(down_in, LANES)], axis=0)
    cot_own = chunk_at(cotangent, 0)
    low_grad_down = dot_nt(cotangent, down_out).astype(BF16)
    cot_ext = jnp.concatenate([cotangent, pad_columns(low_grad_down, LANES)], axis=1)
    grad_hidden_all = dot(cot_ext, down_ext)

    down_parts, back_parts, hidden_blocks, ffn_grads = [None] * owners, [None] * owners, [], []
    grad_down_in = 0.0
    grad_ffn_out = 0.0
    for k in [0, 1, 3, 2] if owners == 4 else range(owners):
        both = dot(ffn_in[k], gate_up_ext)
        gate_act, up_act = both[:, :hidden_units], both[:, hidden_units:]
        sig = jax.nn.sigmoid(gate_act)
        silu = gate_act * sig
        hidden = (silu * up_act).astype(BF16)
        grad_hidden = chunk_at(grad_hidden_all, k)
        grad_gate = (grad_hidden * up_act * (sig * (1.0 + gate_act * (1.0 - sig)))).astype(BF16)
        grad_up = (grad_hidden * silu).astype(BF16)
        grads = jnp.concatenate([grad_gate, grad_up], axis=1)
        back_parts[k] = dot_nt(grads, gate_up_ext)
        down_parts[k] = (hidden, grads)
        grad_down_in = grad_down_in + dot_tn(chunk_at(low_grad_down, k), hidden)
        grad_ffn_out = grad_ffn_out + dot_tn(ffn_in[k][:, model : model + 2 * rank], grads)
    back = sum_to_owners(back_parts, "tensor")
    low_grad_ffn = back[:, model : model + 2 * rank].astype(BF16)
    grad_normed_ffn = back[:, :model] + dot(low_grad_ffn, feedforward_in)
    grad_middle = cot_own.astype(F32) + rms_back(middle, feedforward_norm_gain, grad_normed_ffn)

    grad_attn = grad_middle.astype(BF16)
    low_grad_o = dot_nt(grad_attn, projection_out).astype(BF16)
    grad_blocks = blocks_of_others(
        jnp.concatenate([grad_attn, pad_columns(low_grad_o, LANES)], axis=1), "tensor"
    )
    grad_head = jnp.zeros((span, features), F32)
    grad_o_in = 0.0
    for k in range(owners):
        start = lax.rem(place + k, owners) * share
        grad_head = lax.dynamic_update_slice_in_dim(
            grad_head, dot(grad_blocks[k], out_ext), start, axis=0
        )
        grad_o_in = grad_o_in + dot_tn(
            grad_blocks[k][:, model : model + rank], chunk_at(head_low, k)
        )

    grad_attended, own = attend_back(grad_head, attended, qp, gain_row, heads, head_dim)
    own_three = shifted(own, "context", -3, wrap=False)
    own_two = shifted(own, "context", -2, wrap=False)
    own_one = shifted(own, "context", -1, wrap=False)

    down_sum = sum_to_owners([dot_nt(down_parts[k][0], down_ext) for k in range(owners)], "tensor")
    low_down = down_sum[:, model : model + rank].astype(BF16)
    block_own = (middle + down_sum[:, :model] + dot(low_down, down_out)).astype(BF16)
    block_parts = blocks_of_others(block_own, "tensor")

    def in_place(blocks, kind):
        whole = jnp.zeros((span, model), kind)
        for k in range(owners):
            start = lax.rem(place + k, owners) * share
            whole = lax.dynamic_update_slice_in_dim(whole, blocks[k].astype(kind), start, axis=0)
        return whole

    block_out = in_place(block_parts, BF16)

    def for_owner(items):
        parts = [
            lax.dynamic_index_in_dim(items, lax.rem(place + k, owners), 0, keepdims=False)
            for k in range(owners)
        ]
        return sum_to_owners(parts, "tensor")

    def gathered(block):
        block = paired_sum(block.astype(BF16), "context").astype(BF16)
        return lax.all_gather(block, ("weights", "tensor"), axis=0, tiled=False)

    shared_items = jnp.stack(
        [
            dot_tn(low_o, grad_attn),
            dot_tn(low_grad_ffn[:, :rank], normed_ffn),
            dot_tn(low_grad_ffn[:, rank:], normed_ffn),
            dot_tn(low_down, cot_own),
        ]
    )
    early = gathered(
        jnp.concatenate(
            [
                for_owner(shared_items),
                grad_o_in,
                grad_ffn_out[:rank, :hidden_units],
                grad_ffn_out[rank:, hidden_units:],
                grad_down_in,
            ],
            axis=1,
        )
    )

    grad_projected, halo, tail = delta_back(
        projected, kernels, seg_column, seg_rows, inverse, prefix, state, grad_attended,
        (own_one, own_two, own_three), (map_one, map_two), heads, head_dim, span, group,
    )
    returned = shifted(halo, "context", -1, wrap=False)
    grad_projected = lax.dynamic_update_slice(
        grad_projected, (tail + returned).astype(BF16), (span - HALO, 0)
    )

    low_part = dot_nt(grad_projected, low_in)
    low_grad_attn = paired_sum(low_part.astype(BF16), "tensor").astype(BF16)
    grad_low_in = dot_tn(low_attn, grad_projected)
    normed_sum = sum_to_owners(
        [dot_nt(chunk_at(grad_projected, k), weight_in) for k in range(owners)], "tensor"
    )
    grad_normed = normed_sum + dot(chunk_at(low_grad_attn, 0), attention_in)
    grad_tokens = grad_middle + rms_back(inputs_own, mixer_norm_gain, grad_normed)
    tokens_grad = in_place(blocks_of_others(grad_tokens.astype(BF16), "tensor"), F32)

    attn_items = dot_tn(low_grad_attn, normed)
    attn_item = lax.dynamic_slice_in_dim(attn_items, place * rank, rank, axis=0)
    late = gathered(
        jnp.concatenate(
            [attn_item]
            + [
                grad_low_in[part * rank : (part + 1) * rank, part * features : (part + 1) * features]
                for part in range(3)
            ]
            + [grad_low_in[3 * rank :, 3 * features :]],
            axis=1,
        )
    )

    indices = lax.all_gather(sequence_adapter_index, "weights", axis=0, tiled=True)
    onehot = (
        indices[:, None] == jnp.arange(adapters, dtype=jnp.int32)[None, :]
    ).astype(BF16)
    sequences = indices.shape[0]

    def totals(terms):
        return lax.dot_general(
            onehot, terms, (((0,), (0,)), ((), ())), preferred_element_type=F32
        )

    early = early.reshape(sequences, owners, rank, -1)
    late = late.reshape(sequences, owners, rank, -1)
    early_own = lax.dynamic_index_in_dim(early, place, 1, keepdims=False)
    late_own = lax.dynamic_index_in_dim(late, place, 1, keepdims=False)
    cuts = [model, model + features, model + features + hidden_units,
            model + features + 2 * hidden_units, model + features + 3 * hidden_units]
    flip = lambda array: jnp.swapaxes(array, -1, -2)
    grad_attn_in = jnp.stack([flip(totals(late[:, p, :, :model])) for p in range(4)])
    grad_qkv_out = jnp.stack(
        [
            totals(late_own[:, :, model + p * features : model + (p + 1) * features])
            for p in range(3)
        ]
    )
    grad_beta_out = totals(late_own[:, :, model + 3 * features :])[:, :, :heads]
    grad_o_out = totals(early[:, 0, :, :model])
    grad_ffn_in = jnp.stack([flip(totals(early[:, p, :, :model])) for p in (1, 2)])
    grad_down_out = totals(early[:, 3, :, :model])
    grad_o_in_out = flip(totals(early_own[:, :, cuts[0] : cuts[1]]))
    grad_ffn_out_out = jnp.stack(
        [
            totals(early_own[:, :, cuts[1] : cuts[2]]),
            totals(early_own[:, :, cuts[2] : cuts[3]]),
        ]
    )
    grad_down_in_out = flip(totals(early_own[:, :, cuts[3] : cuts[4]]))
    return (
        block_out,
        tokens_grad,
        grad_attn_in,
        grad_qkv_out,
        grad_beta_out,
        grad_o_in_out,
        grad_o_out,
        grad_ffn_in,
        grad_ffn_out_out,
        grad_down_in_out,
        grad_down_out,
    )


def solution(mesh):
    rows = P(("weights", "context"), None)
    return jax.shard_map(
        on_device,
        mesh=mesh,
        in_specs=(
            rows,
            rows,
            P("weights", None),
            P("weights"),
            P(),
            P(),
            P(),
            P(None, None, "tensor"),
            P(("weights", "context"), "tensor"),
            P(("weights", "context"), "tensor"),
            P(("weights", "context"), "tensor"),
            P(("weights", "context"), "tensor"),
            P("tensor", ("weights", "context")),
            P(("weights", "context"), "tensor"),
            P(("weights", "context"), "tensor"),
            P("tensor", ("weights", "context")),
            P(),
            P(None, None, None, "tensor"),
            P(None, None, "tensor"),
            P(None, "tensor", None),
            P(),
            P(),
            P(None, None, None, "tensor"),
            P(None, "tensor", None),
            P(),
        ),
        out_specs=(
            rows,
            rows,
            P(),
            P(None, None, None, "tensor"),
            P(None, None, "tensor"),
            P(None, "tensor", None),
            P(),
            P(),
            P(None, None, None, "tensor"),
            P(None, "tensor", None),
            P(),
        ),
        check_vma=False,
    )
```

```python
import functools

import jax
import jax.numpy as jnp
from jax import lax
from jax.experimental import pallas as pl
from jax.experimental.pallas import tpu as pltpu
from jax.sharding import PartitionSpec as P

EPSILON = 1e-06
HALO = 8
CHUNK = 128
LANES = 128
F32 = jnp.float32
BF16 = jnp.bfloat16
MIB = 1024 * 1024


def dot_low(left, right, left_dim=1, right_dim=0):
    return lax.dot_general(
        left.astype(BF16),
        right.astype(BF16),
        (((left_dim,), (right_dim,)), ((), ())),
        preferred_element_type=F32,
    )


def conv_rows(x_ref, columns, taps_ref, seg_ref, span):
    here = seg_ref[HALO : HALO + span, :]
    total = taps_ref[0:1, columns] * x_ref[HALO : HALO + span, columns]
    for tap in range(1, taps_ref.shape[0]):
        same = seg_ref[HALO - tap : HALO - tap + span, :] == here
        total = total + taps_ref[tap : tap + 1, columns] * jnp.where(
            same, x_ref[HALO - tap : HALO - tap + span, columns], 0.0
        )
    return total


def inverse_norm(values):
    return lax.rsqrt(jnp.sum(values * values, axis=-1, keepdims=True) + EPSILON)


def head_column(array, head):
    lane = lax.broadcasted_iota(jnp.int32, array.shape, 1)
    return jnp.sum(jnp.where(lane == head, array, 0.0), axis=1, keepdims=True)


def chunk_masks(seg_ref, row_ref, chunk):
    start = HALO + chunk * CHUNK
    column = seg_ref[start : start + CHUNK, :]
    row = row_ref[chunk : chunk + 1, :]
    before = seg_ref[start - 1 : start, :]
    last = seg_ref[start + CHUNK - 1 : start + CHUNK, :]
    same = column == row
    row_ids = lax.broadcasted_iota(jnp.int32, (CHUNK, CHUNK), 0)
    col_ids = lax.broadcasted_iota(jnp.int32, (CHUNK, CHUNK), 1)
    strict = (same & (row_ids > col_ids)).astype(F32)
    causal = (same & (row_ids >= col_ids)).astype(F32)
    running = (column == before).astype(F32)
    closing = (column == last).astype(F32)
    carried = (before == last).astype(F32)
    return strict, causal, running, closing, carried


def unit_lower_inverses(lowers):
    size = lowers[0].shape[0]
    row_ids = lax.broadcasted_iota(jnp.int32, (size, size), 0)
    col_ids = lax.broadcasted_iota(jnp.int32, (size, size), 1)
    identity = (row_ids == col_ids).astype(F32)
    pair = (row_ids >> 1) == (col_ids >> 1)
    highs = [lower.astype(BF16) for lower in lowers]
    inverses = [identity - jnp.where(pair, lower, 0.0) for lower in lowers]
    bits = 2
    while (1 << bits) <= size:
        joined = ((row_ids >> bits) == (col_ids >> bits)) & (
            (row_ids >> (bits - 1)) != (col_ids >> (bits - 1))
        )
        rounded = [inverse.astype(BF16) for inverse in inverses]
        inner = [
            dot_low(jnp.where(joined, high, jnp.zeros_like(high)), inverse)
            for high, inverse in zip(highs, rounded)
        ]
        inverses = [
            inverse - dot_low(low, part) for inverse, low, part in zip(inverses, rounded, inner)
        ]
        bits += 1
    rounded = [inverse.astype(BF16) for inverse in inverses]
    rests = [(lower - high.astype(F32)).astype(BF16) for lower, high in zip(lowers, highs)]
    residuals = [
        identity - low.astype(F32) - (dot_low(high, low) + dot_low(rest, low))
        for low, high, rest in zip(rounded, highs, rests)
    ]
    return [low.astype(F32) + dot_low(low, part) for low, part in zip(rounded, residuals)]


def delta_local_kernel(
    q_ref, k_ref, v_ref, logit_ref, taps_q, taps_k, taps_v, seg_ref, row_ref,
    qp_ref, op_ref, offset_ref, linear_ref, inverse_ref, prefix_ref, solved_ref, score_ref, zq_ref, zk_ref, zv_ref,
    *, span, head_dim, group,
):
    chunks = span // CHUNK
    step = pl.program_id(0)
    masks = [chunk_masks(seg_ref, row_ref, chunk) for chunk in range(chunks)]
    rates_all = jax.nn.sigmoid(logit_ref[HALO : HALO + span, :])
    work = []
    for local in range(group):
        columns = slice(local * head_dim, (local + 1) * head_dim)
        zq_ref[:, columns] = conv_rows(q_ref, columns, taps_q, seg_ref, span)
        zk_ref[:, columns] = conv_rows(k_ref, columns, taps_k, seg_ref, span)
        zv_ref[:, columns] = conv_rows(v_ref, columns, taps_v, seg_ref, span)
        rates_head = head_column(rates_all, step * group + local)
        for chunk in range(chunks):
            rows = slice(chunk * CHUNK, (chunk + 1) * CHUNK)
            queries = jax.nn.silu(zq_ref[rows, columns])
            queries = (queries * (inverse_norm(queries) * head_dim**-0.5)).astype(BF16)
            keys = jax.nn.silu(zk_ref[rows, columns])
            keys = (keys * inverse_norm(keys)).astype(BF16)
            values = jax.nn.silu(zv_ref[rows, columns]).astype(BF16)
            work.append((local, chunk, queries, keys, values, rates_head[rows]))
    lowers = [
        dot_low(keys, keys, 1, 1) * (rates * masks[chunk][0])
        for _, chunk, _, keys, _, rates in work
    ]
    inverses = unit_lower_inverses(lowers)
    parts = []
    for (local, chunk, queries, keys, values, rates), inverse in zip(work, inverses):
        rows = slice(chunk * CHUNK, (chunk + 1) * CHUNK)
        strict, causal, running, closing, carried = masks[chunk]
        inverse = inverse.astype(BF16)
        inverse_ref[local, rows, :] = inverse
        right = jnp.concatenate([rates * values.astype(F32), rates * keys.astype(F32)], axis=1)
        solved = dot_low(inverse, right)
        solved_ref[local, rows, :] = solved.astype(BF16)
        updates = solved[:, :head_dim]
        weighted = running * solved[:, head_dim:]
        both = jnp.concatenate([updates, weighted], axis=1).astype(BF16)
        scores = (dot_low(queries, keys, 1, 1) * causal).astype(BF16)
        score_ref[local, rows, :] = scores
        near = dot_low(scores, both)
        ends = dot_low(closing * keys.astype(F32), both, 0, 0)
        reach = running * queries.astype(F32) - near[:, head_dim:]
        parts.append((near[:, :head_dim], reach.astype(BF16), ends))
    row_ids = lax.broadcasted_iota(jnp.int32, (head_dim, head_dim), 0)
    col_ids = lax.broadcasted_iota(jnp.int32, (head_dim, head_dim), 1)
    identity = (row_ids == col_ids).astype(F32)
    start = jnp.concatenate([jnp.zeros((head_dim, head_dim), F32), identity], axis=1)
    prefixes = [start] * group
    for chunk in range(chunks):
        rows = slice(chunk * CHUNK, (chunk + 1) * CHUNK)
        carried = masks[chunk][4]
        for local in range(group):
            columns = slice(local * head_dim, (local + 1) * head_dim)
            near, reach, ends = parts[local * chunks + chunk]
            prefix = prefixes[local]
            prefix_ref[local, chunk * head_dim : (chunk + 1) * head_dim, :] = prefix.astype(BF16)
            seen = dot_low(reach, prefix)
            op_ref[rows, columns] = near + seen[:, :head_dim]
            qp_ref[rows, columns] = seen[:, head_dim:].astype(BF16)
            moved = jnp.concatenate([carried, carried], axis=1) * prefix - dot_low(
                ends[:, head_dim:], prefix
            )
            prefixes[local] = jnp.concatenate(
                [moved[:, :head_dim] + ends[:, :head_dim], moved[:, head_dim:]], axis=1
            )
    for local in range(group):
        offset_ref[local] = prefixes[local][:, :head_dim].astype(BF16)
        linear_ref[local] = prefixes[local][:, head_dim:].astype(BF16)


def delta_local(projected, taps, seg_column, seg_rows, heads, head_dim, span, group):
    rows = projected.shape[0]
    width = group * head_dim
    steps = heads // group
    third = lambda part: pl.BlockSpec((rows, width), lambda i: (0, part * steps + i))
    tap_third = lambda part: pl.BlockSpec((taps.shape[0], width), lambda i: (0, part * steps + i))
    whole = lambda array: pl.BlockSpec(array.shape, lambda i: (0,) * array.ndim)
    by_head = lambda *shape: pl.BlockSpec((group,) + shape, lambda i: (i, 0, 0))
    columns = pl.BlockSpec((span, width), lambda i: (0, i))
    chunks = span // CHUNK
    kept = lambda *shape, kind=BF16: jax.ShapeDtypeStruct(shape, kind)
    return pl.pallas_call(
        functools.partial(delta_local_kernel, span=span, head_dim=head_dim, group=group),
        grid=(steps,),
        in_specs=[
            third(0), third(1), third(2),
            pl.BlockSpec((rows, LANES), lambda i: (0, 3 * heads * head_dim // LANES)),
            tap_third(0), tap_third(1), tap_third(2), whole(seg_column), whole(seg_rows),
        ],
        out_specs=[
            columns, columns, by_head(head_dim, head_dim), by_head(head_dim, head_dim),
            by_head(span, CHUNK),
            by_head(chunks * head_dim, 2 * head_dim), by_head(span, 2 * head_dim),
            by_head(span, CHUNK), columns, columns, columns,
        ],
        out_shape=[
            kept(span, heads * head_dim),
            kept(span, heads * head_dim, kind=F32),
            kept(heads, head_dim, head_dim),
            kept(heads, head_dim, head_dim),
            kept(heads, span, CHUNK),
            kept(heads, chunks * head_dim, 2 * head_dim),
            kept(heads, span, 2 * head_dim),
            kept(heads, span, CHUNK),
            kept(span, heads * head_dim, kind=F32),
            kept(span, heads * head_dim, kind=F32),
            kept(span, heads * head_dim, kind=F32),
        ],
        compiler_params=pltpu.CompilerParams(vmem_limit_bytes=22 * MIB),
        name="delta_local",
    )(projected, projected, projected, projected, taps, taps, taps, seg_column, seg_rows)


def attend_kernel(
    position_ref, place_ref, op_ref, qp_ref, one_ref, two_ref, map_ref, three_ref, gain_ref, weight_ref,
    out_ref, att_ref, state_ref, *part_refs,
):
    heads, head_dim = one_ref.shape[0], one_ref.shape[1]
    owners = len(part_refs)
    share = out_ref.shape[0] // owners
    for head in range(heads):
        columns = slice(head * head_dim, (head + 1) * head_dim)
        through = one_ref[head].astype(F32) + dot_low(map_ref[head], three_ref[head])
        state = jnp.where(position_ref[0] == 2, two_ref[head].astype(F32), through)
        state_ref[head] = state.astype(BF16)
        attended = op_ref[:, columns] + dot_low(qp_ref[:, columns], state)
        att_ref[:, columns] = attended
        scale = lax.rsqrt(jnp.mean(attended * attended, axis=-1, keepdims=True) + EPSILON)
        out_ref[:, columns] = (attended * scale * gain_ref[...]).astype(BF16)
    for k, part_ref in enumerate(part_refs):
        start = lax.rem(place_ref[0] + k, owners) * share
        rows = out_ref[pl.ds(pl.multiple_of(start, share), share), :]
        part_ref[...] = dot_low(rows, weight_ref[...], 1, 1).astype(BF16)


def attend(position, place, op, qp, one, two, mapped, three, gain, weight, owners):
    vmem = pl.BlockSpec(memory_space=pltpu.VMEM)
    smem = pl.BlockSpec(memory_space=pltpu.SMEM)
    part = jax.ShapeDtypeStruct((op.shape[0] // owners, weight.shape[0]), BF16)
    return pl.pallas_call(
        attend_kernel,
        in_specs=[smem] * 2 + [vmem] * 8,
        out_specs=[vmem] * (3 + owners),
        out_shape=[
            jax.ShapeDtypeStruct(op.shape, BF16),
            jax.ShapeDtypeStruct(op.shape, F32),
            jax.ShapeDtypeStruct(one.shape, BF16),
        ]
        + [part] * owners,
        compiler_params=pltpu.CompilerParams(vmem_limit_bytes=14 * MIB),
        name="attend",
    )(position, place, op, qp, one, two, mapped, three, gain, weight)


def attend_back_kernel(
    place_ref, att_ref, qp_ref, gain_ref, weight_ref, *refs
):
    *block_refs, out_ref, own_ref, grad_ref = refs
    heads, head_dim = own_ref.shape[0], own_ref.shape[1]
    owners = len(block_refs)
    share = out_ref.shape[0] // owners
    for k, block_ref in enumerate(block_refs):
        start = lax.rem(place_ref[0] + k, owners) * share
        grad_ref[pl.ds(pl.multiple_of(start, share), share), :] = dot_low(
            block_ref[...], weight_ref[...]
        )
    for head in range(heads):
        columns = slice(head * head_dim, (head + 1) * head_dim)
        attended = att_ref[:, columns]
        scale = lax.rsqrt(jnp.mean(attended * attended, axis=-1, keepdims=True) + EPSILON)
        gained = grad_ref[:, columns] * gain_ref[...]
        along = jnp.mean(attended * gained, axis=-1, keepdims=True)
        grad = (scale * gained - attended * (scale * scale * scale * along)).astype(BF16)
        out_ref[:, columns] = grad
        own_ref[head] = dot_low(qp_ref[:, columns], grad, 0, 0).astype(BF16)


def attend_back(place, attended, qp, gain, weight, blocks, heads, head_dim):
    vmem = pl.BlockSpec(memory_space=pltpu.VMEM)
    return pl.pallas_call(
        attend_back_kernel,
        in_specs=[pl.BlockSpec(memory_space=pltpu.SMEM)] + [vmem] * (4 + len(blocks)),
        out_specs=[vmem] * 2,
        out_shape=[
            jax.ShapeDtypeStruct(attended.shape, BF16),
            jax.ShapeDtypeStruct((heads, head_dim, head_dim), BF16),
        ],
        scratch_shapes=[pltpu.VMEM(attended.shape, F32)],
        compiler_params=pltpu.CompilerParams(vmem_limit_bytes=14 * MIB),
        name="attend_back",
    )(place, attended, qp, gain, weight, *blocks)


def delta_back_kernel(
    zq_ref, zk_ref, zv_ref, logit_ref, taps_q, taps_k, taps_v, seg_ref, row_ref,
    inverse_ref, prefix_ref, solved_ref, score_ref, state_ref, grad_ref,
    place_ref, one_ref, two_ref, map_ref, three_ref,
    out_ref, halo_ref, tail_ref, dz_ref, *, span, heads, head_dim, group,
):
    chunks = span // CHUNK
    step = pl.program_id(0)
    features = heads * head_dim
    masks = [chunk_masks(seg_ref, row_ref, chunk) for chunk in range(chunks)]
    rates_all = jax.nn.sigmoid(logit_ref[HALO : HALO + span, :])
    lane = lax.broadcasted_iota(jnp.int32, (CHUNK, LANES), 1)

    @pl.when(step == 0)
    def _():
        out_ref[:, 3 * features :] = jnp.zeros((span, LANES), BF16)
        for slot in range(3 * group):
            dz_ref[slot, 0:HALO, :] = jnp.zeros((HALO, head_dim), F32)
            dz_ref[slot, HALO + span :, :] = jnp.zeros((HALO, head_dim), F32)

    kept, leavings = [], []
    for local in range(group):
        columns = slice(local * head_dim, (local + 1) * head_dim)
        rates_head = head_column(rates_all, step * group + local)
        entry = state_ref[local]
        through = one_ref[local].astype(F32) + dot_low(map_ref[local], three_ref[local], 0, 0)
        leavings.append(jnp.where(place_ref[0] == 1, two_ref[local].astype(F32), through))
        for chunk in range(chunks):
            rows = slice(chunk * CHUNK, (chunk + 1) * CHUNK)
            strict, causal, running, closing, carried = masks[chunk]
            queries = jax.nn.silu(zq_ref[rows, columns])
            scale_q = inverse_norm(queries)
            queries = queries * scale_q
            keys = jax.nn.silu(zk_ref[rows, columns])
            scale_k = inverse_norm(keys)
            keys = keys * scale_k
            low_q = (queries * head_dim**-0.5).astype(BF16)
            low_k = keys.astype(BF16)
            values = jax.nn.silu(zv_ref[rows, columns])
            solved = solved_ref[local, rows, :].astype(F32)
            weighted = (running * solved[:, head_dim:]).astype(BF16)
            prefix = prefix_ref[local, chunk * head_dim : (chunk + 1) * head_dim, :]
            state = (
                prefix[:, :head_dim].astype(F32) + dot_low(prefix[:, head_dim:], entry)
            ).astype(BF16)
            errors = (solved[:, :head_dim] - dot_low(weighted, state)).astype(BF16)
            scores = score_ref[local, rows, :]
            grad = grad_ref[rows, columns]
            near = dot_low(scores, grad, 0, 0)
            far = dot_low(running * low_q.astype(F32), grad, 0, 0)
            grad_scores = (dot_low(grad, errors, 1, 1) * causal).astype(BF16)
            kept.append((queries, scale_q, keys, scale_k, low_q, low_k, values,
                         rates_head[rows], weighted, state, errors, near, far, grad_scores))
    grad_errors_all = [None] * (group * chunks)
    leaving_all = [None] * (group * chunks)
    for chunk in reversed(range(chunks)):
        strict, causal, running, closing, carried = masks[chunk]
        for local in range(group):
            item = local * chunks + chunk
            low_k, weighted, near, far = (kept[item][i] for i in (5, 8, 11, 12))
            leaving = leavings[local]
            low_leaving = leaving.astype(BF16)
            leaving_all[item] = low_leaving
            grad_errors = near + closing * dot_low(low_k, low_leaving)
            grad_errors_all[item] = grad_errors.astype(BF16)
            leavings[local] = (
                carried * leaving + far - dot_low(weighted, grad_errors_all[item], 0, 0)
            )
    for local in range(group):
        columns = slice(local * head_dim, (local + 1) * head_dim)
        head = step * group + local
        for chunk in range(chunks):
            rows = slice(chunk * CHUNK, (chunk + 1) * CHUNK)
            inner = slice(HALO + chunk * CHUNK, HALO + (chunk + 1) * CHUNK)
            strict, causal, running, closing, carried = masks[chunk]
            item = local * chunks + chunk
            (queries, scale_q, keys, scale_k, low_q, low_k, values, rates, weighted, state,
             errors, near, far, grad_scores) = kept[item]
            grad_errors, leaving = grad_errors_all[item], leaving_all[item]
            grad = grad_ref[rows, columns]
            grad_queries = running * dot_low(grad, state, 1, 1) + dot_low(grad_scores, low_k)
            grad_keys = dot_low(grad_scores, low_q, 0, 0) + closing * dot_low(
                errors, leaving, 1, 1
            )
            grad_weighted = -running * dot_low(grad_errors, state, 1, 1)
            grad_right = dot_low(
                inverse_ref[local, rows, :],
                jnp.concatenate([grad_errors, grad_weighted.astype(BF16)], axis=1), 0, 0,
            )
            right_v, right_k = grad_right[:, :head_dim], grad_right[:, head_dim:]
            grad_lower = -dot_low(grad_right, solved_ref[local, rows, :], 1, 1) * strict
            gram = dot_low(low_k, low_k, 1, 1)
            grad_rates = jnp.sum(
                right_v * values + right_k * keys + grad_lower * gram, axis=1, keepdims=True
            )
            grad_gram = (rates * grad_lower).astype(BF16)
            grad_keys = (
                grad_keys
                + rates * right_k
                + dot_low(grad_gram, low_k)
                + dot_low(grad_gram, low_k, 0, 0)
            )
            grad_logit = grad_rates * rates * (1.0 - rates)
            previous = out_ref[rows, 3 * features :].astype(F32)
            out_ref[rows, 3 * features :] = jnp.where(lane == head, grad_logit, previous).astype(BF16)
            grad_queries = grad_queries * head_dim**-0.5
            grad_queries = scale_q * (
                grad_queries - queries * jnp.sum(queries * grad_queries, axis=-1, keepdims=True)
            )
            grad_keys = scale_k * (
                grad_keys - keys * jnp.sum(keys * grad_keys, axis=-1, keepdims=True)
            )
            for part, (z_ref, grad_part) in enumerate(
                ((zq_ref, grad_queries), (zk_ref, grad_keys), (zv_ref, rates * right_v))
            ):
                conv = z_ref[rows, columns]
                sig = jax.nn.sigmoid(conv)
                dz_ref[local * 3 + part, inner, :] = grad_part * (
                    sig * (1.0 + conv * (1.0 - sig))
                )
        here = seg_ref[0 : HALO + span, :]
        for part, taps in enumerate((taps_q, taps_k, taps_v)):
            slot = local * 3 + part
            total = taps[0:1, columns] * dz_ref[slot, 0 : HALO + span, :]
            for tap in range(1, taps.shape[0]):
                same = seg_ref[tap : tap + HALO + span, :] == here
                total = total + taps[tap : tap + 1, columns] * jnp.where(
                    same, dz_ref[slot, tap : tap + HALO + span, :], 0.0
                )
            place = pl.ds(pl.multiple_of(part * features + head * head_dim, LANES), head_dim)
            halo_ref[:, place] = total[:HALO]
            tail_ref[:, place] = total[span:]
            out_ref[:, place] = total[HALO:].astype(BF16)


def delta_back(
    projected, taps, seg_column, seg_rows, kept, state, grad, position, arrived, heads, head_dim, span,
    group,
):
    inverse, prefix, solved, scores, conv_q, conv_k, conv_v = kept
    rows = projected.shape[0]
    width = group * head_dim
    steps = heads // group
    columns = pl.BlockSpec((span, width), lambda i: (0, i))
    tap_third = lambda part: pl.BlockSpec((taps.shape[0], width), lambda i: (0, part * steps + i))
    whole = lambda array: pl.BlockSpec(array.shape, lambda i: (0,) * array.ndim)
    by_head = lambda array: pl.BlockSpec((group,) + array.shape[1:], lambda i: (i, 0, 0))
    total = 3 * heads * head_dim
    return pl.pallas_call(
        functools.partial(
            delta_back_kernel, span=span, heads=heads, head_dim=head_dim, group=group
        ),
        grid=(steps,),
        in_specs=[
            columns, columns, columns,
            pl.BlockSpec((rows, LANES), lambda i: (0, total // LANES)),
            tap_third(0), tap_third(1), tap_third(2), whole(seg_column), whole(seg_rows),
            by_head(inverse), by_head(prefix), by_head(solved), by_head(scores), by_head(state),
            columns, pl.BlockSpec(memory_space=pltpu.SMEM), *[by_head(array) for array in arrived],
        ],
        out_specs=[
            pl.BlockSpec((span, total + LANES), lambda i: (0, 0)),
            pl.BlockSpec((HALO, total), lambda i: (0, 0)),
            pl.BlockSpec((HALO, total), lambda i: (0, 0)),
        ],
        out_shape=[
            jax.ShapeDtypeStruct((span, total + LANES), BF16),
            jax.ShapeDtypeStruct((HALO, total), F32),
            jax.ShapeDtypeStruct((HALO, total), F32),
        ],
        scratch_shapes=[pltpu.VMEM((3 * group, span + 2 * HALO, head_dim), F32)],
        compiler_params=pltpu.CompilerParams(vmem_limit_bytes=24 * MIB),
        name="delta_back",
    )(
        conv_q, conv_k, conv_v, projected, taps, taps, taps, seg_column, seg_rows,
        inverse, prefix, solved, scores, state, grad, position, *arrived,
    )


def normed_grad(values, gain, grad):
    scale = lax.rsqrt(jnp.mean(values * values, axis=-1, keepdims=True) + EPSILON)
    gained = gain * grad
    along = jnp.mean(values * gained, axis=-1, keepdims=True)
    return scale * gained - values * (scale * scale * scale * along)


def added(refs, columns):
    total = refs[0][:, columns].astype(F32)
    for ref in refs[1:]:
        total = total + ref[:, columns].astype(F32)
    return total


def middle_kernel(
    place_ref, own_ref, one_ref, two_ref, three_ref, tokens_ref, out_map_ref, gain_ref, in_map_ref,
    middle_ref, packed_ref, low_ref,
):
    model = tokens_ref.shape[1]
    refs = (own_ref, one_ref, two_ref, three_ref)
    low = added(refs, slice(model, model + LANES)).astype(BF16)
    low_ref[...] = low
    middle = (
        tokens_ref[...].astype(F32)
        + added(refs, slice(0, model))
        + dot_low(low, out_map_ref[...])
    )
    middle_ref[...] = middle
    scale = lax.rsqrt(jnp.mean(middle * middle, axis=-1, keepdims=True) + EPSILON)
    normed = (middle * scale * gain_ref[...]).astype(BF16)
    packed_ref[:, :model] = normed
    packed_ref[:, model:] = dot_low(normed, in_map_ref[...], 1, 1).astype(BF16)


def back_kernel(
    place_ref, own_ref, one_ref, two_ref, three_ref, cot_ref, middle_in, gain_ref, in_map_ref,
    out_map_ref, low_ref, grad_ref, packed_ref, *, rank,
):
    model = cot_ref.shape[1]
    refs = (own_ref, one_ref, two_ref, three_ref)
    low_ffn = added(refs, slice(model, model + LANES)).astype(BF16)
    grad = added(refs, slice(0, model)) + dot_low(low_ffn, in_map_ref[...])
    grad = cot_ref[...].astype(F32) + normed_grad(middle_in[...], gain_ref[...], grad)
    grad_ref[...] = grad
    rounded = grad.astype(BF16)
    packed_ref[:, :model] = rounded
    low_out = dot_low(rounded, out_map_ref[...], 1, 1).astype(BF16).astype(F32)
    packed_ref[:, model:] = (
        low_out
        + pltpu.roll(low_ref[...].astype(F32), rank, 1)
        + pltpu.roll(low_ffn.astype(F32), 2 * rank, 1)
    ).astype(BF16)


def tokens_kernel(
    place_ref, own_ref, one_ref, two_ref, three_ref, low_ref, in_map_ref, tokens_ref, gain_ref,
    grad_ref, out_ref,
):
    refs = (own_ref, one_ref, two_ref, three_ref)
    grad = added(refs, slice(None)) + dot_low(low_ref[...], in_map_ref[...])
    out_ref[...] = (
        grad_ref[...] + normed_grad(tokens_ref[...].astype(F32), gain_ref[...], grad)
    ).astype(BF16)


def owner_call(kernel, name, place, share, arrays, outs, strips=2):
    strip = share // strips

    def spec(array, mark):
        if mark == "rows":
            return pl.BlockSpec((strip, array.shape[1]), lambda i, c: (i, 0))
        if mark == "span":
            return pl.BlockSpec((strip, array.shape[1]), lambda i, c: (c[0] * strips + i, 0))
        return pl.BlockSpec(array.shape, lambda i, c: (0, 0))

    return pl.pallas_call(
        kernel,
        grid_spec=pltpu.PrefetchScalarGridSpec(
            num_scalar_prefetch=1,
            grid=(strips,),
            in_specs=[spec(array, mark) for array, mark in arrays],
            out_specs=[pl.BlockSpec((strip, shape[1]), lambda i, c: (i, 0)) for shape, _ in outs],
        ),
        out_shape=[jax.ShapeDtypeStruct(shape, kind) for shape, kind in outs],
        compiler_params=pltpu.CompilerParams(vmem_limit_bytes=56 * MIB),
        name=name,
    )(place, *[array for array, _ in arrays])


def early_kernel(
    place_ref, g0, g1, g2, g3, x0, x1, x2, x3, head_ref, low_down_ref, cot_ref,
    out_one, out_two, down_one, down_two, *refs, rank,
):
    (pack_ref,) = refs
    model = cot_ref.shape[1]
    hidden_units = down_one.shape[1]
    owners, share = 4, g0.shape[0]
    through_g, through_x, through_h = 0.0, 0.0, 0.0
    for k, (g_ref, x_ref) in enumerate(zip((g0, g1, g2, g3), (x0, x1, x2, x3))):
        low = g_ref[:, model:]
        start = lax.rem(place_ref[0] + k, owners) * share
        heads = head_ref[pl.ds(pl.multiple_of(start, share), share), :]
        through_g = through_g + dot_low(low, g_ref[:, :model], 0, 0)
        through_x = through_x + dot_low(low, x_ref[:, :model], 0, 0)
        through_h = through_h + dot_low(low, heads, 0, 0)
    out_terms = out_one[...] + out_two[...]
    pack_ref[0, :, :model] = through_x[2 * rank : 3 * rank].astype(BF16)
    pack_ref[0, :, model:] = out_terms[:rank, :hidden_units].astype(BF16)
    pack_ref[1, :, :model] = through_x[3 * rank : 4 * rank].astype(BF16)
    pack_ref[1, :, model:] = out_terms[rank:, hidden_units:].astype(BF16)
    pack_ref[2, :, :model] = dot_low(low_down_ref[...], cot_ref[...]).astype(BF16)
    pack_ref[2, :, model:] = (down_one[...] + down_two[...]).astype(BF16)
    pack_ref[3, :, :model] = through_g[rank : 2 * rank].astype(BF16)
    pack_ref[3, :, model:] = jnp.zeros((rank, hidden_units), BF16)
    pack_ref[3, :, model : model + through_h.shape[1]] = through_h[:rank].astype(BF16)


def late_kernel(
    position_ref, p0, p1, p2, p3, normed_ref, low_ref, grad_ref, early_ref, low_out_ref, *refs, rank
):
    *out_refs, pack_ref = refs
    model = normed_ref.shape[1]
    features = (grad_ref.shape[1] - LANES) // 3
    total = (p0[...].astype(F32) + p2[...].astype(F32)) + (
        p1[...].astype(F32) + p3[...].astype(F32)
    )
    low_grad = total.astype(BF16)
    low_out_ref[...] = low_grad
    items = dot_low(low_grad, normed_ref[...], 0, 0)
    blocks = dot_low(low_ref[...], grad_ref[...], 0, 0)
    for part in range(4):
        rows = slice(part * rank, (part + 1) * rank)
        pack_ref[part, :, :model] = items[rows].astype(BF16)
        if part < 3:
            pack_ref[part, :, model:] = blocks[rows, part * features : (part + 1) * features].astype(BF16)
        else:
            pack_ref[part, :, model:] = jnp.zeros((rank, features), BF16)
            pack_ref[part, :, model : model + LANES] = blocks[rows, 3 * features :].astype(BF16)
    early_width = early_ref.shape[2]
    for k, out_ref in enumerate(out_refs):
        quarter = lax.rem(position_ref[0] + k, 4)
        out_ref[:, :early_width] = early_ref[quarter]
        out_ref[:, early_width:] = pack_ref[quarter]


def span_call(kernel, name, scalars, arrays, outs, scratch, limit):
    vmem = pl.BlockSpec(memory_space=pltpu.VMEM)
    return pl.pallas_call(
        kernel,
        in_specs=[pl.BlockSpec(memory_space=pltpu.SMEM)] * len(scalars) + [vmem] * len(arrays),
        out_specs=[vmem] * len(outs),
        out_shape=[jax.ShapeDtypeStruct(shape, kind) for shape, kind in outs],
        scratch_shapes=scratch,
        compiler_params=pltpu.CompilerParams(vmem_limit_bytes=limit * MIB),
        name=name,
    )(*scalars, *arrays)


def ffn_kernel(
    place_ref, x_first, x_second, weight_ref, low_ref, grad_ref, down_ref,
    hidden_ref, back_first, back_second, out_low_ref, down_low_ref, *, strip,
):
    share = x_first.shape[0]
    model, hidden_units = weight_ref.shape[0], weight_ref.shape[1] // 2
    rows = jnp.concatenate([x_first[...], x_second[...]], axis=0)

    def theirs(ref):
        parts = [
            ref[pl.ds(pl.multiple_of(place_ref[i] * share, share), share), :] for i in range(2)
        ]
        return jnp.concatenate(parts, axis=0)

    both = dot_low(rows[:, model:], low_ref[...]) + dot_low(rows[:, :model], weight_ref[...])
    gate, up = both[:, :hidden_units], both[:, hidden_units:]
    sig = jax.nn.sigmoid(gate)
    silu = gate * sig
    hidden = (silu * up).astype(BF16)
    hidden_ref[...] = hidden
    grad = theirs(grad_ref)
    grads = jnp.concatenate(
        [
            (grad * up * (sig * (1.0 + gate * (1.0 - sig)))).astype(BF16),
            (grad * silu).astype(BF16),
        ],
        axis=1,
    )
    for start in range(0, model, strip):
        back = dot_low(grads, weight_ref[start : start + strip, :], 1, 1)
        back_first[:, start : start + strip] = back[:share].astype(back_first.dtype)
        back_second[:, start : start + strip] = back[share:].astype(back_second.dtype)
    back = dot_low(grads, low_ref[...], 1, 1)
    back_first[:, model:] = back[:share].astype(back_first.dtype)
    back_second[:, model:] = back[share:].astype(back_second.dtype)
    out_low_ref[...] = dot_low(rows[:, model:], grads, 0, 0)[: out_low_ref.shape[0]]
    down_low_ref[...] = dot_low(theirs(down_ref), hidden, 0, 0)[: down_low_ref.shape[0]]


def ffn_rows(chunks, first, second, weights, low, grad_hidden, low_grad_down, rank, kinds):
    share, wide = first.shape
    hidden_units = grad_hidden.shape[1]
    vmem = pl.BlockSpec(memory_space=pltpu.VMEM)
    return pl.pallas_call(
        functools.partial(ffn_kernel, strip=512),
        in_specs=[pl.BlockSpec(memory_space=pltpu.SMEM)] + [vmem] * 6,
        out_specs=[vmem] * 5,
        out_shape=[
            jax.ShapeDtypeStruct((2 * share, hidden_units), BF16),
            jax.ShapeDtypeStruct((share, wide), kinds[0]),
            jax.ShapeDtypeStruct((share, wide), kinds[1]),
            jax.ShapeDtypeStruct((2 * rank, 2 * hidden_units), F32),
            jax.ShapeDtypeStruct((rank, hidden_units), F32),
        ],
        cost_estimate=pl.CostEstimate(
            flops=16 * share * wide * hidden_units,
            bytes_accessed=4 * wide * hidden_units,
            transcendentals=2 * share * hidden_units,
        ),
        compiler_params=pltpu.CompilerParams(vmem_limit_bytes=14 * MIB),
        name="ffn_rows",
    )(chunks, first, second, weights, low, grad_hidden, low_grad_down)


def in_place_kernel(place_ref, *refs):
    out_ref = refs[-1]
    for k, block_ref in enumerate(refs[:-1]):

        @pl.when(pl.program_id(0) == k)
        def _():
            out_ref[...] = block_ref[...].astype(out_ref.dtype)


def in_place(place, blocks, width, kind):
    owners, share = len(blocks), blocks[0].shape[0]
    return pl.pallas_call(
        in_place_kernel,
        grid_spec=pltpu.PrefetchScalarGridSpec(
            num_scalar_prefetch=1,
            grid=(owners,),
            in_specs=[pl.BlockSpec((share, width), lambda k, c: (0, 0))] * owners,
            out_specs=pl.BlockSpec((share, width), lambda k, c: (lax.rem(c[0] + k, owners), 0)),
        ),
        out_shape=jax.ShapeDtypeStruct((owners * share, width), kind),
        compiler_params=pltpu.CompilerParams(vmem_limit_bytes=8 * MIB),
        name="in_place",
    )(place, *blocks)


def totals_kernel(
    pick_ref, terms_ref, attn_ref, triple_ref, strength_ref, projection_in_ref,
    projection_out_ref, ffn_in_ref, ffn_out_ref, down_in_ref, down_out_ref, *, cuts,
):
    step = pl.program_id(0)
    sequences, _, rank, width = terms_ref.shape
    adapters = projection_out_ref.shape[0]
    shape = (adapters * rank, sequences * rank)
    to = lax.broadcasted_iota(jnp.int32, shape, 0)
    source = lax.broadcasted_iota(jnp.int32, shape, 1)
    wanted = jnp.full(shape, -1, jnp.int32)
    for sequence in range(sequences):
        wanted = jnp.where(
            (source >= sequence * rank) & (source < (sequence + 1) * rank),
            pick_ref[sequence] * rank + source - sequence * rank,
            wanted,
        )
    select = (to == wanted).astype(BF16)
    terms = terms_ref[:, 0].reshape(sequences * rank, width)

    def add_up(out_ref, start, wide):
        total = dot_low(select, terms[:, start : start + wide])
        out_ref[...] = total[:, : out_ref.shape[-1]].reshape(out_ref.shape)

    model = ffn_in_ref.shape[-1]
    add_up(attn_ref, cuts[2], model)

    @pl.when(step < 3)
    def _():
        add_up(triple_ref, cuts[3], triple_ref.shape[-1])

    @pl.when(step < 2)
    def _():
        add_up(ffn_in_ref, cuts[0], model)
        add_up(ffn_out_ref, cuts[1], ffn_out_ref.shape[-1])

    @pl.when(step == 2)
    def _():
        add_up(down_out_ref, cuts[0], model)
        add_up(down_in_ref, cuts[1], down_in_ref.shape[-1])

    @pl.when(step == 3)
    def _():
        add_up(projection_out_ref, cuts[0], model)
        add_up(projection_in_ref, cuts[1], projection_in_ref.shape[-1])
        add_up(strength_ref, cuts[3], LANES)


def totals(picks, terms, cuts, adapters, rank, model, features, hidden_units, heads):
    sequences, quarters, _, width = terms.shape
    part = lambda last, wide: pl.BlockSpec(
        (1, adapters, rank, wide), lambda q, c: (jnp.minimum(q, last), 0, 0, 0)
    )
    one = lambda wide: pl.BlockSpec((adapters, rank, wide), lambda q, c: (0, 0, 0))
    shape = lambda *dims: jax.ShapeDtypeStruct(dims, F32)
    return pl.pallas_call(
        functools.partial(totals_kernel, cuts=cuts),
        grid_spec=pltpu.PrefetchScalarGridSpec(
            num_scalar_prefetch=1,
            grid=(quarters,),
            in_specs=[pl.BlockSpec((sequences, 1, rank, width), lambda q, c: (0, q, 0, 0))],
            out_specs=[
                part(3, model), part(2, features), one(heads), one(features), one(model),
                part(1, model), part(1, hidden_units), one(hidden_units), one(model),
            ],
        ),
        out_shape=[
            shape(4, adapters, rank, model),
            shape(3, adapters, rank, features),
            shape(adapters, rank, heads),
            shape(adapters, rank, features),
            shape(adapters, rank, model),
            shape(2, adapters, rank, model),
            shape(2, adapters, rank, hidden_units),
            shape(adapters, rank, hidden_units),
            shape(adapters, rank, model),
        ],
        compiler_params=pltpu.CompilerParams(vmem_limit_bytes=56 * MIB),
        name="totals",
    )(picks, terms)


def shifted(block, axis, distance, wrap=True):
    size = lax.axis_size(axis)
    if wrap:
        route = [(i, (i + distance) % size) for i in range(size)]
    else:
        route = [(i, i + distance) for i in range(size) if 0 <= i + distance < size]
    return lax.ppermute(block, axis, route)


def sent_to_owners(parts, axis, order=(2, 1, 3)):
    received = {k: shifted(parts[k], axis, k) for k in order}
    return [parts[0]] + [received[k] for k in sorted(order)]


def blocks_of_others(block, axis):
    return [block] + [shifted(block, axis, -k) for k in (1, 2, 3)]


def blocks_by_ring(block, axis, ahead=None):
    half = block.shape[0] // 2
    before = shifted(block, axis, 1)
    after = shifted(block, axis, -1)
    if ahead is not None:
        before, after, ahead = lax.optimization_barrier((before, after, ahead))
    far = jnp.concatenate(
        [shifted(after[:half], axis, -1), shifted(before[half:], axis, 1)], axis=0
    )
    blocks = [block, after, far, before]
    return blocks if ahead is None else (blocks, ahead)


def paired_sum(block, axis):
    blocks = [part.astype(F32) for part in blocks_of_others(block, axis)]
    half = len(blocks) // 2
    while half:
        blocks = [blocks[i] + blocks[i + half] for i in range(half)]
        half //= 2
    return blocks[0]


def dot(left, right):
    return jnp.dot(left, right, preferred_element_type=F32)


def dot_nt(left, right):
    return lax.dot_general(left, right, (((1,), (1,)), ((), ())), preferred_element_type=F32)


def dot_tn(left, right):
    return lax.dot_general(left, right, (((0,), (0,)), ((), ())), preferred_element_type=F32)


def rms_scale(values, gain):
    return values * lax.rsqrt(jnp.mean(values * values, axis=-1, keepdims=True) + EPSILON) * gain


def rms_back(values, gain, grad):
    scale = lax.rsqrt(jnp.mean(values * values, axis=-1, keepdims=True) + EPSILON)
    gained = gain * grad
    return scale * gained - values * (scale**3) * jnp.mean(values * gained, axis=-1, keepdims=True)


def pad_columns(array, width):
    return jnp.pad(array, ((0, 0), (0, width - array.shape[1])))


def pad_rows(array, height):
    return jnp.pad(array, ((0, height - array.shape[0]), (0, 0)))


def on_device(
    tokens,
    cotangent,
    token_document_ids,
    sequence_adapter_index,
    mixer_norm_gain,
    head_norm_gain,
    feedforward_norm_gain,
    short_filter_kernels,
    query_weight,
    key_weight,
    value_weight,
    strength_weight,
    mixer_output_weight,
    gate_weight,
    up_weight,
    down_weight,
    adapter_attention_input,
    adapter_triple_output,
    adapter_strength_output,
    adapter_projection_input,
    adapter_projection_output,
    adapter_feedforward_input,
    adapter_feedforward_output,
    adapter_down_input,
    adapter_down_output,
):
    span, model = tokens.shape
    head_dim = head_norm_gain.shape[0]
    taps = short_filter_kernels.shape[1]
    heads = strength_weight.shape[1]
    features = heads * head_dim
    hidden_units = gate_weight.shape[1]
    adapters = adapter_attention_input.shape[1]
    rank = adapter_attention_input.shape[3]
    owners = lax.axis_size("tensor")
    place = lax.axis_index("tensor")
    position = lax.axis_index("context")
    share = span // owners
    everyone = ("weights", "context")

    def chunk_at(array, k):
        start = lax.rem(place + k, owners) * share
        return lax.dynamic_slice_in_dim(array, start, share, axis=0)

    mixer_pack = jnp.concatenate(
        [
            query_weight, key_weight, value_weight, strength_weight,
            jnp.full(
                (strength_weight.shape[0], LANES - heads),
                sequence_adapter_index[0].astype(BF16),
            ),
            mixer_output_weight.T,
        ],
        axis=1,
    )
    ffn_pack = jnp.concatenate([gate_weight, up_weight, down_weight.T], axis=1)
    mixer_all = lax.all_gather(mixer_pack, everyone, axis=0, tiled=True)
    ffn_all = lax.all_gather(ffn_pack, everyone, axis=0, tiled=True)
    triple = 3 * features + LANES
    weight_in = mixer_all[:, :triple]
    weight_out = mixer_all[:, triple:]
    weight_gate_up = ffn_all[:, : 2 * hidden_units]
    weight_down = ffn_all[:, 2 * hidden_units :]
    picks = mixer_all[:: mixer_all.shape[0] // lax.axis_size("weights"), 3 * features + heads]
    picks = picks.astype(jnp.int32)

    chosen = sequence_adapter_index[0]
    take = lambda table, axis: lax.dynamic_index_in_dim(table, chosen, axis, keepdims=False)
    attention_in = jnp.swapaxes(take(adapter_attention_input, 1), 1, 2).reshape(4 * rank, model)
    triple_out = take(adapter_triple_output, 1)
    strength_out = take(adapter_strength_output, 0)
    projection_in = jnp.swapaxes(take(adapter_projection_input, 0), 0, 1)
    projection_out = take(adapter_projection_output, 0)
    feedforward_in = jnp.swapaxes(take(adapter_feedforward_input, 1), 1, 2).reshape(2 * rank, model)
    feedforward_out = take(adapter_feedforward_output, 1)
    down_in_ext = pad_rows(jnp.swapaxes(take(adapter_down_input, 0), 0, 1), LANES)
    ffn_low = pad_rows(
        jnp.concatenate(
            [
                pad_columns(feedforward_out[0], 2 * hidden_units),
                jnp.pad(feedforward_out[1], ((0, 0), (hidden_units, 0))),
            ],
            axis=0,
        ),
        LANES,
    )
    down_out = take(adapter_down_output, 0)
    low_in = jnp.concatenate(
        [
            jnp.pad(triple_out[part], ((0, 0), (part * features, (2 - part) * features + LANES)))
            for part in range(3)
        ]
        + [jnp.pad(strength_out, ((0, 0), (3 * features, LANES - heads)))],
        axis=0,
    )

    padded_ids = jnp.concatenate(
        [jnp.full((HALO,), -1, jnp.int32), token_document_ids[0], jnp.full((HALO,), -2, jnp.int32)]
    )
    window = lax.dynamic_slice_in_dim(padded_ids, position * span, span + 2 * HALO)
    window = jnp.where(
        jnp.arange(span + 2 * HALO) < span + HALO, window, jnp.full_like(window, -2)
    )
    seg_column = jnp.broadcast_to(window[:, None], (span + 2 * HALO, LANES))
    seg_rows = window[HALO : HALO + span].reshape(span // CHUNK, CHUNK)
    kernels = jnp.transpose(short_filter_kernels, (1, 0, 2)).reshape(taps, -1)

    edge = shifted(tokens[span - HALO :], "context", 1, wrap=False)
    inputs_ext = jnp.concatenate([edge, tokens], axis=0).astype(F32)
    normed_ext = rms_scale(inputs_ext, mixer_norm_gain).astype(BF16)
    low_ext = dot_nt(normed_ext, attention_in).astype(BF16)
    projected = dot(normed_ext, weight_in) + dot(low_ext, low_in)
    normed = normed_ext[HALO:]
    low_attn = low_ext[HALO:]

    where = position[None]
    here = place[None]
    qp, op, offset, linear, *kept = delta_local(
        projected, kernels, seg_column, seg_rows, heads, head_dim, span, heads
    )
    one = shifted(offset, "context", 1, wrap=False)
    linear_two = lax.ppermute(linear, "context", [(2, 3)])
    second = (
        offset.astype(F32)
        + jnp.einsum("hij,hjk->hik", linear, one, preferred_element_type=F32)
    ).astype(BF16)
    out_ext = jnp.concatenate([weight_out, pad_rows(projection_in, LANES)], axis=0)
    second, out_ext = lax.optimization_barrier((second, out_ext))
    two = lax.ppermute(second, "context", [(1, 2)])
    three = lax.ppermute(second, "context", [(1, 3)])
    gain_row = head_norm_gain[None, :]
    head_low, attended, state, *branch_parts = attend(
        where, here, op, qp, one, two, linear_two, three, gain_row, out_ext, owners
    )
    linear_one = lax.ppermute(linear, "context", [(1, 0)])

    wide = model + LANES
    branch = sent_to_owners(branch_parts, "tensor")
    ffn_gain = feedforward_norm_gain[None, :]
    out_map = pad_rows(projection_out, LANES)
    in_map = pad_rows(feedforward_in, LANES)
    middle, packed, low_o = owner_call(
        middle_kernel, "middle_rows", here, share,
        [(part, "rows") for part in branch]
        + [(tokens, "span"), (out_map, "whole"), (ffn_gain, "whole"), (in_map, "whole")],
        [((share, model), F32), ((share, wide), BF16), ((share, LANES), BF16)],
    )
    low_grad_down = pad_columns(dot_nt(cotangent, down_out).astype(BF16), LANES)
    grad_hidden = dot(cotangent, weight_down) + dot(low_grad_down, down_in_ext)
    ffn_in, grad_hidden = blocks_by_ring(packed, "tensor", grad_hidden)

    back_parts, hidden_parts = [None] * owners, [None] * owners
    ffn_out_terms, down_in_terms = [], []
    for pair in ((1, 3), (2, 0)):
        chunks = jnp.stack([lax.rem(place + k, owners) for k in pair])
        hidden_pair, back_parts[pair[0]], back_parts[pair[1]], out_term, down_term = ffn_rows(
            chunks, ffn_in[pair[0]], ffn_in[pair[1]], weight_gate_up, ffn_low, grad_hidden,
            low_grad_down, rank, [F32 if k == 0 else BF16 for k in pair],
        )
        for i, k in enumerate(pair):
            hidden_parts[k] = hidden_pair[i * share : (i + 1) * share]
        ffn_out_terms.append(out_term)
        down_in_terms.append(down_term)
    back = sent_to_owners(back_parts, "tensor", (1, 3, 2))
    hidden = in_place(here, hidden_parts, hidden_units, BF16)
    down_all = dot_nt(hidden, weight_down).astype(BF16)
    back, down_all = lax.optimization_barrier((back, down_all))
    grad_middle, grad_packed = owner_call(
        functools.partial(back_kernel, rank=rank), "back_rows", here, share,
        [(part, "rows") for part in back]
        + [(cotangent, "span"), (middle, "rows"), (ffn_gain, "whole"), (in_map, "whole"),
           (out_map, "whole"), (low_o, "rows")],
        [((share, model), F32), ((share, wide), BF16)],
    )

    grad_blocks = blocks_by_ring(grad_packed, "tensor")

    grad_attended, own = attend_back(
        here, attended, qp, gain_row, out_ext, grad_blocks, heads, head_dim
    )
    hidden, down_all, own = lax.optimization_barrier((hidden, down_all, own))
    down_sum = lax.psum_scatter(down_all, "tensor", scatter_dimension=0, tiled=True).astype(F32)
    down_low = dot_nt(down_in_ext[:rank], hidden).astype(BF16)
    own_one = shifted(own, "context", -1, wrap=False)
    own_one, down_low = lax.optimization_barrier((own_one, down_low))
    own_second = (
        own.astype(F32) + jnp.einsum("hji,hjk->hik", linear, own_one, preferred_element_type=F32)
    ).astype(BF16)
    own_two = lax.ppermute(own_second, "context", [(2, 1)])
    own_three = lax.ppermute(own_second, "context", [(2, 0)])

    low_down = paired_sum(down_low, "tensor").astype(BF16)

    grad_projected, halo, tail = delta_back(
        projected, kernels, seg_column, seg_rows, kept, state, grad_attended, where,
        (own_one, own_two, linear_one, own_three), heads, head_dim, span, heads,
    )
    returned = shifted(halo, "context", -1, wrap=False)
    low_down_own = lax.dynamic_slice_in_dim(low_down, place * share, share, axis=1)
    block_own = (middle + down_sum + dot_tn(low_down_own, down_out)).astype(BF16)
    returned, block_own = lax.optimization_barrier((returned, block_own))
    block_half = share // 2
    block_before = shifted(block_own, "tensor", 1)
    block_after = shifted(block_own, "tensor", -1)
    grad_projected = lax.dynamic_update_slice(
        grad_projected, (tail + returned).astype(BF16), (span - HALO, 0)
    )

    low_part = dot_nt(grad_projected, low_in).astype(BF16)
    low_parts = blocks_of_others(low_part, "tensor")
    early_width = model + hidden_units
    (early,) = span_call(
        functools.partial(early_kernel, rank=rank), "early_terms", (here,),
        [*grad_blocks, *ffn_in, head_low, low_down, cotangent, *ffn_out_terms, *down_in_terms],
        [((4, rank, early_width), BF16)], [], 56,
    )
    *low_parts, block_before, block_after, early = lax.optimization_barrier(
        (*low_parts, block_before, block_after, early)
    )
    late_width = model + features
    low_grad_attn, *quarters = span_call(
        functools.partial(late_kernel, rank=rank), "late_terms", (where,),
        [*low_parts, normed, low_attn, grad_projected, early],
        [((span, 4 * rank), BF16)] + [((rank, early_width + late_width), BF16)] * 4,
        [pltpu.VMEM((4, rank, late_width), BF16)], 24,
    )
    quarters = sent_to_owners(quarters, "context")
    grad_rows, _ = lax.optimization_barrier((grad_projected, low_grad_attn))
    normed_parts = dot_nt(grad_rows, weight_in).astype(BF16)
    *quarters, normed_parts = lax.optimization_barrier((*quarters, normed_parts))
    normed_sent = sent_to_owners([chunk_at(normed_parts, k) for k in range(owners)], "tensor")
    block_far = jnp.concatenate(
        [
            shifted(block_after[:block_half], "tensor", -1),
            shifted(block_before[block_half:], "tensor", 1),
        ],
        axis=0,
    )
    block_out = in_place(here, [block_own, block_after, block_far, block_before], model, BF16)
    (grad_tokens,) = owner_call(
        tokens_kernel, "token_rows", here, share,
        [(part, "rows") for part in normed_sent]
        + [(low_grad_attn, "span"), (attention_in, "whole"), (tokens, "span"),
           (mixer_norm_gain[None, :], "whole"), (grad_middle, "rows")],
        [((share, model), BF16)],
    )
    tokens_grad = in_place(here, blocks_by_ring(grad_tokens, "tensor"), model, F32)

    quarter = sum(part.astype(F32) for part in quarters).astype(BF16)
    terms = lax.all_gather(quarter, everyone, axis=0, tiled=False)
    sequences = lax.axis_size("weights")
    terms = terms.reshape(sequences, 4, rank, -1)
    cuts = (0, model, model + hidden_units, 2 * model + hidden_units)
    sums = totals(
        picks, terms, cuts, adapters, rank, model, features, hidden_units, heads
    )
    flip = lambda array: jnp.swapaxes(array, -1, -2)
    return (
        block_out,
        tokens_grad,
        flip(sums[0]),
        sums[1],
        sums[2],
        flip(sums[3]),
        sums[4],
        flip(sums[5]),
        sums[6],
        flip(sums[7]),
        sums[8],
    )


def solution(mesh):
    rows = P(("weights", "context"), None)
    return jax.shard_map(
        on_device,
        mesh=mesh,
        in_specs=(
            rows,
            rows,
            P("weights", None),
            P("weights"),
            P(),
            P(),
            P(),
            P(None, None, "tensor"),
            P(("weights", "context"), "tensor"),
            P(("weights", "context"), "tensor"),
            P(("weights", "context"), "tensor"),
            P(("weights", "context"), "tensor"),
            P("tensor", ("weights", "context")),
            P(("weights", "context"), "tensor"),
            P(("weights", "context"), "tensor"),
            P("tensor", ("weights", "context")),
            P(),
            P(None, None, None, "tensor"),
            P(None, None, "tensor"),
            P(None, "tensor", None),
            P(),
            P(),
            P(None, None, None, "tensor"),
            P(None, "tensor", None),
            P(),
        ),
        out_specs=(
            rows,
            rows,
            P(),
            P(None, None, None, "tensor"),
            P(None, None, "tensor"),
            P(None, "tensor", None),
            P(),
            P(),
            P(None, None, None, "tensor"),
            P(None, "tensor", None),
            P(),
        ),
        check_vma=False,
    )
```

```python
import functools

import jax
import jax.numpy as jnp
from jax import lax
from jax.experimental import pallas as pl
from jax.experimental.pallas import tpu as pltpu
from jax.sharding import PartitionSpec as P

EPSILON = 1e-06
HALO = 8
CHUNK = 128
LANES = 128
F32 = jnp.float32
BF16 = jnp.bfloat16
MIB = 1024 * 1024


def dot_low(left, right, left_dim=1, right_dim=0):
    return lax.dot_general(
        left.astype(BF16),
        right.astype(BF16),
        (((left_dim,), (right_dim,)), ((), ())),
        preferred_element_type=F32,
    )


def conv_rows(x_ref, columns, taps_ref, seg_ref, span):
    here = seg_ref[HALO : HALO + span, :]
    total = taps_ref[0:1, columns] * x_ref[HALO : HALO + span, columns]
    for tap in range(1, taps_ref.shape[0]):
        same = seg_ref[HALO - tap : HALO - tap + span, :] == here
        total = total + taps_ref[tap : tap + 1, columns] * jnp.where(
            same, x_ref[HALO - tap : HALO - tap + span, columns], 0.0
        )
    return total


def inverse_norm(values):
    return lax.rsqrt(jnp.sum(values * values, axis=-1, keepdims=True) + EPSILON)


def head_column(array, head):
    lane = lax.broadcasted_iota(jnp.int32, array.shape, 1)
    return jnp.sum(jnp.where(lane == head, array, 0.0), axis=1, keepdims=True)


def chunk_masks(seg_ref, row_ref, chunk):
    start = HALO + chunk * CHUNK
    column = seg_ref[start : start + CHUNK, :]
    row = row_ref[chunk : chunk + 1, :]
    before = seg_ref[start - 1 : start, :]
    last = seg_ref[start + CHUNK - 1 : start + CHUNK, :]
    same = column == row
    row_ids = lax.broadcasted_iota(jnp.int32, (CHUNK, CHUNK), 0)
    col_ids = lax.broadcasted_iota(jnp.int32, (CHUNK, CHUNK), 1)
    strict = (same & (row_ids > col_ids)).astype(F32)
    causal = (same & (row_ids >= col_ids)).astype(F32)
    running = (column == before).astype(F32)
    closing = (column == last).astype(F32)
    carried = (before == last).astype(F32)
    return strict, causal, running, closing, carried


def unit_lower_inverses(lowers):
    size = lowers[0].shape[0]
    row_ids = lax.broadcasted_iota(jnp.int32, (size, size), 0)
    col_ids = lax.broadcasted_iota(jnp.int32, (size, size), 1)
    identity = (row_ids == col_ids).astype(F32)
    pair = (row_ids >> 1) == (col_ids >> 1)
    highs = [lower.astype(BF16) for lower in lowers]
    inverses = [identity - jnp.where(pair, lower, 0.0) for lower in lowers]
    bits = 2
    while (1 << bits) <= size:
        joined = ((row_ids >> bits) == (col_ids >> bits)) & (
            (row_ids >> (bits - 1)) != (col_ids >> (bits - 1))
        )
        rounded = [inverse.astype(BF16) for inverse in inverses]
        inner = [
            dot_low(jnp.where(joined, high, jnp.zeros_like(high)), inverse)
            for high, inverse in zip(highs, rounded)
        ]
        inverses = [
            inverse - dot_low(low, part) for inverse, low, part in zip(inverses, rounded, inner)
        ]
        bits += 1
    rounded = [inverse.astype(BF16) for inverse in inverses]
    rests = [(lower - high.astype(F32)).astype(BF16) for lower, high in zip(lowers, highs)]
    residuals = [
        identity - low.astype(F32) - (dot_low(high, low) + dot_low(rest, low))
        for low, high, rest in zip(rounded, highs, rests)
    ]
    return [low.astype(F32) + dot_low(low, part) for low, part in zip(rounded, residuals)]


def delta_local_kernel(
    q_ref, k_ref, v_ref, logit_ref, taps_q, taps_k, taps_v, seg_ref, row_ref,
    qp_ref, op_ref, offset_ref, linear_ref, inverse_ref, prefix_ref, solved_ref, score_ref, zq_ref, zk_ref, zv_ref,
    *, span, head_dim, group,
):
    chunks = span // CHUNK
    step = pl.program_id(0)
    masks = [chunk_masks(seg_ref, row_ref, chunk) for chunk in range(chunks)]
    rates_all = jax.nn.sigmoid(logit_ref[HALO : HALO + span, :])
    work = []
    for local in range(group):
        columns = slice(local * head_dim, (local + 1) * head_dim)
        zq_ref[:, columns] = conv_rows(q_ref, columns, taps_q, seg_ref, span)
        zk_ref[:, columns] = conv_rows(k_ref, columns, taps_k, seg_ref, span)
        zv_ref[:, columns] = conv_rows(v_ref, columns, taps_v, seg_ref, span)
        rates_head = head_column(rates_all, step * group + local)
        for chunk in range(chunks):
            rows = slice(chunk * CHUNK, (chunk + 1) * CHUNK)
            queries = jax.nn.silu(zq_ref[rows, columns])
            queries = (queries * (inverse_norm(queries) * head_dim**-0.5)).astype(BF16)
            keys = jax.nn.silu(zk_ref[rows, columns])
            keys = (keys * inverse_norm(keys)).astype(BF16)
            values = jax.nn.silu(zv_ref[rows, columns]).astype(BF16)
            work.append((local, chunk, queries, keys, values, rates_head[rows]))
    lowers = [
        dot_low(keys, keys, 1, 1) * (rates * masks[chunk][0])
        for _, chunk, _, keys, _, rates in work
    ]
    inverses = unit_lower_inverses(lowers)
    parts = []
    for (local, chunk, queries, keys, values, rates), inverse in zip(work, inverses):
        rows = slice(chunk * CHUNK, (chunk + 1) * CHUNK)
        strict, causal, running, closing, carried = masks[chunk]
        inverse = inverse.astype(BF16)
        inverse_ref[local, rows, :] = inverse
        right = jnp.concatenate([rates * values.astype(F32), rates * keys.astype(F32)], axis=1)
        solved = dot_low(inverse, right)
        solved_ref[local, rows, :] = solved.astype(BF16)
        updates = solved[:, :head_dim]
        weighted = running * solved[:, head_dim:]
        both = jnp.concatenate([updates, weighted], axis=1).astype(BF16)
        scores = (dot_low(queries, keys, 1, 1) * causal).astype(BF16)
        score_ref[local, rows, :] = scores
        near = dot_low(scores, both)
        ends = dot_low(closing * keys.astype(F32), both, 0, 0)
        reach = running * queries.astype(F32) - near[:, head_dim:]
        parts.append((near[:, :head_dim], reach.astype(BF16), ends))
    row_ids = lax.broadcasted_iota(jnp.int32, (head_dim, head_dim), 0)
    col_ids = lax.broadcasted_iota(jnp.int32, (head_dim, head_dim), 1)
    identity = (row_ids == col_ids).astype(F32)
    start = jnp.concatenate([jnp.zeros((head_dim, head_dim), F32), identity], axis=1)
    prefixes = [start] * group
    for chunk in range(chunks):
        rows = slice(chunk * CHUNK, (chunk + 1) * CHUNK)
        carried = masks[chunk][4]
        for local in range(group):
            columns = slice(local * head_dim, (local + 1) * head_dim)
            near, reach, ends = parts[local * chunks + chunk]
            prefix = prefixes[local]
            prefix_ref[local, chunk * head_dim : (chunk + 1) * head_dim, :] = prefix.astype(BF16)
            seen = dot_low(reach, prefix)
            op_ref[rows, columns] = near + seen[:, :head_dim]
            qp_ref[rows, columns] = seen[:, head_dim:].astype(BF16)
            moved = jnp.concatenate([carried, carried], axis=1) * prefix - dot_low(
                ends[:, head_dim:], prefix
            )
            prefixes[local] = jnp.concatenate(
                [moved[:, :head_dim] + ends[:, :head_dim], moved[:, head_dim:]], axis=1
            )
    for local in range(group):
        offset_ref[local] = prefixes[local][:, :head_dim].astype(BF16)
        linear_ref[local] = prefixes[local][:, head_dim:].astype(BF16)


def delta_local(projected, taps, seg_column, seg_rows, heads, head_dim, span, group):
    rows = projected.shape[0]
    width = group * head_dim
    steps = heads // group
    third = lambda part: pl.BlockSpec((rows, width), lambda i: (0, part * steps + i))
    tap_third = lambda part: pl.BlockSpec((taps.shape[0], width), lambda i: (0, part * steps + i))
    whole = lambda array: pl.BlockSpec(array.shape, lambda i: (0,) * array.ndim)
    by_head = lambda *shape: pl.BlockSpec((group,) + shape, lambda i: (i, 0, 0))
    columns = pl.BlockSpec((span, width), lambda i: (0, i))
    chunks = span // CHUNK
    kept = lambda *shape, kind=BF16: jax.ShapeDtypeStruct(shape, kind)
    return pl.pallas_call(
        functools.partial(delta_local_kernel, span=span, head_dim=head_dim, group=group),
        grid=(steps,),
        in_specs=[
            third(0), third(1), third(2),
            pl.BlockSpec((rows, LANES), lambda i: (0, 3 * heads * head_dim // LANES)),
            tap_third(0), tap_third(1), tap_third(2), whole(seg_column), whole(seg_rows),
        ],
        out_specs=[
            columns, columns, by_head(head_dim, head_dim), by_head(head_dim, head_dim),
            by_head(span, CHUNK),
            by_head(chunks * head_dim, 2 * head_dim), by_head(span, 2 * head_dim),
            by_head(span, CHUNK), columns, columns, columns,
        ],
        out_shape=[
            kept(span, heads * head_dim),
            kept(span, heads * head_dim, kind=F32),
            kept(heads, head_dim, head_dim),
            kept(heads, head_dim, head_dim),
            kept(heads, span, CHUNK),
            kept(heads, chunks * head_dim, 2 * head_dim),
            kept(heads, span, 2 * head_dim),
            kept(heads, span, CHUNK),
            kept(span, heads * head_dim, kind=F32),
            kept(span, heads * head_dim, kind=F32),
            kept(span, heads * head_dim, kind=F32),
        ],
        compiler_params=pltpu.CompilerParams(vmem_limit_bytes=22 * MIB),
        name="delta_local",
    )(projected, projected, projected, projected, taps, taps, taps, seg_column, seg_rows)


def attend_kernel(
    position_ref, place_ref, op_ref, qp_ref, one_ref, two_ref, map_ref, three_ref, gain_ref, weight_ref,
    out_ref, att_ref, state_ref, *part_refs,
):
    heads, head_dim = one_ref.shape[0], one_ref.shape[1]
    owners = len(part_refs)
    share = out_ref.shape[0] // owners
    for head in range(heads):
        columns = slice(head * head_dim, (head + 1) * head_dim)
        through = one_ref[head].astype(F32) + dot_low(map_ref[head], three_ref[head])
        state = jnp.where(position_ref[0] == 2, two_ref[head].astype(F32), through)
        state_ref[head] = state.astype(BF16)
        attended = op_ref[:, columns] + dot_low(qp_ref[:, columns], state)
        att_ref[:, columns] = attended
        scale = lax.rsqrt(jnp.mean(attended * attended, axis=-1, keepdims=True) + EPSILON)
        out_ref[:, columns] = (attended * scale * gain_ref[...]).astype(BF16)
    for k, part_ref in enumerate(part_refs):
        start = lax.rem(place_ref[0] + k, owners) * share
        rows = out_ref[pl.ds(pl.multiple_of(start, share), share), :]
        part_ref[...] = dot_low(rows, weight_ref[...], 1, 1).astype(BF16)


def attend(position, place, op, qp, one, two, mapped, three, gain, weight, owners):
    vmem = pl.BlockSpec(memory_space=pltpu.VMEM)
    smem = pl.BlockSpec(memory_space=pltpu.SMEM)
    part = jax.ShapeDtypeStruct((op.shape[0] // owners, weight.shape[0]), BF16)
    return pl.pallas_call(
        attend_kernel,
        in_specs=[smem] * 2 + [vmem] * 8,
        out_specs=[vmem] * (3 + owners),
        out_shape=[
            jax.ShapeDtypeStruct(op.shape, BF16),
            jax.ShapeDtypeStruct(op.shape, F32),
            jax.ShapeDtypeStruct(one.shape, BF16),
        ]
        + [part] * owners,
        compiler_params=pltpu.CompilerParams(vmem_limit_bytes=14 * MIB),
        name="attend",
    )(position, place, op, qp, one, two, mapped, three, gain, weight)


def attend_back_kernel(
    place_ref, att_ref, qp_ref, gain_ref, weight_ref, *refs
):
    *block_refs, out_ref, own_ref, grad_ref = refs
    heads, head_dim = own_ref.shape[0], own_ref.shape[1]
    owners = len(block_refs)
    share = out_ref.shape[0] // owners
    for k, block_ref in enumerate(block_refs):
        start = lax.rem(place_ref[0] + k, owners) * share
        grad_ref[pl.ds(pl.multiple_of(start, share), share), :] = dot_low(
            block_ref[...], weight_ref[...]
        )
    for head in range(heads):
        columns = slice(head * head_dim, (head + 1) * head_dim)
        attended = att_ref[:, columns]
        scale = lax.rsqrt(jnp.mean(attended * attended, axis=-1, keepdims=True) + EPSILON)
        gained = grad_ref[:, columns] * gain_ref[...]
        along = jnp.mean(attended * gained, axis=-1, keepdims=True)
        grad = (scale * gained - attended * (scale * scale * scale * along)).astype(BF16)
        out_ref[:, columns] = grad
        own_ref[head] = dot_low(qp_ref[:, columns], grad, 0, 0).astype(BF16)


def attend_back(place, attended, qp, gain, weight, blocks, heads, head_dim):
    vmem = pl.BlockSpec(memory_space=pltpu.VMEM)
    return pl.pallas_call(
        attend_back_kernel,
        in_specs=[pl.BlockSpec(memory_space=pltpu.SMEM)] + [vmem] * (4 + len(blocks)),
        out_specs=[vmem] * 2,
        out_shape=[
            jax.ShapeDtypeStruct(attended.shape, BF16),
            jax.ShapeDtypeStruct((heads, head_dim, head_dim), BF16),
        ],
        scratch_shapes=[pltpu.VMEM(attended.shape, F32)],
        compiler_params=pltpu.CompilerParams(vmem_limit_bytes=14 * MIB),
        name="attend_back",
    )(place, attended, qp, gain, weight, *blocks)


def delta_back_kernel(
    zq_ref, zk_ref, zv_ref, logit_ref, taps_q, taps_k, taps_v, seg_ref, row_ref,
    inverse_ref, prefix_ref, solved_ref, score_ref, state_ref, grad_ref,
    one_ref, two_ref, three_ref, map_one_ref, map_two_ref,
    out_ref, halo_ref, tail_ref, dz_ref, *, span, heads, head_dim, group,
):
    chunks = span // CHUNK
    step = pl.program_id(0)
    features = heads * head_dim
    masks = [chunk_masks(seg_ref, row_ref, chunk) for chunk in range(chunks)]
    rates_all = jax.nn.sigmoid(logit_ref[HALO : HALO + span, :])
    lane = lax.broadcasted_iota(jnp.int32, (CHUNK, LANES), 1)

    @pl.when(step == 0)
    def _():
        out_ref[:, 3 * features :] = jnp.zeros((span, LANES), BF16)
        for slot in range(3 * group):
            dz_ref[slot, 0:HALO, :] = jnp.zeros((HALO, head_dim), F32)
            dz_ref[slot, HALO + span :, :] = jnp.zeros((HALO, head_dim), F32)

    kept, leavings = [], []
    for local in range(group):
        columns = slice(local * head_dim, (local + 1) * head_dim)
        rates_head = head_column(rates_all, step * group + local)
        entry = state_ref[local]
        through = two_ref[local].astype(F32) + dot_low(
            map_two_ref[local], three_ref[local], 0, 0
        )
        leavings.append(one_ref[local].astype(F32) + dot_low(map_one_ref[local], through, 0, 0))
        for chunk in range(chunks):
            rows = slice(chunk * CHUNK, (chunk + 1) * CHUNK)
            strict, causal, running, closing, carried = masks[chunk]
            queries = jax.nn.silu(zq_ref[rows, columns])
            scale_q = inverse_norm(queries)
            queries = queries * scale_q
            keys = jax.nn.silu(zk_ref[rows, columns])
            scale_k = inverse_norm(keys)
            keys = keys * scale_k
            low_q = (queries * head_dim**-0.5).astype(BF16)
            low_k = keys.astype(BF16)
            values = jax.nn.silu(zv_ref[rows, columns])
            solved = solved_ref[local, rows, :].astype(F32)
            weighted = (running * solved[:, head_dim:]).astype(BF16)
            prefix = prefix_ref[local, chunk * head_dim : (chunk + 1) * head_dim, :]
            state = (
                prefix[:, :head_dim].astype(F32) + dot_low(prefix[:, head_dim:], entry)
            ).astype(BF16)
            errors = (solved[:, :head_dim] - dot_low(weighted, state)).astype(BF16)
            scores = score_ref[local, rows, :]
            grad = grad_ref[rows, columns]
            near = dot_low(scores, grad, 0, 0)
            far = dot_low(running * low_q.astype(F32), grad, 0, 0)
            grad_scores = (dot_low(grad, errors, 1, 1) * causal).astype(BF16)
            kept.append((queries, scale_q, keys, scale_k, low_q, low_k, values,
                         rates_head[rows], weighted, state, errors, near, far, grad_scores))
    grad_errors_all = [None] * (group * chunks)
    leaving_all = [None] * (group * chunks)
    for chunk in reversed(range(chunks)):
        strict, causal, running, closing, carried = masks[chunk]
        for local in range(group):
            item = local * chunks + chunk
            low_k, weighted, near, far = (kept[item][i] for i in (5, 8, 11, 12))
            leaving = leavings[local]
            low_leaving = leaving.astype(BF16)
            leaving_all[item] = low_leaving
            grad_errors = near + closing * dot_low(low_k, low_leaving)
            grad_errors_all[item] = grad_errors.astype(BF16)
            leavings[local] = (
                carried * leaving + far - dot_low(weighted, grad_errors_all[item], 0, 0)
            )
    for local in range(group):
        columns = slice(local * head_dim, (local + 1) * head_dim)
        head = step * group + local
        for chunk in range(chunks):
            rows = slice(chunk * CHUNK, (chunk + 1) * CHUNK)
            inner = slice(HALO + chunk * CHUNK, HALO + (chunk + 1) * CHUNK)
            strict, causal, running, closing, carried = masks[chunk]
            item = local * chunks + chunk
            (queries, scale_q, keys, scale_k, low_q, low_k, values, rates, weighted, state,
             errors, near, far, grad_scores) = kept[item]
            grad_errors, leaving = grad_errors_all[item], leaving_all[item]
            grad = grad_ref[rows, columns]
            grad_queries = running * dot_low(grad, state, 1, 1) + dot_low(grad_scores, low_k)
            grad_keys = dot_low(grad_scores, low_q, 0, 0) + closing * dot_low(
                errors, leaving, 1, 1
            )
            grad_weighted = -running * dot_low(grad_errors, state, 1, 1)
            grad_right = dot_low(
                inverse_ref[local, rows, :],
                jnp.concatenate([grad_errors, grad_weighted.astype(BF16)], axis=1), 0, 0,
            )
            right_v, right_k = grad_right[:, :head_dim], grad_right[:, head_dim:]
            grad_lower = -dot_low(grad_right, solved_ref[local, rows, :], 1, 1) * strict
            gram = dot_low(low_k, low_k, 1, 1)
            grad_rates = jnp.sum(
                right_v * values + right_k * keys + grad_lower * gram, axis=1, keepdims=True
            )
            grad_gram = (rates * grad_lower).astype(BF16)
            grad_keys = (
                grad_keys
                + rates * right_k
                + dot_low(grad_gram, low_k)
                + dot_low(grad_gram, low_k, 0, 0)
            )
            grad_logit = grad_rates * rates * (1.0 - rates)
            previous = out_ref[rows, 3 * features :].astype(F32)
            out_ref[rows, 3 * features :] = jnp.where(lane == head, grad_logit, previous).astype(BF16)
            grad_queries = grad_queries * head_dim**-0.5
            grad_queries = scale_q * (
                grad_queries - queries * jnp.sum(queries * grad_queries, axis=-1, keepdims=True)
            )
            grad_keys = scale_k * (
                grad_keys - keys * jnp.sum(keys * grad_keys, axis=-1, keepdims=True)
            )
            for part, (z_ref, grad_part) in enumerate(
                ((zq_ref, grad_queries), (zk_ref, grad_keys), (zv_ref, rates * right_v))
            ):
                conv = z_ref[rows, columns]
                sig = jax.nn.sigmoid(conv)
                dz_ref[local * 3 + part, inner, :] = grad_part * (
                    sig * (1.0 + conv * (1.0 - sig))
                )
        here = seg_ref[0 : HALO + span, :]
        for part, taps in enumerate((taps_q, taps_k, taps_v)):
            slot = local * 3 + part
            total = taps[0:1, columns] * dz_ref[slot, 0 : HALO + span, :]
            for tap in range(1, taps.shape[0]):
                same = seg_ref[tap : tap + HALO + span, :] == here
                total = total + taps[tap : tap + 1, columns] * jnp.where(
                    same, dz_ref[slot, tap : tap + HALO + span, :], 0.0
                )
            place = pl.ds(pl.multiple_of(part * features + head * head_dim, LANES), head_dim)
            halo_ref[:, place] = total[:HALO]
            tail_ref[:, place] = total[span:]
            out_ref[:, place] = total[HALO:].astype(BF16)


def delta_back(
    projected, taps, seg_column, seg_rows, kept, state, grad, arrived, heads, head_dim, span, group,
):
    inverse, prefix, solved, scores, conv_q, conv_k, conv_v = kept
    rows = projected.shape[0]
    width = group * head_dim
    steps = heads // group
    columns = pl.BlockSpec((span, width), lambda i: (0, i))
    tap_third = lambda part: pl.BlockSpec((taps.shape[0], width), lambda i: (0, part * steps + i))
    whole = lambda array: pl.BlockSpec(array.shape, lambda i: (0,) * array.ndim)
    by_head = lambda array: pl.BlockSpec((group,) + array.shape[1:], lambda i: (i, 0, 0))
    total = 3 * heads * head_dim
    return pl.pallas_call(
        functools.partial(
            delta_back_kernel, span=span, heads=heads, head_dim=head_dim, group=group
        ),
        grid=(steps,),
        in_specs=[
            columns, columns, columns,
            pl.BlockSpec((rows, LANES), lambda i: (0, total // LANES)),
            tap_third(0), tap_third(1), tap_third(2), whole(seg_column), whole(seg_rows),
            by_head(inverse), by_head(prefix), by_head(solved), by_head(scores), by_head(state),
            columns, *[by_head(array) for array in arrived],
        ],
        out_specs=[
            pl.BlockSpec((span, total + LANES), lambda i: (0, 0)),
            pl.BlockSpec((HALO, total), lambda i: (0, 0)),
            pl.BlockSpec((HALO, total), lambda i: (0, 0)),
        ],
        out_shape=[
            jax.ShapeDtypeStruct((span, total + LANES), BF16),
            jax.ShapeDtypeStruct((HALO, total), F32),
            jax.ShapeDtypeStruct((HALO, total), F32),
        ],
        scratch_shapes=[pltpu.VMEM((3 * group, span + 2 * HALO, head_dim), F32)],
        compiler_params=pltpu.CompilerParams(vmem_limit_bytes=56 * MIB),
        name="delta_back",
    )(
        conv_q, conv_k, conv_v, projected, taps, taps, taps, seg_column, seg_rows,
        inverse, prefix, solved, scores, state, grad, *arrived,
    )


def normed_grad(values, gain, grad):
    scale = lax.rsqrt(jnp.mean(values * values, axis=-1, keepdims=True) + EPSILON)
    gained = gain * grad
    along = jnp.mean(values * gained, axis=-1, keepdims=True)
    return scale * gained - values * (scale * scale * scale * along)


def added(refs, columns):
    total = refs[0][:, columns].astype(F32)
    for ref in refs[1:]:
        total = total + ref[:, columns].astype(F32)
    return total


def middle_kernel(
    place_ref, own_ref, one_ref, two_ref, three_ref, tokens_ref, out_map_ref, gain_ref, in_map_ref,
    middle_ref, packed_ref, low_ref,
):
    model = tokens_ref.shape[1]
    refs = (own_ref, one_ref, two_ref, three_ref)
    low = added(refs, slice(model, model + LANES)).astype(BF16)
    low_ref[...] = low
    middle = (
        tokens_ref[...].astype(F32)
        + added(refs, slice(0, model))
        + dot_low(low, out_map_ref[...])
    )
    middle_ref[...] = middle
    scale = lax.rsqrt(jnp.mean(middle * middle, axis=-1, keepdims=True) + EPSILON)
    normed = (middle * scale * gain_ref[...]).astype(BF16)
    packed_ref[:, :model] = normed
    packed_ref[:, model:] = dot_low(normed, in_map_ref[...], 1, 1).astype(BF16)


def back_kernel(
    place_ref, own_ref, one_ref, two_ref, three_ref, cot_ref, middle_in, gain_ref, in_map_ref,
    out_map_ref, low_ref, grad_ref, packed_ref, *, rank,
):
    model = cot_ref.shape[1]
    refs = (own_ref, one_ref, two_ref, three_ref)
    low_ffn = added(refs, slice(model, model + LANES)).astype(BF16)
    grad = added(refs, slice(0, model)) + dot_low(low_ffn, in_map_ref[...])
    grad = cot_ref[...].astype(F32) + normed_grad(middle_in[...], gain_ref[...], grad)
    grad_ref[...] = grad
    rounded = grad.astype(BF16)
    packed_ref[:, :model] = rounded
    low_out = dot_low(rounded, out_map_ref[...], 1, 1).astype(BF16).astype(F32)
    packed_ref[:, model:] = (
        low_out
        + pltpu.roll(low_ref[...].astype(F32), rank, 1)
        + pltpu.roll(low_ffn.astype(F32), 2 * rank, 1)
    ).astype(BF16)


def tokens_kernel(
    place_ref, own_ref, one_ref, two_ref, three_ref, low_ref, in_map_ref, tokens_ref, gain_ref,
    grad_ref, out_ref,
):
    refs = (own_ref, one_ref, two_ref, three_ref)
    grad = added(refs, slice(None)) + dot_low(low_ref[...], in_map_ref[...])
    out_ref[...] = (
        grad_ref[...] + normed_grad(tokens_ref[...].astype(F32), gain_ref[...], grad)
    ).astype(BF16)


def owner_call(kernel, name, place, share, arrays, outs, strips=2):
    strip = share // strips

    def spec(array, mark):
        if mark == "rows":
            return pl.BlockSpec((strip, array.shape[1]), lambda i, c: (i, 0))
        if mark == "span":
            return pl.BlockSpec((strip, array.shape[1]), lambda i, c: (c[0] * strips + i, 0))
        return pl.BlockSpec(array.shape, lambda i, c: (0, 0))

    return pl.pallas_call(
        kernel,
        grid_spec=pltpu.PrefetchScalarGridSpec(
            num_scalar_prefetch=1,
            grid=(strips,),
            in_specs=[spec(array, mark) for array, mark in arrays],
            out_specs=[pl.BlockSpec((strip, shape[1]), lambda i, c: (i, 0)) for shape, _ in outs],
        ),
        out_shape=[jax.ShapeDtypeStruct(shape, kind) for shape, kind in outs],
        compiler_params=pltpu.CompilerParams(vmem_limit_bytes=56 * MIB),
        name=name,
    )(place, *[array for array, _ in arrays])


def early_kernel(
    place_ref, g0, g1, g2, g3, x0, x1, x2, x3, head_ref, low_down_ref, cot_ref,
    out_one, out_two, down_one, down_two, pack_ref, *, rank,
):
    model = cot_ref.shape[1]
    hidden_units = down_one.shape[1]
    owners, share = 4, g0.shape[0]
    through_g, through_x, through_h = 0.0, 0.0, 0.0
    for k, (g_ref, x_ref) in enumerate(zip((g0, g1, g2, g3), (x0, x1, x2, x3))):
        low = g_ref[:, model:]
        start = lax.rem(place_ref[0] + k, owners) * share
        heads = head_ref[pl.ds(pl.multiple_of(start, share), share), :]
        through_g = through_g + dot_low(low, g_ref[:, :model], 0, 0)
        through_x = through_x + dot_low(low, x_ref[:, :model], 0, 0)
        through_h = through_h + dot_low(low, heads, 0, 0)
    out_terms = out_one[...] + out_two[...]
    pack_ref[0, :, :model] = through_x[2 * rank : 3 * rank].astype(BF16)
    pack_ref[0, :, model:] = out_terms[:rank, :hidden_units].astype(BF16)
    pack_ref[1, :, :model] = through_x[3 * rank : 4 * rank].astype(BF16)
    pack_ref[1, :, model:] = out_terms[rank:, hidden_units:].astype(BF16)
    pack_ref[2, :, :model] = dot_low(low_down_ref[...], cot_ref[...]).astype(BF16)
    pack_ref[2, :, model:] = (down_one[...] + down_two[...]).astype(BF16)
    pack_ref[3, :, :model] = through_g[rank : 2 * rank].astype(BF16)
    pack_ref[3, :, model:] = jnp.zeros((rank, hidden_units), BF16)
    pack_ref[3, :, model : model + through_h.shape[1]] = through_h[:rank].astype(BF16)


def late_kernel(
    position_ref, p0, p1, p2, p3, normed_ref, low_ref, grad_ref, early_ref, low_out_ref, *refs, rank
):
    *out_refs, pack_ref = refs
    model = normed_ref.shape[1]
    features = (grad_ref.shape[1] - LANES) // 3
    total = (p0[...].astype(F32) + p2[...].astype(F32)) + (
        p1[...].astype(F32) + p3[...].astype(F32)
    )
    low_grad = total.astype(BF16)
    low_out_ref[...] = low_grad
    items = dot_low(low_grad, normed_ref[...], 0, 0)
    blocks = dot_low(low_ref[...], grad_ref[...], 0, 0)
    for part in range(4):
        rows = slice(part * rank, (part + 1) * rank)
        pack_ref[part, :, :model] = items[rows].astype(BF16)
        if part < 3:
            pack_ref[part, :, model:] = blocks[rows, part * features : (part + 1) * features].astype(BF16)
        else:
            pack_ref[part, :, model:] = jnp.zeros((rank, features), BF16)
            pack_ref[part, :, model : model + LANES] = blocks[rows, 3 * features :].astype(BF16)
    early_width = early_ref.shape[2]
    for k, out_ref in enumerate(out_refs):
        quarter = lax.rem(position_ref[0] + k, 4)
        out_ref[:, :early_width] = early_ref[quarter]
        out_ref[:, early_width:] = pack_ref[quarter]


def span_call(kernel, name, scalars, arrays, outs, scratch, limit):
    vmem = pl.BlockSpec(memory_space=pltpu.VMEM)
    return pl.pallas_call(
        kernel,
        in_specs=[pl.BlockSpec(memory_space=pltpu.SMEM)] * len(scalars) + [vmem] * len(arrays),
        out_specs=[vmem] * len(outs),
        out_shape=[jax.ShapeDtypeStruct(shape, kind) for shape, kind in outs],
        scratch_shapes=scratch,
        compiler_params=pltpu.CompilerParams(vmem_limit_bytes=limit * MIB),
        name=name,
    )(*scalars, *arrays)


def ffn_kernel(
    place_ref, weight_ref, low_ref, grad_ref, down_ref, *refs, count, strip,
):
    x_refs, hidden_ref, back_refs = refs[:count], refs[count], refs[count + 1 : -2]
    out_low_ref, down_low_ref = refs[-2:]
    share = x_refs[0].shape[0]
    model, hidden_units = weight_ref.shape[0], weight_ref.shape[1] // 2
    rows = jnp.concatenate([ref[...] for ref in x_refs], axis=0)

    def theirs(ref):
        parts = [
            ref[pl.ds(pl.multiple_of(place_ref[i] * share, share), share), :] for i in range(count)
        ]
        return jnp.concatenate(parts, axis=0)

    def send(back, start, width):
        for i, ref in enumerate(back_refs):
            ref[:, start : start + width] = back[i * share : (i + 1) * share].astype(ref.dtype)

    both = dot_low(rows[:, model:], low_ref[...]) + dot_low(rows[:, :model], weight_ref[...])
    gate, up = both[:, :hidden_units], both[:, hidden_units:]
    sig = jax.nn.sigmoid(gate)
    silu = gate * sig
    hidden = (silu * up).astype(BF16)
    hidden_ref[...] = hidden
    grad = theirs(grad_ref)
    grads = jnp.concatenate(
        [
            (grad * up * (sig * (1.0 + gate * (1.0 - sig)))).astype(BF16),
            (grad * silu).astype(BF16),
        ],
        axis=1,
    )
    for start in range(0, model, strip):
        send(dot_low(grads, weight_ref[start : start + strip, :], 1, 1), start, strip)
    send(dot_low(grads, low_ref[...], 1, 1), model, low_ref.shape[0])
    out_low_ref[...] = dot_low(rows[:, model:], grads, 0, 0)[: out_low_ref.shape[0]]
    down_low_ref[...] = dot_low(theirs(down_ref), hidden, 0, 0)[: down_low_ref.shape[0]]


def ffn_rows(chunks, blocks, weights, low, grad_hidden, low_grad_down, rank, kind):
    share, wide = blocks[0].shape
    count = len(blocks)
    hidden_units = grad_hidden.shape[1]
    vmem = pl.BlockSpec(memory_space=pltpu.VMEM)
    return pl.pallas_call(
        functools.partial(ffn_kernel, count=count, strip=512),
        in_specs=[pl.BlockSpec(memory_space=pltpu.SMEM)] + [vmem] * (4 + count),
        out_specs=[vmem] * (3 + count),
        out_shape=[jax.ShapeDtypeStruct((count * share, hidden_units), BF16)]
        + [jax.ShapeDtypeStruct((share, wide), kind)] * count
        + [
            jax.ShapeDtypeStruct((2 * rank, 2 * hidden_units), F32),
            jax.ShapeDtypeStruct((rank, hidden_units), F32),
        ],
        cost_estimate=pl.CostEstimate(
            flops=8 * count * share * wide * hidden_units,
            bytes_accessed=4 * wide * hidden_units,
            transcendentals=count * share * hidden_units,
        ),
        compiler_params=pltpu.CompilerParams(vmem_limit_bytes=14 * MIB),
        name="ffn_rows",
    )(chunks, weights, low, grad_hidden, low_grad_down, *blocks)


def in_place_kernel(place_ref, *refs):
    out_ref = refs[-1]
    for k, block_ref in enumerate(refs[:-1]):

        @pl.when(pl.program_id(0) == k)
        def _():
            out_ref[...] = block_ref[...].astype(out_ref.dtype)


def in_place(place, blocks, width, kind):
    owners, share = len(blocks), blocks[0].shape[0]
    return pl.pallas_call(
        in_place_kernel,
        grid_spec=pltpu.PrefetchScalarGridSpec(
            num_scalar_prefetch=1,
            grid=(owners,),
            in_specs=[pl.BlockSpec((share, width), lambda k, c: (0, 0))] * owners,
            out_specs=pl.BlockSpec((share, width), lambda k, c: (lax.rem(c[0] + k, owners), 0)),
        ),
        out_shape=jax.ShapeDtypeStruct((owners * share, width), kind),
        compiler_params=pltpu.CompilerParams(vmem_limit_bytes=8 * MIB),
        name="in_place",
    )(place, *blocks)


def totals_kernel(
    pick_ref, terms_ref, attn_ref, triple_ref, strength_ref, projection_in_ref,
    projection_out_ref, ffn_in_ref, ffn_out_ref, down_in_ref, down_out_ref, *, cuts,
):
    step = pl.program_id(0)
    sequences, _, rank, width = terms_ref.shape
    adapters = projection_out_ref.shape[0]
    shape = (adapters * rank, sequences * rank)
    to = lax.broadcasted_iota(jnp.int32, shape, 0)
    source = lax.broadcasted_iota(jnp.int32, shape, 1)
    wanted = jnp.full(shape, -1, jnp.int32)
    for sequence in range(sequences):
        wanted = jnp.where(
            (source >= sequence * rank) & (source < (sequence + 1) * rank),
            pick_ref[sequence] * rank + source - sequence * rank,
            wanted,
        )
    select = (to == wanted).astype(BF16)
    terms = terms_ref[:, 0].reshape(sequences * rank, width)

    def add_up(out_ref, start, wide):
        total = dot_low(select, terms[:, start : start + wide])
        out_ref[...] = total[:, : out_ref.shape[-1]].reshape(out_ref.shape)

    model = ffn_in_ref.shape[-1]
    add_up(attn_ref, cuts[2], model)

    @pl.when(step < 3)
    def _():
        add_up(triple_ref, cuts[3], triple_ref.shape[-1])

    @pl.when(step < 2)
    def _():
        add_up(ffn_in_ref, cuts[0], model)
        add_up(ffn_out_ref, cuts[1], ffn_out_ref.shape[-1])

    @pl.when(step == 2)
    def _():
        add_up(down_out_ref, cuts[0], model)
        add_up(down_in_ref, cuts[1], down_in_ref.shape[-1])

    @pl.when(step == 3)
    def _():
        add_up(projection_out_ref, cuts[0], model)
        add_up(projection_in_ref, cuts[1], projection_in_ref.shape[-1])
        strengths = dot_low(terms[:, cuts[3] : cuts[3] + LANES], select, 0, 1)
        for adapter in range(adapters):
            strength_ref[adapter] = strengths[
                : strength_ref.shape[1], adapter * rank : (adapter + 1) * rank
            ]


def totals(picks, terms, cuts, adapters, rank, model, features, hidden_units, heads):
    sequences, quarters, _, width = terms.shape
    part = lambda last, wide: pl.BlockSpec(
        (1, adapters, rank, wide), lambda q, c: (jnp.minimum(q, last), 0, 0, 0)
    )
    one = lambda wide: pl.BlockSpec((adapters, rank, wide), lambda q, c: (0, 0, 0))
    shape = lambda *dims: jax.ShapeDtypeStruct(dims, F32)
    return pl.pallas_call(
        functools.partial(totals_kernel, cuts=cuts),
        grid_spec=pltpu.PrefetchScalarGridSpec(
            num_scalar_prefetch=1,
            grid=(quarters,),
            in_specs=[pl.BlockSpec((sequences, 1, rank, width), lambda q, c: (0, q, 0, 0))],
            out_specs=[
                part(3, model), part(2, features),
                pl.BlockSpec((adapters, heads, rank), lambda q, c: (0, 0, 0)), one(features), one(model),
                part(1, model), part(1, hidden_units), one(hidden_units), one(model),
            ],
        ),
        out_shape=[
            shape(4, adapters, rank, model),
            shape(3, adapters, rank, features),
            shape(adapters, heads, rank),
            shape(adapters, rank, features),
            shape(adapters, rank, model),
            shape(2, adapters, rank, model),
            shape(2, adapters, rank, hidden_units),
            shape(adapters, rank, hidden_units),
            shape(adapters, rank, model),
        ],
        compiler_params=pltpu.CompilerParams(vmem_limit_bytes=56 * MIB),
        name="totals",
    )(picks, terms)


def shifted(block, axis, distance, wrap=True):
    size = lax.axis_size(axis)
    if wrap:
        route = [(i, (i + distance) % size) for i in range(size)]
    else:
        route = [(i, i + distance) for i in range(size) if 0 <= i + distance < size]
    return lax.ppermute(block, axis, route)


def sent_to_owners(parts, axis, order=(2, 1, 3)):
    received = {k: shifted(parts[k], axis, k) for k in order}
    return [parts[0]] + [received[k] for k in sorted(order)]


def blocks_of_others(block, axis):
    return [block] + [shifted(block, axis, -k) for k in (1, 2, 3)]


def blocks_by_ring(block, axis, ahead=None):
    half = block.shape[0] // 2
    before = shifted(block, axis, 1)
    after = shifted(block, axis, -1)
    if ahead is not None:
        before, after, ahead = lax.optimization_barrier((before, after, ahead))
    far = jnp.concatenate(
        [shifted(after[:half], axis, -1), shifted(before[half:], axis, 1)], axis=0
    )
    blocks = [block, after, far, before]
    return blocks if ahead is None else (blocks, ahead)


def paired_sum(block, axis):
    blocks = [part.astype(F32) for part in blocks_of_others(block, axis)]
    half = len(blocks) // 2
    while half:
        blocks = [blocks[i] + blocks[i + half] for i in range(half)]
        half //= 2
    return blocks[0]


def dot(left, right):
    return jnp.dot(left, right, preferred_element_type=F32)


def dot_nt(left, right):
    return lax.dot_general(left, right, (((1,), (1,)), ((), ())), preferred_element_type=F32)


def dot_tn(left, right):
    return lax.dot_general(left, right, (((0,), (0,)), ((), ())), preferred_element_type=F32)


def rms_scale(values, gain):
    return values * lax.rsqrt(jnp.mean(values * values, axis=-1, keepdims=True) + EPSILON) * gain


def rms_back(values, gain, grad):
    scale = lax.rsqrt(jnp.mean(values * values, axis=-1, keepdims=True) + EPSILON)
    gained = gain * grad
    return scale * gained - values * (scale**3) * jnp.mean(values * gained, axis=-1, keepdims=True)


def pad_columns(array, width):
    return jnp.pad(array, ((0, 0), (0, width - array.shape[1])))


def pad_rows(array, height):
    return jnp.pad(array, ((0, height - array.shape[0]), (0, 0)))


def on_device(
    tokens,
    cotangent,
    token_document_ids,
    sequence_adapter_index,
    mixer_norm_gain,
    head_norm_gain,
    feedforward_norm_gain,
    short_filter_kernels,
    query_weight,
    key_weight,
    value_weight,
    strength_weight,
    mixer_output_weight,
    gate_weight,
    up_weight,
    down_weight,
    adapter_attention_input,
    adapter_triple_output,
    adapter_strength_output,
    adapter_projection_input,
    adapter_projection_output,
    adapter_feedforward_input,
    adapter_feedforward_output,
    adapter_down_input,
    adapter_down_output,
):
    span, model = tokens.shape
    head_dim = head_norm_gain.shape[0]
    taps = short_filter_kernels.shape[1]
    heads = strength_weight.shape[1]
    features = heads * head_dim
    hidden_units = gate_weight.shape[1]
    adapters = adapter_attention_input.shape[1]
    rank = adapter_attention_input.shape[3]
    owners = lax.axis_size("tensor")
    place = lax.axis_index("tensor")
    position = lax.axis_index("context")
    share = span // owners
    everyone = ("weights", "context")

    def chunk_at(array, k):
        start = lax.rem(place + k, owners) * share
        return lax.dynamic_slice_in_dim(array, start, share, axis=0)

    mixer_pack = jnp.concatenate(
        [
            query_weight, key_weight, value_weight, strength_weight,
            jnp.full(
                (strength_weight.shape[0], LANES - heads),
                sequence_adapter_index[0].astype(BF16),
            ),
            mixer_output_weight.T,
        ],
        axis=1,
    )
    ffn_pack = jnp.concatenate([gate_weight, up_weight, down_weight.T], axis=1)
    mixer_all = lax.all_gather(mixer_pack, everyone, axis=0, tiled=True)
    ffn_all = lax.all_gather(ffn_pack, everyone, axis=0, tiled=True)
    chosen = sequence_adapter_index[0]
    take = lambda table, axis: lax.dynamic_index_in_dim(table, chosen, axis, keepdims=False)
    attention_in = jnp.swapaxes(take(adapter_attention_input, 1), 1, 2).reshape(4 * rank, model)
    triple_out = take(adapter_triple_output, 1)
    strength_out = take(adapter_strength_output, 0)
    projection_in = jnp.swapaxes(take(adapter_projection_input, 0), 0, 1)
    projection_out = take(adapter_projection_output, 0)
    feedforward_in = jnp.swapaxes(take(adapter_feedforward_input, 1), 1, 2).reshape(2 * rank, model)
    feedforward_out = take(adapter_feedforward_output, 1)
    down_in_ext = pad_rows(jnp.swapaxes(take(adapter_down_input, 0), 0, 1), LANES)
    ffn_low = pad_rows(
        jnp.concatenate(
            [
                pad_columns(feedforward_out[0], 2 * hidden_units),
                jnp.pad(feedforward_out[1], ((0, 0), (hidden_units, 0))),
            ],
            axis=0,
        ),
        LANES,
    )
    down_out = take(adapter_down_output, 0)
    low_in = jnp.concatenate(
        [
            jnp.pad(triple_out[part], ((0, 0), (part * features, (2 - part) * features + LANES)))
            for part in range(3)
        ]
        + [jnp.pad(strength_out, ((0, 0), (3 * features, LANES - heads)))],
        axis=0,
    )

    padded_ids = jnp.concatenate(
        [jnp.full((HALO,), -1, jnp.int32), token_document_ids[0], jnp.full((HALO,), -2, jnp.int32)]
    )
    window = lax.dynamic_slice_in_dim(padded_ids, position * span, span + 2 * HALO)
    window = jnp.where(
        jnp.arange(span + 2 * HALO) < span + HALO, window, jnp.full_like(window, -2)
    )
    seg_column = jnp.broadcast_to(window[:, None], (span + 2 * HALO, LANES))
    seg_rows = window[HALO : HALO + span].reshape(span // CHUNK, CHUNK)
    kernels = jnp.transpose(short_filter_kernels, (1, 0, 2)).reshape(taps, -1)

    edge = shifted(tokens[span - HALO :], "context", 1, wrap=False)
    inputs_ext = jnp.concatenate([edge, tokens], axis=0).astype(F32)
    normed_ext = rms_scale(inputs_ext, mixer_norm_gain).astype(BF16)
    low_ext = dot_nt(normed_ext, attention_in).astype(BF16)
    out_map = pad_rows(projection_out, LANES)
    in_map = pad_rows(feedforward_in, LANES)
    low_grad_down = pad_columns(dot_nt(cotangent, down_out).astype(BF16), LANES)
    ffn_gain = feedforward_norm_gain[None, :]
    projection_in = pad_rows(projection_in, LANES)
    triple = 3 * features + LANES
    weight_in = mixer_all[:, :triple]
    weight_out = mixer_all[:, triple:]
    weight_gate_up = ffn_all[:, : 2 * hidden_units]
    weight_down = ffn_all[:, 2 * hidden_units :]
    picks = mixer_all[:: mixer_all.shape[0] // lax.axis_size("weights"), 3 * features + heads]
    picks = picks.astype(jnp.int32)

    projected = dot(normed_ext, weight_in) + dot(low_ext, low_in)
    normed = normed_ext[HALO:]
    low_attn = low_ext[HALO:]

    where = position[None]
    here = place[None]
    qp, op, offset, linear, *kept = delta_local(
        projected, kernels, seg_column, seg_rows, heads, head_dim, span, heads
    )
    one = shifted(offset, "context", 1, wrap=False)
    linear_two = lax.ppermute(linear, "context", [(2, 3)])
    second = (
        offset.astype(F32)
        + jnp.einsum("hij,hjk->hik", linear, one, preferred_element_type=F32)
    ).astype(BF16)
    out_ext = jnp.concatenate([weight_out, projection_in], axis=0)
    second, out_ext = lax.optimization_barrier((second, out_ext))
    two = lax.ppermute(second, "context", [(1, 2)])
    three = lax.ppermute(second, "context", [(1, 3)])
    gain_row = head_norm_gain[None, :]
    head_low, attended, state, *branch_parts = attend(
        where, here, op, qp, one, two, linear_two, three, gain_row, out_ext, owners
    )
    wide = model + LANES
    branch = sent_to_owners(branch_parts, "tensor")
    linear_one = shifted(linear, "context", -1, wrap=False)
    linear_after = lax.ppermute(linear, "context", [(2, 0)])
    *branch, linear_one, linear_after = lax.optimization_barrier(
        (*branch, linear_one, linear_after)
    )
    middle, packed, low_o = owner_call(
        middle_kernel, "middle_rows", here, share,
        [(part, "rows") for part in branch]
        + [(tokens, "span"), (out_map, "whole"), (ffn_gain, "whole"), (in_map, "whole")],
        [((share, model), F32), ((share, wide), BF16), ((share, LANES), BF16)],
    )
    grad_hidden = dot(cotangent, weight_down) + dot(low_grad_down, down_in_ext)
    ffn_in, grad_hidden = blocks_by_ring(packed, "tensor", grad_hidden)

    back_parts, hidden_parts = [None] * owners, [None] * owners
    ffn_out_terms, down_in_terms = [], []
    for which in ((1, 3), (2, 0)):
        hidden_rows, *backs, out_term, down_term = ffn_rows(
            jnp.stack([lax.rem(place + k, owners) for k in which]), [ffn_in[k] for k in which],
            weight_gate_up, ffn_low, grad_hidden, low_grad_down, rank, BF16,
        )
        for i, k in enumerate(which):
            hidden_parts[k] = hidden_rows[i * share : (i + 1) * share]
            back_parts[k] = backs[i]
        ffn_out_terms.append(out_term)
        down_in_terms.append(down_term)
    back = sent_to_owners(back_parts, "tensor", (1, 3, 2))
    hidden = in_place(here, hidden_parts, hidden_units, BF16)
    down_all = dot_nt(hidden, weight_down).astype(BF16)
    down_low = dot_nt(down_in_ext[:rank], hidden).astype(BF16)
    back, down_all, down_low = lax.optimization_barrier((back, down_all, down_low))
    grad_middle, grad_packed = owner_call(
        functools.partial(back_kernel, rank=rank), "back_rows", here, share,
        [(part, "rows") for part in back]
        + [(cotangent, "span"), (middle, "rows"), (ffn_gain, "whole"), (in_map, "whole"),
           (out_map, "whole"), (low_o, "rows")],
        [((share, model), F32), ((share, wide), BF16)],
    )

    grad_blocks = blocks_by_ring(grad_packed, "tensor")
    low_down = paired_sum(down_low, "tensor").astype(BF16)
    grad_blocks, low_down = lax.optimization_barrier((grad_blocks, low_down))

    grad_attended, own = attend_back(
        here, attended, qp, gain_row, out_ext, grad_blocks, heads, head_dim
    )
    down_all, own = lax.optimization_barrier((down_all, own))
    down_sum = lax.psum_scatter(down_all, "tensor", scatter_dimension=0, tiled=True).astype(F32)
    own_three = shifted(own, "context", -3, wrap=False)
    own_two = shifted(own, "context", -2, wrap=False)
    own_one = shifted(own, "context", -1, wrap=False)
    early_width = model + hidden_units
    (early,) = span_call(
        functools.partial(early_kernel, rank=rank), "early_terms", (here,),
        [*grad_blocks, *ffn_in, head_low, low_down, cotangent, *ffn_out_terms, *down_in_terms],
        [((4, rank, early_width), BF16)], [], 56,
    )
    own_one, own_two, own_three, early = lax.optimization_barrier(
        (own_one, own_two, own_three, early)
    )

    grad_projected, halo, tail = delta_back(
        projected, kernels, seg_column, seg_rows, kept, state, grad_attended,
        (own_one, own_two, own_three, linear_one, linear_after), heads, head_dim, span, heads // 2,
    )
    returned = shifted(halo, "context", -1, wrap=False)
    low_down_own = lax.dynamic_slice_in_dim(low_down, place * share, share, axis=1)
    block_own = (middle + down_sum + dot_tn(low_down_own, down_out)).astype(BF16)
    returned, block_own = lax.optimization_barrier((returned, block_own))
    block_half = share // 2
    block_before = shifted(block_own, "tensor", 1)
    block_after = shifted(block_own, "tensor", -1)
    grad_projected = lax.dynamic_update_slice(
        grad_projected, (tail + returned).astype(BF16), (span - HALO, 0)
    )

    low_part = dot_nt(grad_projected, low_in).astype(BF16)
    low_parts = blocks_of_others(low_part, "tensor")
    grad_rows, _ = lax.optimization_barrier((grad_projected, low_part))
    normed_parts = dot_nt(grad_rows, weight_in).astype(BF16)
    low_parts, normed_parts = lax.optimization_barrier(
        (low_parts, [chunk_at(normed_parts, k) for k in range(owners)])
    )
    late_width = model + features
    low_grad_attn, *quarters = span_call(
        functools.partial(late_kernel, rank=rank), "late_terms", (where,),
        [*low_parts, normed, low_attn, grad_projected, early],
        [((span, 4 * rank), BF16)] + [((rank, early_width + late_width), BF16)] * 4,
        [pltpu.VMEM((4, rank, late_width), BF16)], 24,
    )
    quarters = sent_to_owners(quarters, "context")
    *quarters, block_before, block_after = lax.optimization_barrier(
        (*quarters, block_before, block_after)
    )
    normed_sent = sent_to_owners(normed_parts, "tensor")
    block_far = jnp.concatenate(
        [
            shifted(block_after[:block_half], "tensor", -1),
            shifted(block_before[block_half:], "tensor", 1),
        ],
        axis=0,
    )
    block_out = in_place(here, [block_own, block_after, block_far, block_before], model, BF16)
    *normed_sent, block_out, picks = lax.optimization_barrier((*normed_sent, block_out, picks))
    (grad_tokens,) = owner_call(
        tokens_kernel, "token_rows", here, share,
        [(part, "rows") for part in normed_sent]
        + [(low_grad_attn, "span"), (attention_in, "whole"), (tokens, "span"),
           (mixer_norm_gain[None, :], "whole"), (grad_middle, "rows")],
        [((share, model), BF16)],
    )
    tokens_grad = in_place(here, blocks_by_ring(grad_tokens, "tensor"), model, F32)

    quarter = sum(part.astype(F32) for part in quarters).astype(BF16)
    terms = lax.all_gather(quarter, everyone, axis=0, tiled=False)
    sequences = lax.axis_size("weights")
    terms = terms.reshape(sequences, 4, rank, -1)
    cuts = (0, model, model + hidden_units, 2 * model + hidden_units)
    sums = totals(
        picks, terms, cuts, adapters, rank, model, features, hidden_units, heads
    )
    flip = lambda array: jnp.swapaxes(array, -1, -2)
    return (
        block_out,
        tokens_grad,
        flip(sums[0]),
        sums[1],
        flip(sums[2]),
        flip(sums[3]),
        sums[4],
        flip(sums[5]),
        sums[6],
        flip(sums[7]),
        sums[8],
    )


def solution(mesh):
    rows = P(("weights", "context"), None)
    return jax.shard_map(
        on_device,
        mesh=mesh,
        in_specs=(
            rows,
            rows,
            P("weights", None),
            P("weights"),
            P(),
            P(),
            P(),
            P(None, None, "tensor"),
            P(("weights", "context"), "tensor"),
            P(("weights", "context"), "tensor"),
            P(("weights", "context"), "tensor"),
            P(("weights", "context"), "tensor"),
            P("tensor", ("weights", "context")),
            P(("weights", "context"), "tensor"),
            P(("weights", "context"), "tensor"),
            P("tensor", ("weights", "context")),
            P(),
            P(None, None, None, "tensor"),
            P(None, None, "tensor"),
            P(None, "tensor", None),
            P(),
            P(),
            P(None, None, None, "tensor"),
            P(None, "tensor", None),
            P(),
        ),
        out_specs=(
            rows,
            rows,
            P(),
            P(None, None, None, "tensor"),
            P(None, None, "tensor"),
            P(None, "tensor", None),
            P(),
            P(),
            P(None, None, None, "tensor"),
            P(None, "tensor", None),
            P(),
        ),
        check_vma=False,
    )
```

```python
import functools

import jax
import jax.numpy as jnp
from jax import lax
from jax.experimental import pallas as pl
from jax.experimental.pallas import tpu as pltpu
from jax.sharding import PartitionSpec as P

EPSILON = 1e-06
HALO = 16
CHUNK = 128
LANES = 128
F32 = jnp.float32
BF16 = jnp.bfloat16
MIB = 1024 * 1024


def dot_low(left, right, left_dim=1, right_dim=0):
    return lax.dot_general(
        left.astype(BF16),
        right.astype(BF16),
        (((left_dim,), (right_dim,)), ((), ())),
        preferred_element_type=F32,
    )


def conv_rows(x_ref, columns, taps_ref, seg_ref, span):
    here = seg_ref[HALO : HALO + span, :]
    total = taps_ref[0:1, columns] * x_ref[HALO : HALO + span, columns]
    for tap in range(1, taps_ref.shape[0]):
        same = seg_ref[HALO - tap : HALO - tap + span, :] == here
        total = total + taps_ref[tap : tap + 1, columns] * jnp.where(
            same, x_ref[HALO - tap : HALO - tap + span, columns], 0.0
        )
    return total


def inverse_norm(values):
    return lax.rsqrt(jnp.sum(values * values, axis=-1, keepdims=True) + EPSILON)


def head_column(array, head):
    lane = lax.broadcasted_iota(jnp.int32, array.shape, 1)
    return jnp.sum(jnp.where(lane == head, array, 0.0), axis=1, keepdims=True)


def chunk_masks(seg_ref, row_ref, chunk):
    start = HALO + chunk * CHUNK
    column = seg_ref[start : start + CHUNK, :]
    row = row_ref[chunk : chunk + 1, :]
    before = seg_ref[start - 1 : start, :]
    last = seg_ref[start + CHUNK - 1 : start + CHUNK, :]
    same = column == row
    row_ids = lax.broadcasted_iota(jnp.int32, (CHUNK, CHUNK), 0)
    col_ids = lax.broadcasted_iota(jnp.int32, (CHUNK, CHUNK), 1)
    strict = (same & (row_ids > col_ids)).astype(F32)
    causal = (same & (row_ids >= col_ids)).astype(F32)
    running = (column == before).astype(F32)
    closing = (column == last).astype(F32)
    carried = (before == last).astype(F32)
    return strict, causal, running, closing, carried


def unit_lower_inverses(lowers):
    size = lowers[0].shape[0]
    row_ids = lax.broadcasted_iota(jnp.int32, (size, size), 0)
    col_ids = lax.broadcasted_iota(jnp.int32, (size, size), 1)
    identity = (row_ids == col_ids).astype(F32)
    pair = (row_ids >> 1) == (col_ids >> 1)
    highs = [lower.astype(BF16) for lower in lowers]
    inverses = [identity - jnp.where(pair, lower, 0.0) for lower in lowers]
    bits = 2
    while (1 << bits) <= size:
        joined = ((row_ids >> bits) == (col_ids >> bits)) & (
            (row_ids >> (bits - 1)) != (col_ids >> (bits - 1))
        )
        rounded = [inverse.astype(BF16) for inverse in inverses]
        inner = [
            dot_low(jnp.where(joined, high, jnp.zeros_like(high)), inverse)
            for high, inverse in zip(highs, rounded)
        ]
        inverses = [
            inverse - dot_low(low, part) for inverse, low, part in zip(inverses, rounded, inner)
        ]
        bits += 1
    rounded = [inverse.astype(BF16) for inverse in inverses]
    rests = [(lower - high.astype(F32)).astype(BF16) for lower, high in zip(lowers, highs)]
    residuals = [
        identity - low.astype(F32) - (dot_low(high, low) + dot_low(rest, low))
        for low, high, rest in zip(rounded, highs, rests)
    ]
    return [low.astype(F32) + dot_low(low, part) for low, part in zip(rounded, residuals)]


def delta_local_kernel(
    q_ref, k_ref, v_ref, logit_ref, taps_q, taps_k, taps_v, seg_ref, row_ref,
    qp_ref, op_ref, offset_ref, linear_ref, inverse_ref, prefix_ref, solved_ref, score_ref, zq_ref, zk_ref, zv_ref,
    *, span, head_dim, group,
):
    chunks = span // CHUNK
    step = pl.program_id(0)
    masks = [chunk_masks(seg_ref, row_ref, chunk) for chunk in range(chunks)]
    rates_all = jax.nn.sigmoid(logit_ref[HALO : HALO + span, :])
    work = []
    for local in range(group):
        columns = slice(local * head_dim, (local + 1) * head_dim)
        zq_ref[:, columns] = conv_rows(q_ref, columns, taps_q, seg_ref, span)
        zk_ref[:, columns] = conv_rows(k_ref, columns, taps_k, seg_ref, span)
        zv_ref[:, columns] = conv_rows(v_ref, columns, taps_v, seg_ref, span)
        rates_head = head_column(rates_all, step * group + local)
        for chunk in range(chunks):
            rows = slice(chunk * CHUNK, (chunk + 1) * CHUNK)
            queries = jax.nn.silu(zq_ref[rows, columns])
            queries = (queries * (inverse_norm(queries) * head_dim**-0.5)).astype(BF16)
            keys = jax.nn.silu(zk_ref[rows, columns])
            keys = (keys * inverse_norm(keys)).astype(BF16)
            values = jax.nn.silu(zv_ref[rows, columns]).astype(BF16)
            work.append((local, chunk, queries, keys, values, rates_head[rows]))
    lowers = [
        dot_low(keys, keys, 1, 1) * (rates * masks[chunk][0])
        for _, chunk, _, keys, _, rates in work
    ]
    inverses = unit_lower_inverses(lowers)
    parts = []
    for (local, chunk, queries, keys, values, rates), inverse in zip(work, inverses):
        rows = slice(chunk * CHUNK, (chunk + 1) * CHUNK)
        strict, causal, running, closing, carried = masks[chunk]
        inverse = inverse.astype(BF16)
        inverse_ref[local, rows, :] = inverse
        right = jnp.concatenate([rates * values.astype(F32), rates * keys.astype(F32)], axis=1)
        solved = dot_low(inverse, right)
        solved_ref[local, rows, :] = solved.astype(BF16)
        updates = solved[:, :head_dim]
        weighted = running * solved[:, head_dim:]
        both = jnp.concatenate([updates, weighted], axis=1).astype(BF16)
        scores = (dot_low(queries, keys, 1, 1) * causal).astype(BF16)
        score_ref[local, rows, :] = scores
        near = dot_low(scores, both)
        ends = dot_low(closing * keys.astype(F32), both, 0, 0)
        reach = running * queries.astype(F32) - near[:, head_dim:]
        parts.append((near[:, :head_dim], reach.astype(BF16), ends))
    row_ids = lax.broadcasted_iota(jnp.int32, (head_dim, head_dim), 0)
    col_ids = lax.broadcasted_iota(jnp.int32, (head_dim, head_dim), 1)
    identity = (row_ids == col_ids).astype(F32)
    start = jnp.concatenate([jnp.zeros((head_dim, head_dim), F32), identity], axis=1)
    prefixes = [start] * group
    for chunk in range(chunks):
        rows = slice(chunk * CHUNK, (chunk + 1) * CHUNK)
        carried = masks[chunk][4]
        for local in range(group):
            columns = slice(local * head_dim, (local + 1) * head_dim)
            near, reach, ends = parts[local * chunks + chunk]
            prefix = prefixes[local]
            prefix_ref[local, chunk * head_dim : (chunk + 1) * head_dim, :] = prefix.astype(BF16)
            seen = dot_low(reach, prefix)
            op_ref[rows, columns] = near + seen[:, :head_dim]
            qp_ref[rows, columns] = seen[:, head_dim:].astype(BF16)
            moved = jnp.concatenate([carried, carried], axis=1) * prefix - dot_low(
                ends[:, head_dim:], prefix
            )
            prefixes[local] = jnp.concatenate(
                [moved[:, :head_dim] + ends[:, :head_dim], moved[:, head_dim:]], axis=1
            )
    for local in range(group):
        offset_ref[local] = prefixes[local][:, :head_dim].astype(BF16)
        linear_ref[local] = prefixes[local][:, head_dim:].astype(BF16)


def delta_local(projected, taps, seg_column, seg_rows, heads, head_dim, span, group):
    rows = projected.shape[0]
    width = group * head_dim
    steps = heads // group
    third = lambda part: pl.BlockSpec((rows, width), lambda i: (0, part * steps + i))
    tap_third = lambda part: pl.BlockSpec((taps.shape[0], width), lambda i: (0, part * steps + i))
    whole = lambda array: pl.BlockSpec(array.shape, lambda i: (0,) * array.ndim)
    by_head = lambda *shape: pl.BlockSpec((group,) + shape, lambda i: (i, 0, 0))
    columns = pl.BlockSpec((span, width), lambda i: (0, i))
    chunks = span // CHUNK
    kept = lambda *shape, kind=BF16: jax.ShapeDtypeStruct(shape, kind)
    return pl.pallas_call(
        functools.partial(delta_local_kernel, span=span, head_dim=head_dim, group=group),
        grid=(steps,),
        in_specs=[
            third(0), third(1), third(2),
            pl.BlockSpec((rows, LANES), lambda i: (0, 3 * heads * head_dim // LANES)),
            tap_third(0), tap_third(1), tap_third(2), whole(seg_column), whole(seg_rows),
        ],
        out_specs=[
            columns, columns, by_head(head_dim, head_dim), by_head(head_dim, head_dim),
            by_head(span, CHUNK),
            by_head(chunks * head_dim, 2 * head_dim), by_head(span, 2 * head_dim),
            by_head(span, CHUNK), columns, columns, columns,
        ],
        out_shape=[
            kept(span, heads * head_dim),
            kept(span, heads * head_dim, kind=F32),
            kept(heads, head_dim, head_dim),
            kept(heads, head_dim, head_dim),
            kept(heads, span, CHUNK),
            kept(heads, chunks * head_dim, 2 * head_dim),
            kept(heads, span, 2 * head_dim),
            kept(heads, span, CHUNK),
            kept(span, heads * head_dim, kind=F32),
            kept(span, heads * head_dim, kind=F32),
            kept(span, heads * head_dim, kind=F32),
        ],
        compiler_params=pltpu.CompilerParams(vmem_limit_bytes=22 * MIB),
        name="delta_local",
    )(projected, projected, projected, projected, taps, taps, taps, seg_column, seg_rows)


def attend_kernel(
    position_ref, place_ref, op_ref, qp_ref, one_ref, two_ref, map_ref, three_ref, gain_ref, weight_ref,
    state_ref, *refs,
):
    *part_refs, out_ref = refs
    heads, head_dim = one_ref.shape[0], one_ref.shape[1]
    owners = len(part_refs)
    share = out_ref.shape[0] // owners
    for head in range(heads):
        columns = slice(head * head_dim, (head + 1) * head_dim)
        through = one_ref[head].astype(F32) + dot_low(map_ref[head], three_ref[head])
        state = jnp.where(position_ref[0] == 2, two_ref[head].astype(F32), through)
        state_ref[head] = state.astype(BF16)
        attended = op_ref[:, columns] + dot_low(qp_ref[:, columns], state_ref[head])
        scale = lax.rsqrt(jnp.mean(attended * attended, axis=-1, keepdims=True) + EPSILON)
        out_ref[:, columns] = (attended * scale * gain_ref[...]).astype(BF16)
    for k, part_ref in enumerate(part_refs):
        start = lax.rem(place_ref[0] + k, owners) * share
        rows = out_ref[pl.ds(pl.multiple_of(start, share), share), :]
        part_ref[...] = dot_low(rows, weight_ref[...], 1, 1).astype(BF16)


def attend(position, place, op, qp, one, two, mapped, three, gain, weight, owners):
    vmem = pl.BlockSpec(memory_space=pltpu.VMEM)
    smem = pl.BlockSpec(memory_space=pltpu.SMEM)
    part = jax.ShapeDtypeStruct((op.shape[0] // owners, weight.shape[0]), BF16)
    return pl.pallas_call(
        attend_kernel,
        in_specs=[smem] * 2 + [vmem] * 8,
        out_specs=[vmem] * (1 + owners),
        out_shape=[jax.ShapeDtypeStruct(one.shape, BF16)] + [part] * owners,
        scratch_shapes=[pltpu.VMEM(op.shape, BF16)],
        compiler_params=pltpu.CompilerParams(vmem_limit_bytes=14 * MIB),
        name="attend",
    )(position, place, op, qp, one, two, mapped, three, gain, weight)


def attend_back_kernel(
    place_ref, op_ref, qp_ref, state_ref, gain_ref, weight_ref, *refs
):
    *block_refs, out_ref, own_ref, low_ref, grad_ref, head_ref = refs
    heads, head_dim = own_ref.shape[0], own_ref.shape[1]
    owners = len(block_refs)
    share = out_ref.shape[0] // owners
    for k, block_ref in enumerate(block_refs):
        start = lax.rem(place_ref[0] + k, owners) * share
        grad_ref[pl.ds(pl.multiple_of(start, share), share), :] = dot_low(
            block_ref[...], weight_ref[...]
        )
    for head in range(heads):
        columns = slice(head * head_dim, (head + 1) * head_dim)
        attended = op_ref[:, columns] + dot_low(qp_ref[:, columns], state_ref[head])
        scale = lax.rsqrt(jnp.mean(attended * attended, axis=-1, keepdims=True) + EPSILON)
        head_ref[:, columns] = (attended * scale * gain_ref[...]).astype(BF16)
        gained = grad_ref[:, columns] * gain_ref[...]
        along = jnp.mean(attended * gained, axis=-1, keepdims=True)
        grad = (scale * gained - attended * (scale * scale * scale * along)).astype(BF16)
        out_ref[:, columns] = grad
        own_ref[head] = dot_low(qp_ref[:, columns], grad, 0, 0).astype(BF16)
    total = 0.0
    for k, block_ref in enumerate(block_refs):
        start = lax.rem(place_ref[0] + k, owners) * share
        rows = head_ref[pl.ds(pl.multiple_of(start, share), share), :]
        total = total + dot_low(block_ref[:, block_ref.shape[1] - LANES :], rows, 0, 0)
    low_ref[...] = total[: low_ref.shape[0]]


def attend_back(place, op, qp, state, gain, weight, blocks, rank):
    vmem = pl.BlockSpec(memory_space=pltpu.VMEM)
    return pl.pallas_call(
        attend_back_kernel,
        in_specs=[pl.BlockSpec(memory_space=pltpu.SMEM)] + [vmem] * (5 + len(blocks)),
        out_specs=[vmem] * 3,
        out_shape=[
            jax.ShapeDtypeStruct(op.shape, BF16),
            jax.ShapeDtypeStruct(state.shape, BF16),
            jax.ShapeDtypeStruct((rank, op.shape[1]), F32),
        ],
        scratch_shapes=[pltpu.VMEM(op.shape, F32), pltpu.VMEM(op.shape, BF16)],
        compiler_params=pltpu.CompilerParams(vmem_limit_bytes=14 * MIB),
        name="attend_back",
    )(place, op, qp, state, gain, weight, *blocks)


def delta_back_kernel(
    zq_ref, zk_ref, zv_ref, logit_ref, taps_q, taps_k, taps_v, seg_ref, row_ref,
    inverse_ref, prefix_ref, solved_ref, score_ref, state_ref, grad_ref,
    one_ref, two_ref, three_ref, map_one_ref, map_two_ref,
    out_ref, halo_ref, tail_ref, dz_ref, *, span, heads, head_dim, group,
):
    chunks = span // CHUNK
    step = pl.program_id(0)
    features = heads * head_dim
    masks = [chunk_masks(seg_ref, row_ref, chunk) for chunk in range(chunks)]
    rates_all = jax.nn.sigmoid(logit_ref[HALO : HALO + span, :])
    lane = lax.broadcasted_iota(jnp.int32, (CHUNK, LANES), 1)

    @pl.when(step == 0)
    def _():
        out_ref[:, 3 * features :] = jnp.zeros((span, LANES), BF16)
        for slot in range(3 * group):
            dz_ref[slot, 0:HALO, :] = jnp.zeros((HALO, head_dim), F32)
            dz_ref[slot, HALO + span :, :] = jnp.zeros((HALO, head_dim), F32)

    kept, leavings = [], []
    for local in range(group):
        columns = slice(local * head_dim, (local + 1) * head_dim)
        rates_head = head_column(rates_all, step * group + local)
        entry = state_ref[local]
        through = two_ref[local].astype(F32) + dot_low(
            map_two_ref[local], three_ref[local], 0, 0
        )
        leavings.append(one_ref[local].astype(F32) + dot_low(map_one_ref[local], through, 0, 0))
        for chunk in range(chunks):
            rows = slice(chunk * CHUNK, (chunk + 1) * CHUNK)
            strict, causal, running, closing, carried = masks[chunk]
            queries = jax.nn.silu(zq_ref[rows, columns])
            scale_q = inverse_norm(queries)
            queries = queries * scale_q
            keys = jax.nn.silu(zk_ref[rows, columns])
            scale_k = inverse_norm(keys)
            keys = keys * scale_k
            low_q = (queries * head_dim**-0.5).astype(BF16)
            low_k = keys.astype(BF16)
            values = jax.nn.silu(zv_ref[rows, columns])
            solved = solved_ref[local, rows, :].astype(F32)
            weighted = (running * solved[:, head_dim:]).astype(BF16)
            prefix = prefix_ref[local, chunk * head_dim : (chunk + 1) * head_dim, :]
            state = (
                prefix[:, :head_dim].astype(F32) + dot_low(prefix[:, head_dim:], entry)
            ).astype(BF16)
            errors = (solved[:, :head_dim] - dot_low(weighted, state)).astype(BF16)
            scores = score_ref[local, rows, :]
            grad = grad_ref[rows, columns]
            near = dot_low(scores, grad, 0, 0)
            far = dot_low(running * low_q.astype(F32), grad, 0, 0)
            grad_scores = (dot_low(grad, errors, 1, 1) * causal).astype(BF16)
            kept.append((queries, scale_q, keys, scale_k, low_q, low_k, values,
                         rates_head[rows], weighted, state, errors, near, far, grad_scores))
    grad_errors_all = [None] * (group * chunks)
    leaving_all = [None] * (group * chunks)
    for chunk in reversed(range(chunks)):
        strict, causal, running, closing, carried = masks[chunk]
        for local in range(group):
            item = local * chunks + chunk
            low_k, weighted, near, far = (kept[item][i] for i in (5, 8, 11, 12))
            leaving = leavings[local]
            low_leaving = leaving.astype(BF16)
            leaving_all[item] = low_leaving
            grad_errors = near + closing * dot_low(low_k, low_leaving)
            grad_errors_all[item] = grad_errors.astype(BF16)
            leavings[local] = (
                carried * leaving + far - dot_low(weighted, grad_errors_all[item], 0, 0)
            )
    for local in range(group):
        columns = slice(local * head_dim, (local + 1) * head_dim)
        head = step * group + local
        for chunk in range(chunks):
            rows = slice(chunk * CHUNK, (chunk + 1) * CHUNK)
            inner = slice(HALO + chunk * CHUNK, HALO + (chunk + 1) * CHUNK)
            strict, causal, running, closing, carried = masks[chunk]
            item = local * chunks + chunk
            (queries, scale_q, keys, scale_k, low_q, low_k, values, rates, weighted, state,
             errors, near, far, grad_scores) = kept[item]
            grad_errors, leaving = grad_errors_all[item], leaving_all[item]
            grad = grad_ref[rows, columns]
            grad_queries = running * dot_low(grad, state, 1, 1) + dot_low(grad_scores, low_k)
            grad_keys = dot_low(grad_scores, low_q, 0, 0) + closing * dot_low(
                errors, leaving, 1, 1
            )
            grad_weighted = -running * dot_low(grad_errors, state, 1, 1)
            grad_right = dot_low(
                inverse_ref[local, rows, :],
                jnp.concatenate([grad_errors, grad_weighted.astype(BF16)], axis=1), 0, 0,
            )
            right_v, right_k = grad_right[:, :head_dim], grad_right[:, head_dim:]
            grad_lower = -dot_low(grad_right, solved_ref[local, rows, :], 1, 1) * strict
            gram = dot_low(low_k, low_k, 1, 1)
            grad_rates = jnp.sum(
                right_v * values + right_k * keys + grad_lower * gram, axis=1, keepdims=True
            )
            grad_gram = (rates * grad_lower).astype(BF16)
            grad_keys = (
                grad_keys
                + rates * right_k
                + dot_low(grad_gram, low_k)
                + dot_low(grad_gram, low_k, 0, 0)
            )
            grad_logit = grad_rates * rates * (1.0 - rates)
            previous = out_ref[rows, 3 * features :].astype(F32)
            out_ref[rows, 3 * features :] = jnp.where(lane == head, grad_logit, previous).astype(BF16)
            grad_queries = grad_queries * head_dim**-0.5
            grad_queries = scale_q * (
                grad_queries - queries * jnp.sum(queries * grad_queries, axis=-1, keepdims=True)
            )
            grad_keys = scale_k * (
                grad_keys - keys * jnp.sum(keys * grad_keys, axis=-1, keepdims=True)
            )
            for part, (z_ref, grad_part) in enumerate(
                ((zq_ref, grad_queries), (zk_ref, grad_keys), (zv_ref, rates * right_v))
            ):
                conv = z_ref[rows, columns]
                sig = jax.nn.sigmoid(conv)
                dz_ref[local * 3 + part, inner, :] = grad_part * (
                    sig * (1.0 + conv * (1.0 - sig))
                )
        here = seg_ref[0 : HALO + span, :]
        for part, taps in enumerate((taps_q, taps_k, taps_v)):
            slot = local * 3 + part
            total = taps[0:1, columns] * dz_ref[slot, 0 : HALO + span, :]
            for tap in range(1, taps.shape[0]):
                same = seg_ref[tap : tap + HALO + span, :] == here
                total = total + taps[tap : tap + 1, columns] * jnp.where(
                    same, dz_ref[slot, tap : tap + HALO + span, :], 0.0
                )
            place = pl.ds(pl.multiple_of(part * features + head * head_dim, LANES), head_dim)
            halo_ref[:, place] = total[:HALO]
            tail_ref[:, place] = total[span:]
            out_ref[:, place] = total[HALO:].astype(BF16)


def delta_back(
    projected, taps, seg_column, seg_rows, kept, state, grad, arrived, heads, head_dim, span, group,
):
    inverse, prefix, solved, scores, conv_q, conv_k, conv_v = kept
    rows = projected.shape[0]
    width = group * head_dim
    steps = heads // group
    columns = pl.BlockSpec((span, width), lambda i: (0, i))
    tap_third = lambda part: pl.BlockSpec((taps.shape[0], width), lambda i: (0, part * steps + i))
    whole = lambda array: pl.BlockSpec(array.shape, lambda i: (0,) * array.ndim)
    by_head = lambda array: pl.BlockSpec((group,) + array.shape[1:], lambda i: (i, 0, 0))
    total = 3 * heads * head_dim
    return pl.pallas_call(
        functools.partial(
            delta_back_kernel, span=span, heads=heads, head_dim=head_dim, group=group
        ),
        grid=(steps,),
        in_specs=[
            columns, columns, columns,
            pl.BlockSpec((rows, LANES), lambda i: (0, total // LANES)),
            tap_third(0), tap_third(1), tap_third(2), whole(seg_column), whole(seg_rows),
            by_head(inverse), by_head(prefix), by_head(solved), by_head(scores), by_head(state),
            columns, *[by_head(array) for array in arrived],
        ],
        out_specs=[
            pl.BlockSpec((span, total + LANES), lambda i: (0, 0)),
            pl.BlockSpec((HALO, total), lambda i: (0, 0)),
            pl.BlockSpec((HALO, total), lambda i: (0, 0)),
        ],
        out_shape=[
            jax.ShapeDtypeStruct((span, total + LANES), BF16),
            jax.ShapeDtypeStruct((HALO, total), F32),
            jax.ShapeDtypeStruct((HALO, total), F32),
        ],
        scratch_shapes=[pltpu.VMEM((3 * group, span + 2 * HALO, head_dim), F32)],
        compiler_params=pltpu.CompilerParams(vmem_limit_bytes=56 * MIB),
        name="delta_back",
    )(
        conv_q, conv_k, conv_v, projected, taps, taps, taps, seg_column, seg_rows,
        inverse, prefix, solved, scores, state, grad, *arrived,
    )


def normed_grad(values, gain, grad):
    scale = lax.rsqrt(jnp.mean(values * values, axis=-1, keepdims=True) + EPSILON)
    gained = gain * grad
    along = jnp.mean(values * gained, axis=-1, keepdims=True)
    return scale * gained - values * (scale * scale * scale * along)


def added(refs, columns):
    total = refs[0][:, columns].astype(F32)
    for ref in refs[1:]:
        total = total + ref[:, columns].astype(F32)
    return total


def middle_kernel(
    place_ref, own_ref, one_ref, two_ref, three_ref, tokens_ref, out_map_ref, gain_ref, in_map_ref,
    middle_ref, packed_ref, low_ref,
):
    model = tokens_ref.shape[1]
    refs = (own_ref, one_ref, two_ref, three_ref)
    low = added(refs, slice(model, model + LANES)).astype(BF16)
    low_ref[...] = low
    middle = (
        tokens_ref[...].astype(F32)
        + added(refs, slice(0, model))
        + dot_low(low, out_map_ref[...])
    )
    middle_ref[...] = middle
    scale = lax.rsqrt(jnp.mean(middle * middle, axis=-1, keepdims=True) + EPSILON)
    normed = (middle * scale * gain_ref[...]).astype(BF16)
    packed_ref[:, :model] = normed
    packed_ref[:, model:] = dot_low(normed, in_map_ref[...], 1, 1).astype(BF16)


def back_kernel(
    place_ref, own_ref, one_ref, two_ref, three_ref, cot_ref, middle_in, gain_ref, in_map_ref,
    out_map_ref, low_ref, grad_ref, packed_ref, *, rank,
):
    model = cot_ref.shape[1]
    refs = (own_ref, one_ref, two_ref, three_ref)
    low_ffn = added(refs, slice(model, model + LANES)).astype(BF16)
    grad = added(refs, slice(0, model)) + dot_low(low_ffn, in_map_ref[...])
    grad = cot_ref[...].astype(F32) + normed_grad(middle_in[...], gain_ref[...], grad)
    grad_ref[...] = grad
    rounded = grad.astype(BF16)
    packed_ref[:, :model] = rounded
    low_out = dot_low(rounded, out_map_ref[...], 1, 1).astype(BF16).astype(F32)
    packed_ref[:, model:] = (
        low_out
        + pltpu.roll(low_ref[...].astype(F32), rank, 1)
        + pltpu.roll(low_ffn.astype(F32), 2 * rank, 1)
    ).astype(BF16)


def tokens_kernel(
    place_ref, own_ref, one_ref, two_ref, three_ref, low_ref, in_map_ref, tokens_ref, gain_ref,
    grad_ref, out_ref,
):
    refs = (own_ref, one_ref, two_ref, three_ref)
    grad = added(refs, slice(None)) + dot_low(low_ref[...], in_map_ref[...])
    out_ref[...] = (
        grad_ref[...] + normed_grad(tokens_ref[...].astype(F32), gain_ref[...], grad)
    ).astype(BF16)


def owner_call(kernel, name, place, share, arrays, outs, strips=2):
    strip = share // strips

    def spec(array, mark):
        if mark == "rows":
            return pl.BlockSpec((strip, array.shape[1]), lambda i, c: (i, 0))
        if mark == "span":
            return pl.BlockSpec((strip, array.shape[1]), lambda i, c: (c[0] * strips + i, 0))
        return pl.BlockSpec(array.shape, lambda i, c: (0, 0))

    return pl.pallas_call(
        kernel,
        grid_spec=pltpu.PrefetchScalarGridSpec(
            num_scalar_prefetch=1,
            grid=(strips,),
            in_specs=[spec(array, mark) for array, mark in arrays],
            out_specs=[pl.BlockSpec((strip, shape[1]), lambda i, c: (i, 0)) for shape, _ in outs],
        ),
        out_shape=[jax.ShapeDtypeStruct(shape, kind) for shape, kind in outs],
        compiler_params=pltpu.CompilerParams(vmem_limit_bytes=56 * MIB),
        name=name,
    )(place, *[array for array, _ in arrays])


def early_kernel(
    g0, g1, g2, g3, x0, x1, x2, x3, heads_ref, low_down_ref, cot_ref,
    out_one, out_two, down_one, down_two, pack_ref, *, rank,
):
    model = cot_ref.shape[1]
    hidden_units = down_one.shape[1]
    through_g, through_x = 0.0, 0.0
    for g_ref, x_ref in zip((g0, g1, g2, g3), (x0, x1, x2, x3)):
        low = g_ref[:, model:]
        through_g = through_g + dot_low(low, g_ref[:, :model], 0, 0)
        through_x = through_x + dot_low(low, x_ref[:, :model], 0, 0)
    out_terms = out_one[...] + out_two[...]
    pack_ref[0, :, :model] = through_x[2 * rank : 3 * rank].astype(BF16)
    pack_ref[0, :, model:] = out_terms[:rank, :hidden_units].astype(BF16)
    pack_ref[1, :, :model] = through_x[3 * rank : 4 * rank].astype(BF16)
    pack_ref[1, :, model:] = out_terms[rank:, hidden_units:].astype(BF16)
    pack_ref[2, :, :model] = dot_low(low_down_ref[...], cot_ref[...]).astype(BF16)
    pack_ref[2, :, model:] = (down_one[...] + down_two[...]).astype(BF16)
    pack_ref[3, :, :model] = through_g[rank : 2 * rank].astype(BF16)
    pack_ref[3, :, model:] = jnp.zeros((rank, hidden_units), BF16)
    pack_ref[3, :, model : model + heads_ref.shape[1]] = heads_ref[...].astype(BF16)


def late_kernel(
    position_ref, p0, p1, p2, p3, normed_ref, low_ref, grad_ref, early_ref, low_out_ref, *refs, rank
):
    *out_refs, pack_ref = refs
    model = normed_ref.shape[1]
    features = (grad_ref.shape[1] - LANES) // 3
    total = (p0[...].astype(F32) + p2[...].astype(F32)) + (
        p1[...].astype(F32) + p3[...].astype(F32)
    )
    low_grad = total.astype(BF16)
    low_out_ref[...] = low_grad
    items = dot_low(low_grad, normed_ref[HALO:, :], 0, 0)
    blocks = dot_low(low_ref[HALO:, :], grad_ref[...], 0, 0)
    for part in range(4):
        rows = slice(part * rank, (part + 1) * rank)
        pack_ref[part, :, :model] = items[rows].astype(BF16)
        if part < 3:
            pack_ref[part, :, model:] = blocks[rows, part * features : (part + 1) * features].astype(BF16)
        else:
            pack_ref[part, :, model:] = jnp.zeros((rank, features), BF16)
            pack_ref[part, :, model : model + LANES] = blocks[rows, 3 * features :].astype(BF16)
    early_width = early_ref.shape[2]
    for k, out_ref in enumerate(out_refs):
        quarter = lax.rem(position_ref[0] + k, 4)
        out_ref[:, :early_width] = early_ref[quarter]
        out_ref[:, early_width:] = pack_ref[quarter]


def span_call(kernel, name, scalars, arrays, outs, scratch, limit):
    vmem = pl.BlockSpec(memory_space=pltpu.VMEM)
    return pl.pallas_call(
        kernel,
        in_specs=[pl.BlockSpec(memory_space=pltpu.SMEM)] * len(scalars) + [vmem] * len(arrays),
        out_specs=[vmem] * len(outs),
        out_shape=[jax.ShapeDtypeStruct(shape, kind) for shape, kind in outs],
        scratch_shapes=scratch,
        compiler_params=pltpu.CompilerParams(vmem_limit_bytes=limit * MIB),
        name=name,
    )(*scalars, *arrays)


def ffn_kernel(
    place_ref, weight_ref, low_ref, grad_ref, down_ref, *refs, count, strip,
):
    x_refs, hidden_ref, back_refs = refs[:count], refs[count], refs[count + 1 : -2]
    out_low_ref, down_low_ref = refs[-2:]
    share = x_refs[0].shape[0]
    model, hidden_units = weight_ref.shape[0], weight_ref.shape[1] // 2
    rows = jnp.concatenate([ref[...] for ref in x_refs], axis=0)

    def theirs(ref):
        parts = [
            ref[pl.ds(pl.multiple_of(place_ref[i] * share, share), share), :] for i in range(count)
        ]
        return jnp.concatenate(parts, axis=0)

    def send(back, start, width):
        for i, ref in enumerate(back_refs):
            ref[:, start : start + width] = back[i * share : (i + 1) * share].astype(ref.dtype)

    both = dot_low(rows[:, model:], low_ref[...]) + dot_low(rows[:, :model], weight_ref[...])
    gate, up = both[:, :hidden_units], both[:, hidden_units:]
    sig = jax.nn.sigmoid(gate)
    silu = gate * sig
    hidden = (silu * up).astype(BF16)
    hidden_ref[...] = hidden
    grad = theirs(grad_ref)
    grads = jnp.concatenate(
        [
            (grad * up * (sig * (1.0 + gate * (1.0 - sig)))).astype(BF16),
            (grad * silu).astype(BF16),
        ],
        axis=1,
    )
    for start in range(0, model, strip):
        send(dot_low(grads, weight_ref[start : start + strip, :], 1, 1), start, strip)
    send(dot_low(grads, low_ref[...], 1, 1), model, low_ref.shape[0])
    out_low_ref[...] = dot_low(rows[:, model:], grads, 0, 0)[: out_low_ref.shape[0]]
    down_low_ref[...] = dot_low(theirs(down_ref), hidden, 0, 0)[: down_low_ref.shape[0]]


def ffn_rows(chunks, blocks, weights, low, grad_hidden, low_grad_down, rank, kind):
    share, wide = blocks[0].shape
    count = len(blocks)
    hidden_units = grad_hidden.shape[1]
    vmem = pl.BlockSpec(memory_space=pltpu.VMEM)
    return pl.pallas_call(
        functools.partial(ffn_kernel, count=count, strip=512),
        in_specs=[pl.BlockSpec(memory_space=pltpu.SMEM)] + [vmem] * (4 + count),
        out_specs=[vmem] * (3 + count),
        out_shape=[jax.ShapeDtypeStruct((count * share, hidden_units), BF16)]
        + [jax.ShapeDtypeStruct((share, wide), kind)] * count
        + [
            jax.ShapeDtypeStruct((2 * rank, 2 * hidden_units), F32),
            jax.ShapeDtypeStruct((rank, hidden_units), F32),
        ],
        cost_estimate=pl.CostEstimate(
            flops=8 * count * share * wide * hidden_units,
            bytes_accessed=4 * wide * hidden_units,
            transcendentals=count * share * hidden_units,
        ),
        compiler_params=pltpu.CompilerParams(vmem_limit_bytes=14 * MIB),
        name="ffn_rows",
    )(chunks, weights, low, grad_hidden, low_grad_down, *blocks)


def in_place_kernel(place_ref, *refs):
    out_ref = refs[-1]
    for k, block_ref in enumerate(refs[:-1]):

        @pl.when(pl.program_id(0) == k)
        def _():
            out_ref[...] = block_ref[...].astype(out_ref.dtype)


def in_place(place, blocks, width, kind):
    owners, share = len(blocks), blocks[0].shape[0]
    return pl.pallas_call(
        in_place_kernel,
        grid_spec=pltpu.PrefetchScalarGridSpec(
            num_scalar_prefetch=1,
            grid=(owners,),
            in_specs=[pl.BlockSpec((share, width), lambda k, c: (0, 0))] * owners,
            out_specs=pl.BlockSpec((share, width), lambda k, c: (lax.rem(c[0] + k, owners), 0)),
        ),
        out_shape=jax.ShapeDtypeStruct((owners * share, width), kind),
        compiler_params=pltpu.CompilerParams(vmem_limit_bytes=8 * MIB),
        name="in_place",
    )(place, *blocks)


def totals_kernel(
    pick_ref, terms_ref, attn_ref, triple_ref, strength_ref, projection_in_ref,
    projection_out_ref, ffn_in_ref, ffn_out_ref, down_in_ref, down_out_ref, *, cuts,
):
    step = pl.program_id(0)
    sequences, _, rank, width = terms_ref.shape
    adapters = projection_out_ref.shape[0]
    shape = (adapters * rank, sequences * rank)
    to = lax.broadcasted_iota(jnp.int32, shape, 0)
    source = lax.broadcasted_iota(jnp.int32, shape, 1)
    wanted = jnp.full(shape, -1, jnp.int32)
    for sequence in range(sequences):
        wanted = jnp.where(
            (source >= sequence * rank) & (source < (sequence + 1) * rank),
            pick_ref[sequence] * rank + source - sequence * rank,
            wanted,
        )
    select = (to == wanted).astype(BF16)
    terms = terms_ref[:, 0].reshape(sequences * rank, width)

    def add_up(out_ref, start, wide):
        total = dot_low(select, terms[:, start : start + wide])
        out_ref[...] = total[:, : out_ref.shape[-1]].reshape(out_ref.shape)

    model = ffn_in_ref.shape[-1]
    add_up(attn_ref, cuts[2], model)

    @pl.when(step < 3)
    def _():
        add_up(triple_ref, cuts[3], triple_ref.shape[-1])

    @pl.when(step < 2)
    def _():
        add_up(ffn_in_ref, cuts[0], model)
        add_up(ffn_out_ref, cuts[1], ffn_out_ref.shape[-1])

    @pl.when(step == 2)
    def _():
        add_up(down_out_ref, cuts[0], model)
        add_up(down_in_ref, cuts[1], down_in_ref.shape[-1])

    @pl.when(step == 3)
    def _():
        add_up(projection_out_ref, cuts[0], model)
        add_up(projection_in_ref, cuts[1], projection_in_ref.shape[-1])
        strengths = dot_low(terms[:, cuts[3] : cuts[3] + LANES], select, 0, 1)
        for adapter in range(adapters):
            strength_ref[adapter] = strengths[
                : strength_ref.shape[1], adapter * rank : (adapter + 1) * rank
            ]


def totals(picks, terms, cuts, adapters, rank, model, features, hidden_units, heads):
    sequences, quarters, _, width = terms.shape
    part = lambda last, wide: pl.BlockSpec(
        (1, adapters, rank, wide), lambda q, c: (jnp.minimum(q, last), 0, 0, 0)
    )
    one = lambda wide: pl.BlockSpec((adapters, rank, wide), lambda q, c: (0, 0, 0))
    shape = lambda *dims: jax.ShapeDtypeStruct(dims, F32)
    return pl.pallas_call(
        functools.partial(totals_kernel, cuts=cuts),
        grid_spec=pltpu.PrefetchScalarGridSpec(
            num_scalar_prefetch=1,
            grid=(quarters,),
            in_specs=[pl.BlockSpec((sequences, 1, rank, width), lambda q, c: (0, q, 0, 0))],
            out_specs=[
                part(3, model), part(2, features),
                pl.BlockSpec((adapters, heads, rank), lambda q, c: (0, 0, 0)), one(features), one(model),
                part(1, model), part(1, hidden_units), one(hidden_units), one(model),
            ],
        ),
        out_shape=[
            shape(4, adapters, rank, model),
            shape(3, adapters, rank, features),
            shape(adapters, heads, rank),
            shape(adapters, rank, features),
            shape(adapters, rank, model),
            shape(2, adapters, rank, model),
            shape(2, adapters, rank, hidden_units),
            shape(adapters, rank, hidden_units),
            shape(adapters, rank, model),
        ],
        compiler_params=pltpu.CompilerParams(vmem_limit_bytes=56 * MIB),
        name="totals",
    )(picks, terms)


def shifted(block, axis, distance, wrap=True):
    size = lax.axis_size(axis)
    if wrap:
        route = [(i, (i + distance) % size) for i in range(size)]
    else:
        route = [(i, i + distance) for i in range(size) if 0 <= i + distance < size]
    return lax.ppermute(block, axis, route)


def sent_to_owners(parts, axis, order=(2, 1, 3)):
    received = {k: shifted(parts[k], axis, k) for k in order}
    return [parts[0]] + [received[k] for k in sorted(order)]


def blocks_of_others(block, axis):
    return [block] + [shifted(block, axis, -k) for k in (1, 2, 3)]


def blocks_by_ring(block, axis, ahead=None):
    half = block.shape[0] // 2
    before = shifted(block, axis, 1)
    after = shifted(block, axis, -1)
    if ahead is not None:
        before, after, ahead = lax.optimization_barrier((before, after, ahead))
    far = jnp.concatenate(
        [shifted(after[:half], axis, -1), shifted(before[half:], axis, 1)], axis=0
    )
    blocks = [block, after, far, before]
    return blocks if ahead is None else (blocks, ahead)


def paired_sum(block, axis):
    blocks = [part.astype(F32) for part in blocks_of_others(block, axis)]
    half = len(blocks) // 2
    while half:
        blocks = [blocks[i] + blocks[i + half] for i in range(half)]
        half //= 2
    return blocks[0]


def dot(left, right):
    return jnp.dot(left, right, preferred_element_type=F32)


def dot_nt(left, right):
    return lax.dot_general(left, right, (((1,), (1,)), ((), ())), preferred_element_type=F32)


def dot_tn(left, right):
    return lax.dot_general(left, right, (((0,), (0,)), ((), ())), preferred_element_type=F32)


def rms_scale(values, gain):
    return values * lax.rsqrt(jnp.mean(values * values, axis=-1, keepdims=True) + EPSILON) * gain


def rms_back(values, gain, grad):
    scale = lax.rsqrt(jnp.mean(values * values, axis=-1, keepdims=True) + EPSILON)
    gained = gain * grad
    return scale * gained - values * (scale**3) * jnp.mean(values * gained, axis=-1, keepdims=True)


def pad_columns(array, width):
    return jnp.pad(array, ((0, 0), (0, width - array.shape[1])))


def pad_rows(array, height):
    return jnp.pad(array, ((0, height - array.shape[0]), (0, 0)))


def on_device(
    tokens,
    cotangent,
    token_document_ids,
    sequence_adapter_index,
    mixer_norm_gain,
    head_norm_gain,
    feedforward_norm_gain,
    short_filter_kernels,
    query_weight,
    key_weight,
    value_weight,
    strength_weight,
    mixer_output_weight,
    gate_weight,
    up_weight,
    down_weight,
    adapter_attention_input,
    adapter_triple_output,
    adapter_strength_output,
    adapter_projection_input,
    adapter_projection_output,
    adapter_feedforward_input,
    adapter_feedforward_output,
    adapter_down_input,
    adapter_down_output,
):
    span, model = tokens.shape
    head_dim = head_norm_gain.shape[0]
    taps = short_filter_kernels.shape[1]
    heads = strength_weight.shape[1]
    features = heads * head_dim
    hidden_units = gate_weight.shape[1]
    adapters = adapter_attention_input.shape[1]
    rank = adapter_attention_input.shape[3]
    owners = lax.axis_size("tensor")
    place = lax.axis_index("tensor")
    position = lax.axis_index("context")
    share = span // owners
    everyone = ("weights", "context")

    def chunk_at(array, k):
        start = lax.rem(place + k, owners) * share
        return lax.dynamic_slice_in_dim(array, start, share, axis=0)

    mixer_pack = jnp.concatenate(
        [
            query_weight, key_weight, value_weight, strength_weight,
            jnp.full(
                (strength_weight.shape[0], LANES - heads),
                sequence_adapter_index[0].astype(BF16),
            ),
            mixer_output_weight.T,
        ],
        axis=1,
    )
    ffn_pack = jnp.concatenate([gate_weight, up_weight, down_weight.T], axis=1)
    mixer_all = lax.all_gather(mixer_pack, everyone, axis=0, tiled=True)
    ffn_all = lax.all_gather(ffn_pack, everyone, axis=0, tiled=True)
    chosen = sequence_adapter_index[0]
    take = lambda table, axis: lax.dynamic_index_in_dim(table, chosen, axis, keepdims=False)
    attention_in = jnp.swapaxes(take(adapter_attention_input, 1), 1, 2).reshape(4 * rank, model)
    triple_out = take(adapter_triple_output, 1)
    strength_out = take(adapter_strength_output, 0)
    projection_in = jnp.swapaxes(take(adapter_projection_input, 0), 0, 1)
    projection_out = take(adapter_projection_output, 0)
    feedforward_in = jnp.swapaxes(take(adapter_feedforward_input, 1), 1, 2).reshape(2 * rank, model)
    feedforward_out = take(adapter_feedforward_output, 1)
    down_in_ext = pad_rows(jnp.swapaxes(take(adapter_down_input, 0), 0, 1), LANES)
    ffn_low = pad_rows(
        jnp.concatenate(
            [
                pad_columns(feedforward_out[0], 2 * hidden_units),
                jnp.pad(feedforward_out[1], ((0, 0), (hidden_units, 0))),
            ],
            axis=0,
        ),
        LANES,
    )
    down_out = take(adapter_down_output, 0)
    low_in = jnp.concatenate(
        [
            jnp.pad(triple_out[part], ((0, 0), (part * features, (2 - part) * features + LANES)))
            for part in range(3)
        ]
        + [jnp.pad(strength_out, ((0, 0), (3 * features, LANES - heads)))],
        axis=0,
    )

    padded_ids = jnp.concatenate(
        [jnp.full((HALO,), -1, jnp.int32), token_document_ids[0], jnp.full((HALO,), -2, jnp.int32)]
    )
    window = lax.dynamic_slice_in_dim(padded_ids, position * span, span + 2 * HALO)
    window = jnp.where(
        jnp.arange(span + 2 * HALO) < span + HALO, window, jnp.full_like(window, -2)
    )
    seg_column = jnp.broadcast_to(window[:, None], (span + 2 * HALO, LANES))
    seg_rows = window[HALO : HALO + span].reshape(span // CHUNK, CHUNK)
    kernels = jnp.transpose(short_filter_kernels, (1, 0, 2)).reshape(taps, -1)

    edge = shifted(tokens[span - HALO :], "context", 1, wrap=False)
    inputs_ext = jnp.concatenate([edge, tokens], axis=0).astype(F32)
    normed_ext = rms_scale(inputs_ext, mixer_norm_gain).astype(BF16)
    low_ext = dot_nt(normed_ext, attention_in).astype(BF16)
    out_map = pad_rows(projection_out, LANES)
    in_map = pad_rows(feedforward_in, LANES)
    low_grad_down = pad_columns(dot_nt(cotangent, down_out).astype(BF16), LANES)
    ffn_gain = feedforward_norm_gain[None, :]
    projection_in = pad_rows(projection_in, LANES)
    triple = 3 * features + LANES
    weight_in = mixer_all[:, :triple]
    weight_out = mixer_all[:, triple:]
    weight_gate_up = ffn_all[:, : 2 * hidden_units]
    weight_down = ffn_all[:, 2 * hidden_units :]
    picks = mixer_all[:: mixer_all.shape[0] // lax.axis_size("weights"), 3 * features + heads]
    picks = picks.astype(jnp.int32)

    projected = dot(normed_ext, weight_in) + dot(low_ext, low_in)

    where = position[None]
    here = place[None]
    qp, op, offset, linear, *kept = delta_local(
        projected, kernels, seg_column, seg_rows, heads, head_dim, span, heads
    )
    one = shifted(offset, "context", 1, wrap=False)
    linear_two = lax.ppermute(linear, "context", [(2, 3)])
    second = (
        offset.astype(F32)
        + jnp.einsum("hij,hjk->hik", linear, one, preferred_element_type=F32)
    ).astype(BF16)
    out_ext = jnp.concatenate([weight_out, projection_in], axis=0)
    second, out_ext = lax.optimization_barrier((second, out_ext))
    two = lax.ppermute(second, "context", [(1, 2)])
    three = lax.ppermute(second, "context", [(1, 3)])
    gain_row = head_norm_gain[None, :]
    state, *branch_parts = attend(
        where, here, op, qp, one, two, linear_two, three, gain_row, out_ext, owners
    )
    wide = model + LANES
    branch = sent_to_owners(branch_parts, "tensor")
    linear_one = shifted(linear, "context", -1, wrap=False)
    linear_after = lax.ppermute(linear, "context", [(2, 0)])
    *branch, linear_one, linear_after = lax.optimization_barrier(
        (*branch, linear_one, linear_after)
    )
    middle, packed, low_o = owner_call(
        middle_kernel, "middle_rows", here, share,
        [(part, "rows") for part in branch]
        + [(tokens, "span"), (out_map, "whole"), (ffn_gain, "whole"), (in_map, "whole")],
        [((share, model), F32), ((share, wide), BF16), ((share, LANES), BF16)],
    )
    grad_hidden = dot(cotangent, weight_down) + dot(low_grad_down, down_in_ext)
    ffn_in, grad_hidden = blocks_by_ring(packed, "tensor", grad_hidden)

    back_parts, hidden_parts = [None] * owners, [None] * owners
    ffn_out_terms, down_in_terms = [], []
    for which in ((1, 3), (2, 0)):
        hidden_rows, *backs, out_term, down_term = ffn_rows(
            jnp.stack([lax.rem(place + k, owners) for k in which]), [ffn_in[k] for k in which],
            weight_gate_up, ffn_low, grad_hidden, low_grad_down, rank, BF16,
        )
        for i, k in enumerate(which):
            hidden_parts[k] = hidden_rows[i * share : (i + 1) * share]
            back_parts[k] = backs[i]
        ffn_out_terms.append(out_term)
        down_in_terms.append(down_term)
    back = sent_to_owners(back_parts, "tensor", (1, 3, 2))
    hidden = in_place(here, hidden_parts, hidden_units, BF16)
    down_all = dot_nt(hidden, weight_down).astype(BF16)
    down_low = dot_nt(down_in_ext[:rank], hidden).astype(BF16)
    back, down_all, down_low = lax.optimization_barrier((back, down_all, down_low))
    grad_middle, grad_packed = owner_call(
        functools.partial(back_kernel, rank=rank), "back_rows", here, share,
        [(part, "rows") for part in back]
        + [(cotangent, "span"), (middle, "rows"), (ffn_gain, "whole"), (in_map, "whole"),
           (out_map, "whole"), (low_o, "rows")],
        [((share, model), F32), ((share, wide), BF16)],
    )

    grad_blocks = blocks_by_ring(grad_packed, "tensor")
    low_down = paired_sum(down_low, "tensor").astype(BF16)
    grad_blocks, low_down = lax.optimization_barrier((grad_blocks, low_down))

    grad_attended, own, grad_o_in = attend_back(
        here, op, qp, state, gain_row, out_ext, grad_blocks, rank
    )
    down_all, own = lax.optimization_barrier((down_all, own))
    down_sum = lax.psum_scatter(down_all, "tensor", scatter_dimension=0, tiled=True).astype(F32)
    own_three = shifted(own, "context", -3, wrap=False)
    own_two = shifted(own, "context", -2, wrap=False)
    own_one = shifted(own, "context", -1, wrap=False)
    early_width = model + hidden_units
    (early,) = span_call(
        functools.partial(early_kernel, rank=rank), "early_terms", (),
        [*grad_blocks, *ffn_in, grad_o_in, low_down, cotangent, *ffn_out_terms, *down_in_terms],
        [((4, rank, early_width), BF16)], [], 56,
    )
    own_one, own_two, own_three, early = lax.optimization_barrier(
        (own_one, own_two, own_three, early)
    )

    grad_projected, halo, tail = delta_back(
        projected, kernels, seg_column, seg_rows, kept, state, grad_attended,
        (own_one, own_two, own_three, linear_one, linear_after), heads, head_dim, span, heads // 2,
    )
    returned = shifted(halo, "context", -1, wrap=False)
    low_down_own = lax.dynamic_slice_in_dim(low_down, place * share, share, axis=1)
    block_own = (middle + down_sum + dot_tn(low_down_own, down_out)).astype(BF16)
    returned, block_own = lax.optimization_barrier((returned, block_own))
    block_half = share // 2
    block_before = shifted(block_own, "tensor", 1)
    block_after = shifted(block_own, "tensor", -1)
    grad_projected = lax.dynamic_update_slice(
        grad_projected, (tail + returned).astype(BF16), (span - HALO, 0)
    )

    low_part = dot_nt(grad_projected, low_in).astype(BF16)
    low_parts = blocks_of_others(low_part, "tensor")
    grad_rows, _ = lax.optimization_barrier((grad_projected, low_part))
    normed_parts = dot_nt(grad_rows, weight_in).astype(BF16)
    low_parts, normed_parts = lax.optimization_barrier(
        (low_parts, [chunk_at(normed_parts, k) for k in range(owners)])
    )
    late_width = model + features
    low_grad_attn, *quarters = span_call(
        functools.partial(late_kernel, rank=rank), "late_terms", (where,),
        [*low_parts, normed_ext, low_ext, grad_projected, early],
        [((span, 4 * rank), BF16)] + [((rank, early_width + late_width), BF16)] * 4,
        [pltpu.VMEM((4, rank, late_width), BF16)], 24,
    )
    quarters = sent_to_owners(quarters, "context")
    *quarters, block_before, block_after = lax.optimization_barrier(
        (*quarters, block_before, block_after)
    )
    normed_sent = sent_to_owners(normed_parts, "tensor")
    block_far = jnp.concatenate(
        [
            shifted(block_after[:block_half], "tensor", -1),
            shifted(block_before[block_half:], "tensor", 1),
        ],
        axis=0,
    )
    *normed_sent, block_far, picks = lax.optimization_barrier((*normed_sent, block_far, picks))
    block_out = in_place(here, [block_own, block_after, block_far, block_before], model, BF16)
    (grad_tokens,) = owner_call(
        tokens_kernel, "token_rows", here, share,
        [(part, "rows") for part in normed_sent]
        + [(low_grad_attn, "span"), (attention_in, "whole"), (tokens, "span"),
           (mixer_norm_gain[None, :], "whole"), (grad_middle, "rows")],
        [((share, model), BF16)],
    )
    token_blocks, block_out = blocks_by_ring(grad_tokens, "tensor", block_out)
    tokens_grad = in_place(here, token_blocks, model, F32)

    quarter = sum(part.astype(F32) for part in quarters).astype(BF16)
    terms = lax.all_gather(quarter, everyone, axis=0, tiled=False)
    terms = terms.reshape(lax.axis_size("weights"), 4, rank, -1)
    cuts = (0, model, model + hidden_units, 2 * model + hidden_units)
    sums = totals(
        picks, terms, cuts, adapters, rank, model, features, hidden_units, heads
    )
    flip = lambda array: jnp.swapaxes(array, -1, -2)
    return (
        block_out,
        tokens_grad,
        flip(sums[0]),
        sums[1],
        flip(sums[2]),
        flip(sums[3]),
        sums[4],
        flip(sums[5]),
        sums[6],
        flip(sums[7]),
        sums[8],
    )


def solution(mesh):
    rows = P(("weights", "context"), None)
    return jax.shard_map(
        on_device,
        mesh=mesh,
        in_specs=(
            rows,
            rows,
            P("weights", None),
            P("weights"),
            P(),
            P(),
            P(),
            P(None, None, "tensor"),
            P(("weights", "context"), "tensor"),
            P(("weights", "context"), "tensor"),
            P(("weights", "context"), "tensor"),
            P(("weights", "context"), "tensor"),
            P("tensor", ("weights", "context")),
            P(("weights", "context"), "tensor"),
            P(("weights", "context"), "tensor"),
            P("tensor", ("weights", "context")),
            P(),
            P(None, None, None, "tensor"),
            P(None, None, "tensor"),
            P(None, "tensor", None),
            P(),
            P(),
            P(None, None, None, "tensor"),
            P(None, "tensor", None),
            P(),
        ),
        out_specs=(
            rows,
            rows,
            P(),
            P(None, None, None, "tensor"),
            P(None, None, "tensor"),
            P(None, "tensor", None),
            P(),
            P(),
            P(None, None, None, "tensor"),
            P(None, "tensor", None),
            P(),
        ),
        check_vma=False,
    )
```
